32 devices in a mesh: fsdp: 4 (over x, core), seq: 8 (over z, y).
Axes of the slice: x: 2, y: 2, z: 4, core: 2. Of those that a mesh axis runs over, the one named last changes fastest.
Arguments:
- tokens: bfloat16 [4096, 2048], P(('fsdp', 'seq')), may hold values from -6 to 6
- positions: int32 [4096], P(('fsdp', 'seq')), may hold values from 0 to 1023
- doc_start: int32 [4096], P(('fsdp', 'seq')), may hold values from 0 to 63, as said below
- cotangent: bfloat16 [4096, 2048], P(('fsdp', 'seq')), may hold values from -6 to 6
- w_query: bfloat16 [2048, 2048], P(('fsdp', 'seq')), may hold values from -0.1875 to 0.1875
- w_key: bfloat16 [2048, 256], P(('fsdp', 'seq')), may hold values from -0.125 to 0.125
- w_value: bfloat16 [2048, 256], P(('fsdp', 'seq')), may hold values from -0.125 to 0.125
- w_out: bfloat16 [2048, 2048], P(None, ('fsdp', 'seq')), may hold values from -1.5 to 1.5
- attn_gain: bfloat16 [2048], P(('fsdp', 'seq')), may hold values from 0.5 to 1.5
- w_gate: bfloat16 [2048, 5632], P(('fsdp', 'seq')), may hold values from -0.125 to 0.125
- w_up: bfloat16 [2048, 5632], P(('fsdp', 'seq')), may hold values from -0.125 to 0.125
- w_down: bfloat16 [5632, 2048], P(('fsdp', 'seq')), may hold values from -0.078125 to 0.078125
- mlp_gain: bfloat16 [2048], P(('fsdp', 'seq')), may hold values from 0.5 to 1.5
Outputs:
- output: bfloat16 [4096, 2048], P(('fsdp', 'seq'))
- input_grad: float32 [4096, 2048], P(('fsdp', 'seq'))
- grad_query: float32 [2048, 2048], P(('fsdp', 'seq'))
- grad_key: float32 [2048, 256], P(('fsdp', 'seq'))
- grad_value: float32 [2048, 256], P(('fsdp', 'seq'))
- grad_out: float32 [2048, 2048], P(None, ('fsdp', 'seq'))
- grad_attn_gain: float32 [2048], P(('fsdp', 'seq'))
- grad_gate: float32 [2048, 5632], P(('fsdp', 'seq'))
- grad_up: float32 [2048, 5632], P(('fsdp', 'seq'))
- grad_down: float32 [5632, 2048], P(('fsdp', 'seq'))
- grad_mlp_gain: float32 [2048], P(('fsdp', 'seq'))
The draws below stay inside these ranges and needn't reach their ends.
Inputs may be any that keep to these rules, and one draw needn't show every extreme that they name: `doc_start`: within each sequence of 1024 rows the value is 0 up to a cut c with 1 <= c <= 63 and c from row c to the sequence's end; in one sequence c = 63.
All inputs are finite; a program needn't handle non-finite values.
Results may differ from the reference program's by a relative error of at most 0.017.
Values may be sent and summed in bfloat16 or wider, within the bound.
A program may use at most 384 MiB of HBM per device.

```python
import jax
import jax.numpy as jnp
from jax import lax

D = 2048
FF = 5632
HEADS = 32
KV_HEADS = 4
HEAD_DIM = 64
TOK_DEV = 128
QW = 2048
KVW = 256
SEQ_LEN = 1024
TOKENS = 4096


def draw_doc_start(key, part):
    key = jax.random.fold_in(key, 7)
    groups = TOKENS // SEQ_LEN
    cut_rows = jax.random.randint(key, (groups,), 1, TOK_DEV // 2)
    chosen = jax.random.randint(jax.random.fold_in(key, 11), (), 0, groups)
    cut_rows = jnp.where(jnp.arange(groups, dtype=jnp.int32) == chosen, TOK_DEV // 2 - 1, cut_rows)
    offsets = jnp.arange(SEQ_LEN, dtype=jnp.int32)
    start_rows = jnp.where(offsets[None, :] >= cut_rows[:, None], cut_rows[:, None], 0)
    return start_rows.reshape(TOKENS).astype(jnp.int32)


def plant(values, stream_key, least, largest):
    index_at = [jax.random.randint(jax.random.fold_in(stream_key, axis), (), 0, length) for axis, length in enumerate(values.shape)]
    longest = values.shape.index(max(values.shape))
    neighbour = index_at[:longest] + [(index_at[longest] + 1) % values.shape[longest]] + index_at[longest + 1:]
    return values.at[tuple(index_at)].set(least).at[tuple(neighbour)].set(largest)


def levels(rng, extent, pieces, smallest, largest):
    def one(position, blocks):
        steps = jax.random.uniform(jax.random.fold_in(jax.random.fold_in(rng, 6), position), (blocks,), jnp.float32, smallest / len(pieces), largest / len(pieces))
        return jnp.repeat(jnp.exp(steps), extent[position] // blocks).reshape((-1,) + (1,) * (len(extent) - position - 1))

    factor_of = one(*pieces[0])
    for cut in pieces[1:]:
        factor_of = factor_of * one(*cut)
    return factor_of


def scatter_about(key, dims, spread, limit, shards=(), kind=jnp.bfloat16):
    gain = levels(key, dims, shards, -0.22, 0.18) if shards else 1.0
    values = jax.random.normal(key, dims, jnp.float32) * spread * gain
    return jnp.minimum(jnp.maximum(values, -limit), limit).astype(kind)


def setup_inputs(seed: int = 0) -> dict:
    key_of = jax.random.split(jax.random.key(seed), 14)
    tokens = scatter_about(key_of[0], (TOKENS, D), 1.0, 6.0, ((0, 32),))
    positions = plant(jax.random.randint(key_of[1], (TOKENS,), 0, SEQ_LEN), jax.random.fold_in(key_of[1], 1), 0, SEQ_LEN - 1).astype(jnp.int32)
    doc_start = draw_doc_start(jax.random.fold_in(key_of[13], 71), 0)
    cotangent = scatter_about(key_of[3], (TOKENS, D), 1.0, 6.0, ((0, 32),))
    w_query = scatter_about(key_of[4], (D, QW), (D // 2) ** -0.5, 0.1875, ((0, 32),))
    w_key = scatter_about(key_of[5], (D, KVW), D ** -0.5, 0.125, ((0, 32),))
    w_value = scatter_about(key_of[6], (D, KVW), D ** -0.5, 0.125, ((0, 32),))
    w_out = scatter_about(key_of[7], (QW, D), (HEAD_DIM // 4) ** -0.5, 1.5, ((1, 32),))
    attn_gain = jnp.clip(1.0 + 0.1 * jax.random.normal(key_of[8], (D,), jnp.float32), 0.5, 1.5).astype(jnp.bfloat16)
    w_gate = scatter_about(key_of[9], (D, FF), D ** -0.5, 0.125, ((0, 32),))
    w_up = scatter_about(key_of[10], (D, FF), D ** -0.5, 0.125, ((0, 32),))
    w_down = scatter_about(key_of[11], (FF, D), FF ** -0.5, 0.078125, ((0, 32),))
    mlp_gain = jnp.clip(1.0 + 0.1 * jax.random.normal(key_of[12], (D,), jnp.float32), 0.5, 1.5).astype(jnp.bfloat16)
    return {"tokens": tokens, "positions": positions, "doc_start": doc_start, "cotangent": cotangent, "w_query": w_query, "w_key": w_key, "w_value": w_value, "w_out": w_out, "attn_gain": attn_gain, "w_gate": w_gate, "w_up": w_up, "w_down": w_down, "mlp_gain": mlp_gain}


EPSILON = 1e-05
MASKED = -1e+30
PRECISE = lax.Precision.HIGHEST

@jax.custom_vjp
def low(v):
    return lax.optimization_barrier(v.astype(jnp.bfloat16)).astype(jnp.float32)

@jax.custom_vjp
def low_back(v):
    return v

def low_keep(v):
    return (low(v), None)

def low_pass(kept, grad):
    return (grad,)

def back_keep(v):
    return (v, None)

def back_low(kept, grad):
    return (low(grad),)
low.defvjp(low_keep, low_pass)
low_back.defvjp(back_keep, back_low)

def matmul(matrix_a, matrix_b):
    return jnp.dot(matrix_a, matrix_b, precision=PRECISE, preferred_element_type=jnp.float32)

def rms_norm(values, gain_vec):
    return values * lax.rsqrt(lax.optimization_barrier(jnp.mean(values * values, axis=-1, keepdims=True)) + EPSILON) * gain_vec

def rotate(values):
    half_dim = values.shape[-1] // 2
    return jnp.concatenate([-values[..., half_dim:], values[..., :half_dim]], axis=-1)

def tables(positions):
    half_dim = HEAD_DIM // 2
    frequency = 10000.0 ** (-2.0 * jnp.arange(half_dim, dtype=jnp.float32) / HEAD_DIM)
    angles = positions.astype(jnp.float32)[:, None] * frequency[None, :]
    cos_table = jnp.concatenate([jnp.cos(angles), jnp.cos(angles)], axis=-1)[:, None, :]
    sin_table = jnp.concatenate([jnp.sin(angles), jnp.sin(angles)], axis=-1)[:, None, :]
    return (cos_table, sin_table)

def rope_apply(values, cos_table, sin_table):
    return values * cos_table + rotate(values) * sin_table

def group_attention(queries, keys_rot, values_low, starts):
    group_size = HEADS // KV_HEADS
    block_len = min(512, SEQ_LEN)
    block_count = SEQ_LEN // block_len
    score_scale = HEAD_DIM ** (-0.5)
    columns = jnp.arange(SEQ_LEN, dtype=jnp.int32)

    def block_attention(inputs):
        query_block, start_block, first_row = inputs
        scores = jnp.einsum('qkgd,jkd->kgqj', query_block, keys_rot, precision=PRECISE) * score_scale
        scores = low_back(scores)
        row_ids = first_row + jnp.arange(block_len, dtype=jnp.int32)
        allowed = (columns[None, :] >= start_block[:, None]) & (columns[None, :] <= row_ids[:, None])
        scores = jnp.where(allowed[None, None], scores, MASKED)
        weights = jax.nn.softmax(scores, axis=-1)
        return jnp.einsum('kgqj,jkd->qkgd', low(weights), values_low, precision=PRECISE)
    firsts = jnp.arange(block_count, dtype=jnp.int32) * block_len
    result = lax.map(jax.checkpoint(block_attention), (queries.reshape(block_count, block_len, KV_HEADS, group_size, HEAD_DIM), starts.reshape(block_count, block_len), firsts))
    return result.reshape(SEQ_LEN, HEADS * HEAD_DIM)

def reference(tokens, positions, doc_start, cotangent, w_query, w_key, w_value, w_out, attn_gain, w_gate, w_up, w_down, mlp_gain):
    cos_table, sin_table = tables(positions)
    groups = TOKENS // SEQ_LEN
    group_size = HEADS // KV_HEADS

    def layer_forward(inputs_f, query_w, key_w, value_w, out_w, attn_g, gate_w, up_w, down_w, mlp_g):
        attn_in = low(rms_norm(inputs_f, attn_g))
        query_pre = low_back(matmul(attn_in, query_w))
        key_pre = low_back(matmul(attn_in, key_w))
        value_pre = low_back(matmul(attn_in, value_w))
        queries = low(rope_apply(query_pre.reshape(TOKENS, HEADS, HEAD_DIM), cos_table, sin_table))
        keys_rot = low(rope_apply(key_pre.reshape(TOKENS, KV_HEADS, HEAD_DIM), cos_table, sin_table))
        values_low = low(value_pre).reshape(TOKENS, KV_HEADS, HEAD_DIM)
        attended = lax.map(lambda inputs: group_attention(*inputs), (queries.reshape(groups, SEQ_LEN, KV_HEADS, group_size, HEAD_DIM), keys_rot.reshape(groups, SEQ_LEN, KV_HEADS, HEAD_DIM), values_low.reshape(groups, SEQ_LEN, KV_HEADS, HEAD_DIM), doc_start.reshape(groups, SEQ_LEN)))
        context_low = low(low_back(attended.reshape(TOKENS, HEADS * HEAD_DIM)))
        mid_f = inputs_f + low_back(matmul(context_low, out_w))
        mlp_in = low(rms_norm(mid_f, mlp_g))
        gate_pre = low_back(matmul(mlp_in, gate_w))
        up_pre = low_back(matmul(mlp_in, up_w))
        hidden_low = low(jax.nn.silu(gate_pre) * up_pre)
        return mid_f + low_back(matmul(hidden_low, down_w))
    floats = tuple((arg.astype(jnp.float32) for arg in (tokens, w_query, w_key, w_value, w_out, attn_gain, w_gate, w_up, w_down, mlp_gain)))
    result, pullback = jax.vjp(layer_forward, *floats)
    gradients = pullback(cotangent.astype(jnp.float32))
    return (result.astype(jnp.bfloat16), gradients[0], gradients[1], gradients[2], gradients[3], gradients[4], gradients[5], gradients[6], gradients[7], gradients[8], gradients[9])
```

```python
import jax
import jax.numpy as jnp
from jax import lax
from jax.sharding import Mesh
from jax.sharding import PartitionSpec as P

HEADS = 32
KV_HEADS = 4
HEAD_DIM = 64
EPSILON = 1e-05
MASKED = -1e30
ALL = ("x", "core", "z", "y")
TEAM = ("z", "core")
DATA = ("x", "y")
BF = jnp.bfloat16
F32 = jnp.float32


def dot_plain(a, b):
    return jnp.dot(a, b, preferred_element_type=F32)


def dot_right_t(a, b):
    return lax.dot_general(a, b, (((1,), (1,)), ((), ())), preferred_element_type=F32)


def dot_left_t(a, b):
    return lax.dot_general(a, b, (((0,), (0,)), ((), ())), preferred_element_type=F32)


def team_gather(rows):
    return lax.all_gather(rows, TEAM, axis=0, tiled=True)


def team_sum_scatter(partial):
    team = lax.axis_size(TEAM)
    blocks = partial.reshape(team, partial.shape[0] // team, partial.shape[1])
    arrived = lax.all_to_all(blocks, TEAM, 0, 0, tiled=False)
    return jnp.sum(arrived.astype(F32), axis=0)


def team_exchange(blocks):
    return lax.all_to_all(blocks, TEAM, 0, 0, tiled=False)


def weights_gather(blocks):
    z, c = lax.axis_size("z"), lax.axis_size("core")
    rows, cols = blocks.shape[1:]
    got = lax.all_gather(blocks, DATA, axis=0)
    x, y = lax.axis_size("x"), lax.axis_size("y")
    got = got.reshape(x, y, z, c, rows, cols).transpose(0, 3, 2, 1, 4, 5)
    return got.reshape(x * c * z * y * rows, cols)


def grads_scatter(partial):
    x, y, z, c = (lax.axis_size(a) for a in ("x", "y", "z", "core"))
    cols = partial.shape[1]
    rows = partial.shape[0] // (x * y * z * c)
    parts = partial.astype(BF).reshape(x, c, z, y, rows, cols).transpose(0, 3, 2, 1, 4, 5)
    parts = parts.reshape(x * y, z * c * rows, cols)
    arrived = lax.all_to_all(parts, DATA, 0, 0, tiled=False)
    return jnp.sum(arrived.astype(F32), axis=0).reshape(z * c, rows, cols)


def turn(values):
    half = values.shape[-1] // 2
    return jnp.concatenate([-values[..., half:], values[..., :half]], axis=-1)


def rope_apply(values, cos_table, sin_table):
    return values * cos_table + turn(values) * sin_table


def rope_reverse(gradient, cos_table, sin_table):
    half = gradient.shape[-1] // 2
    scaled = gradient * sin_table
    return gradient * cos_table + jnp.concatenate(
        [scaled[..., half:], -scaled[..., :half]], axis=-1
    )


def shards(
    tokens, positions, doc_start, cotangent, w_query, w_key, w_value, w_out,
    attn_gain, w_gate, w_up, w_down, mlp_gain,
):
    nx, nc, nz, ny = (lax.axis_size(a) for a in ALL)
    team = nz * nc
    rows, width = tokens.shape
    own = w_query.shape[0]
    heads = HEADS // team
    qcols = heads * HEAD_DIM
    kv_rep = team // KV_HEADS
    ff = w_gate.shape[1]
    piece = w_down.shape[0]
    ffcols = piece * nx * ny
    y_at = lax.axis_index("y")
    core_at = lax.axis_index("core")
    scale = HEAD_DIM ** (-0.5)

    gain_a = attn_gain.astype(F32)[:, None]
    gain_m = mlp_gain.astype(F32)[:, None]

    def by_heads(w):
        return w.reshape(own, team, -1).transpose(1, 0, 2)

    def by_kv(w):
        return jnp.repeat(w.reshape(own, KV_HEADS, HEAD_DIM).transpose(1, 0, 2), kv_rep, axis=0)

    def scaled(w, gain):
        return (w.astype(F32) * gain).astype(BF)

    def by_ff(w):
        w = w.reshape(own, nx, nc, nz, ny, piece).transpose(3, 2, 0, 1, 4, 5)
        return w.reshape(team, own, ffcols)

    attn_blocks = jnp.concatenate(
        [
            by_heads(scaled(w_query, gain_a)),
            by_kv(scaled(w_key, gain_a)),
            by_kv(scaled(w_value, gain_a)),
            by_heads(w_out.T),
        ],
        axis=-1,
    )
    mlp_blocks = jnp.concatenate([by_ff(scaled(w_gate, gain_m)), by_ff(scaled(w_up, gain_m))], axis=-1)
    w_attn = weights_gather(team_exchange(attn_blocks))
    w_qkv = w_attn[:, : qcols + 2 * HEAD_DIM]
    w_out_t = w_attn[:, qcols + 2 * HEAD_DIM :]

    xf = tokens.astype(F32)
    inv1 = lax.rsqrt(jnp.mean(xf * xf, axis=-1, keepdims=True) + EPSILON)
    n1 = xf * inv1
    half = HEAD_DIM // 2
    frequency = 10000.0 ** (-2.0 * jnp.arange(half, dtype=F32) / HEAD_DIM)
    angles = positions.astype(F32)[:, None] * frequency[None, :]
    table = jnp.concatenate(
        [
            jnp.cos(angles),
            jnp.sin(angles),
            jnp.broadcast_to(doc_start.astype(F32)[:, None], (rows, HEAD_DIM)),
        ],
        axis=-1,
    )
    n1g = team_gather(n1.astype(BF))
    tab = team_gather(table)
    cos_t = jnp.concatenate([tab[:, :half], tab[:, :half]], axis=-1)
    sin_t = jnp.concatenate([tab[:, half : 2 * half], tab[:, half : 2 * half]], axis=-1)
    starts = tab[:, 2 * half].astype(jnp.int32).reshape(nz, nc, rows)

    qkv = dot_plain(n1g, w_qkv)
    total = team * rows
    q = rope_apply(
        qkv[:, :qcols].reshape(total, heads, HEAD_DIM), cos_t[:, None], sin_t[:, None]
    ).astype(BF)
    k = rope_apply(qkv[:, qcols : qcols + HEAD_DIM], cos_t, sin_t).astype(BF)
    v = qkv[:, qcols + HEAD_DIM :].astype(BF)

    kv_own = jnp.concatenate([k, v], axis=-1).reshape(nz, nc, rows, 2 * HEAD_DIM)
    kv_all = lax.all_gather(kv_own, "y", axis=0).transpose(2, 1, 0, 3, 4)
    kv_all = kv_all.reshape(nc, nz * ny * rows, 2 * HEAD_DIM)
    k_all, v_all = kv_all[..., :HEAD_DIM], kv_all[..., HEAD_DIM:]
    qh = q.reshape(nz, nc, rows, heads, HEAD_DIM).transpose(0, 1, 3, 2, 4)

    def block_scores(z):
        keys = (z + 1) * ny * rows
        s = jnp.einsum("chrd,ckd->chrk", qh[z], k_all[:, :keys], preferred_element_type=F32) * scale
        row_at = (z * ny + y_at) * rows + jnp.arange(rows, dtype=jnp.int32)
        cols = jnp.arange(keys, dtype=jnp.int32)
        allowed = (cols[None, None, :] >= starts[z][:, :, None]) & (
            cols[None, None, :] <= row_at[None, :, None]
        )
        s = jnp.where(allowed[:, None], s, MASKED)
        top = jnp.max(s, axis=-1, keepdims=True)
        e = jnp.exp(s - top)
        return e / jnp.sum(e, axis=-1, keepdims=True), keys

    contexts = []
    for z in range(nz):
        p, keys = block_scores(z)
        contexts.append(
            jnp.einsum("chrk,ckd->chrd", p.astype(BF), v_all[:, :keys], preferred_element_type=F32)
        )
    context = jnp.stack(contexts)
    ob = context.transpose(0, 1, 3, 2, 4).reshape(total, qcols).astype(BF)

    mid_f = xf + team_sum_scatter(dot_right_t(ob, w_out_t).astype(BF))
    inv2 = lax.rsqrt(jnp.mean(mid_f * mid_f, axis=-1, keepdims=True) + EPSILON)
    n2 = mid_f * inv2
    n2g = team_gather(n2.astype(BF))

    w_mlp = weights_gather(team_exchange(mlp_blocks))
    w_dn = lax.all_gather(w_down, DATA, axis=0, tiled=True)
    gt = dot_plain(n2g, w_mlp[:, :ffcols])
    up = dot_plain(n2g, w_mlp[:, ffcols:])
    sg = jax.nn.sigmoid(gt)
    hid = (gt * sg * up).astype(BF)
    output = (mid_f + team_sum_scatter(dot_plain(hid, w_dn).astype(BF))).astype(BF)

    cotg = team_gather(cotangent)
    dhid = dot_right_t(cotg, w_dn)
    down_part = dot_left_t(hid, cotg).astype(BF)
    dgt = (dhid * up * sg * (1.0 + gt * (1.0 - sg))).astype(BF)
    dup = (dhid * gt * sg).astype(BF)
    dmlp = jnp.concatenate([dgt, dup], axis=-1)
    dn2 = team_sum_scatter(dot_right_t(dmlp, w_mlp).astype(BF))
    mlp_part = dot_left_t(n2g, dmlp).astype(BF)
    gain_m_part = jnp.sum(dn2 * n2, axis=0)
    dx2 = cotangent.astype(F32) + inv2 * (dn2 - n2 * jnp.mean(dn2 * n2, axis=-1, keepdims=True))
    dag = team_gather(dx2.astype(BF))
    out_part = dot_left_t(dag, ob)
    dob = dot_plain(dag, w_out_t).astype(BF)

    doh = dob.reshape(nz, nc, rows, heads, HEAD_DIM).transpose(0, 1, 3, 2, 4)
    delta = jnp.sum(doh.astype(F32) * context, axis=-1)
    dqs = []
    dk = jnp.zeros((nc, nz * ny * rows, HEAD_DIM), F32)
    dv = jnp.zeros((nc, nz * ny * rows, HEAD_DIM), F32)
    for z in range(nz):
        p, keys = block_scores(z)
        dv = dv.at[:, :keys].add(
            jnp.einsum("chrk,chrd->ckd", p.astype(BF), doh[z], preferred_element_type=F32)
        )
        dp = jnp.einsum("chrd,ckd->chrk", doh[z], v_all[:, :keys], preferred_element_type=F32)
        ds = (p * (dp - delta[z][..., None])).astype(BF)
        dqs.append(
            jnp.einsum("chrk,ckd->chrd", ds, k_all[:, :keys], preferred_element_type=F32) * scale
        )
        dk = dk.at[:, :keys].add(
            jnp.einsum("chrk,chrd->ckd", ds, qh[z], preferred_element_type=F32) * scale
        )
    dq = jnp.stack(dqs).transpose(0, 1, 3, 2, 4).reshape(total, heads, HEAD_DIM)
    dkv = jnp.concatenate([dk, dv], axis=-1).astype(BF)
    dkv = dkv.reshape(nc, nz, ny, rows, 2 * HEAD_DIM).transpose(2, 1, 0, 3, 4)
    dkv = lax.all_to_all(dkv, "y", 0, 0, tiled=False).astype(F32).sum(0)
    dkv = dkv.reshape(total, 2 * HEAD_DIM)
    dkv = lax.psum(dkv, "core")
    dka = rope_reverse(dkv[:, :HEAD_DIM], cos_t, sin_t)
    dva = dkv[:, HEAD_DIM:]
    dka = jnp.where(core_at == 0, dka, 0.0)
    dva = jnp.where(core_at == 1, dva, 0.0)
    dqa = rope_reverse(dq, cos_t[:, None], sin_t[:, None]).reshape(total, qcols)
    dqkv = jnp.concatenate([dqa, dka, dva], axis=-1).astype(BF)
    dn1 = team_sum_scatter(dot_right_t(dqkv, w_qkv).astype(BF))
    qkv_part = dot_left_t(n1g, dqkv)
    gain_a_part = jnp.sum(dn1 * n1, axis=0)
    input_grad = dx2 + inv1 * (dn1 - n1 * jnp.mean(dn1 * n1, axis=-1, keepdims=True))

    attn_part = jnp.concatenate([qkv_part, out_part], axis=-1)
    attn_g = team_exchange(grads_scatter(attn_part).astype(BF)).astype(F32)
    mlp_g = team_exchange(grads_scatter(mlp_part).astype(BF)).astype(F32)
    down_blocks = down_part.reshape(nx * ny, piece, width)
    grad_down = jnp.sum(lax.all_to_all(down_blocks, DATA, 0, 0, tiled=False).astype(F32), axis=0)
    grad_query = attn_g[:, :, :qcols].transpose(1, 0, 2).reshape(own, HEADS * HEAD_DIM) * gain_a
    kv_g = attn_g[:, :, qcols : qcols + 2 * HEAD_DIM].reshape(KV_HEADS, kv_rep, own, 2 * HEAD_DIM).sum(1)
    grad_key = kv_g[..., :HEAD_DIM].transpose(1, 0, 2).reshape(own, KV_HEADS * HEAD_DIM) * gain_a
    grad_value = kv_g[..., HEAD_DIM:].transpose(1, 0, 2).reshape(own, KV_HEADS * HEAD_DIM) * gain_a
    grad_out = attn_g[:, :, qcols + 2 * HEAD_DIM :].transpose(1, 0, 2).reshape(own, HEADS * HEAD_DIM).T

    def from_ff(g):
        g = g.reshape(nz, nc, own, nx, ny, piece).transpose(2, 3, 1, 0, 4, 5)
        return g.reshape(own, ff) * gain_m

    grad_gate = from_ff(mlp_g[:, :, :ffcols])
    grad_up = from_ff(mlp_g[:, :, ffcols:])
    gains = jnp.stack([gain_a_part, gain_m_part], 0).reshape(2, nx * team * ny, own).transpose(1, 0, 2)
    gains = lax.all_to_all(gains, ALL, 0, 0, tiled=False).sum(0)
    grad_attn_gain = gains[0] / gain_a[:, 0]
    grad_mlp_gain = gains[1] / gain_m[:, 0]
    return (
        output, input_grad, grad_query, grad_key, grad_value, grad_out,
        grad_attn_gain, grad_gate, grad_up, grad_down, grad_mlp_gain,
    )


def solution(mesh):
    fsdp, seq = mesh.shape["fsdp"], mesh.shape["seq"]
    nc, nz = 2, 4
    grid = Mesh(mesh.devices.reshape(fsdp // nc, nc, nz, seq // nz), ALL)
    row, col, vec = P(ALL, None), P(None, ALL), P(ALL)
    in_specs = (row, vec, vec, row, row, row, row, col, vec, row, row, row, vec)
    out_specs = (row, row, row, row, row, col, vec, row, row, row, vec)
    return jax.shard_map(shards, mesh=grid, in_specs=in_specs, out_specs=out_specs, check_vma=False)
```

```python
import functools

import jax
import jax.numpy as jnp
from jax import lax
from jax.experimental import pallas as pl
from jax.experimental.pallas import tpu as pltpu
from jax.sharding import Mesh
from jax.sharding import PartitionSpec as P

HEADS = 32
KV_HEADS = 4
HEAD_DIM = 64
EPSILON = 1e-05
MASKED = -1e30
ALL = ("x", "core", "z", "y")
TEAM = ("z", "core")
DATA = ("x", "y")
BF = jnp.bfloat16
F32 = jnp.float32


def dot_plain(a, b):
    return jnp.dot(a, b, preferred_element_type=F32)


def dot_right_t(a, b):
    return lax.dot_general(a, b, (((1,), (1,)), ((), ())), preferred_element_type=F32)


def dot_left_t(a, b):
    return lax.dot_general(a, b, (((0,), (0,)), ((), ())), preferred_element_type=F32)


MESH = pl.DeviceIdType.MESH
VM = pltpu.VMEM
DMA = pltpu.SemaphoreType.DMA
ROWS = 16


def place():
    return tuple(lax.axis_index(a) for a in ALL)


def others(nx, ny):
    return [(i, j) for i in range(nx) for j in range(ny) if (i, j) != (0, 0)]


def data_peer(step, nx, ny):
    x, _, _, y = place()
    return lax.rem(x + step[0], nx), lax.rem(y + step[1], ny)


def team_peer(step, nz, nc):
    _, c, z, _ = place()
    return lax.rem(z + step[0], nz), lax.rem(c + step[1], nc)


def greet(nx, nc, nz, ny):
    barrier = pltpu.get_barrier_semaphore()
    for step in others(nx, ny):
        px, py = data_peer(step, nx, ny)
        pl.semaphore_signal(barrier, inc=1, device_id={"x": px, "y": py}, device_id_type=MESH)
    for step in others(nz, nc):
        pz, pc = team_peer(step, nz, nc)
        pl.semaphore_signal(barrier, inc=1, device_id={"z": pz, "core": pc}, device_id_type=MESH)
    pl.semaphore_wait(barrier, nx * ny - 1 + nz * nc - 1)


def remote(source, target, send, recv, device):
    return pltpu.make_async_remote_copy(
        src_ref=source, dst_ref=target, send_sem=send, recv_sem=recv,
        device_id=device, device_id_type=MESH,
    )


class Gather:
    SEMS = [DMA((4, 4)), DMA((2, 4))]

    def __init__(self, own, full, send, recv, local):
        self.own, self.full, self.send, self.recv = own, full, send, recv
        self.x, self.c, self.z, self.y = place()
        self.nz = full.shape[0]
        self.local = pltpu.make_async_copy(own, full.at[self.z, self.c], local)

    def copy(self, at, kind):
        slot = self.full.at[at, self.c]
        device = ({"z": self.z + 1}, {"z": self.z - 1}, {"core": 1 - self.c})[kind]
        return remote(
            slot, slot, self.send.at[kind, at], self.recv.at[0 if kind < 2 else 1, at], device
        )

    def start(self):
        self.local.start()
        self.local.wait()
        pl.when(self.z < self.nz - 1)(lambda: self.copy(self.z, 0).start())
        pl.when(self.z > 0)(lambda: self.copy(self.z, 1).start())
        self.copy(self.z, 2).start()

    def hop(self, far):
        @pl.when(self.z - far >= 0)
        def _():
            at = self.z - far
            self.copy(at, 0).wait_recv()
            pl.when(self.z < self.nz - 1)(lambda: self.copy(at, 0).start())
            self.copy(at, 2).start()

        @pl.when(self.z + far < self.nz)
        def _():
            at = self.z + far
            self.copy(at, 1).wait_recv()
            pl.when(self.z > 0)(lambda: self.copy(at, 1).start())
            self.copy(at, 2).start()

    def finish(self):
        for at in range(self.nz):
            pl.when((at <= self.z) & (self.z < self.nz - 1))(lambda at=at: self.copy(at, 0).wait_send())
            pl.when((at >= self.z) & (self.z > 0))(lambda at=at: self.copy(at, 1).wait_send())
            self.copy(at, 2).wait_send()
            self.copy(at, 2).wait_recv()


class Reduce:
    SEMS = [DMA((3, 4)), DMA((3, 4))]

    @staticmethod
    def buffers(nz, rows, width):
        return [VM((nz, rows, width), BF), VM((2, nz, rows, width), BF)]

    def __init__(self, part, held, came, send, recv):
        self.part, self.held, self.came, self.send, self.recv = part, held, came, send, recv
        self.x, self.c, self.z, self.y = place()
        self.nz, _, self.rows, self.width = part.shape

    def across(self, to):
        return remote(
            self.part.at[to, 1 - self.c], self.held.at[to], self.send.at[2, to], self.recv.at[2, to],
            {"core": 1 - self.c},
        )

    def along(self, to, way):
        device = ({"z": self.z + 1}, {"z": self.z - 1})[way]
        return remote(
            self.held.at[to], self.came.at[way, to], self.send.at[way, to], self.recv.at[way, to], device
        )

    def order(self):
        return [a for k in range(self.nz) for a in (self.nz - 1 - k, k)][: self.nz]

    def start(self):
        for to in self.order():
            self.across(to).start()
        zeros = jnp.zeros((ROWS, self.width), BF)
        for way, end in ((0, 0), (1, self.nz - 1)):

            @pl.when(self.z == end)
            def _(way=way):
                def clear(i, carry):
                    for to in range(self.nz):
                        self.came[way, to, pl.ds(pl.multiple_of(i * ROWS, ROWS), ROWS), :] = zeros
                    return carry

                lax.fori_loop(0, self.rows // ROWS, clear, 0)

    def add(self, to, ways, out=None):
        def body(i, carry):
            at = pl.ds(pl.multiple_of(i * ROWS, ROWS), ROWS)
            total = self.part[to, self.c, at, :].astype(F32) + self.held[to, at, :].astype(F32)
            for way in ways:
                total = total + self.came[way, to, at, :].astype(F32)
            if out is None:
                self.held[to, at, :] = total.astype(BF)
            else:
                out(at, total)
            return carry

        lax.fori_loop(0, self.rows // ROWS, body, 0)

    def hop(self, k):
        for way, to in ((0, self.nz - 1 - k), (1, k)):
            active = (self.z < to) if way == 0 else (self.z > to)
            first = (self.z == 0) if way == 0 else (self.z == self.nz - 1)

            @pl.when(active)
            def _(way=way, to=to, first=first):
                self.across(to).wait_recv()
                pl.when(jnp.logical_not(first))(lambda: self.along(to, way).wait_recv())
                self.add(to, (way,))
                self.along(to, way).start()

    def last(self, out):
        self.across(self.z).wait_recv()
        pl.when(self.z > 0)(lambda: self.along(self.z, 0).wait_recv())
        pl.when(self.z < self.nz - 1)(lambda: self.along(self.z, 1).wait_recv())
        self.add(self.z, (0, 1), out)

    def finish(self):
        for to in range(self.nz):
            self.across(to).wait_send()
            pl.when(self.z < to)(lambda to=to: self.along(to, 0).wait_send())
            pl.when(self.z > to)(lambda to=to: self.along(to, 1).wait_send())


class Spread:
    def __init__(self, source, target, send, recv, local, nx, ny):
        self.source, self.target, self.send, self.recv = source, target, send, recv
        self.nx, self.ny = nx, ny
        self.x, _, _, self.y = place()
        self.local = pltpu.make_async_copy(source(self.x, self.y), target(self.x, self.y), local)

    def copies(self):
        for i, step in enumerate(others(self.nx, self.ny)):
            px, py = data_peer(step, self.nx, self.ny)
            yield remote(
                self.source(px, py), self.target(self.x, self.y), self.send.at[i], self.recv.at[i],
                {"x": px, "y": py},
            )

    def start(self):
        for copy in self.copies():
            copy.start()
        self.local.start()

    def arrived(self):
        self.local.wait()
        for copy in self.copies():
            copy.wait_recv()

    def finish(self):
        for copy in self.copies():
            copy.wait_send()


class Swap:
    def __init__(self, blocks, slot, send, recv, local):
        self.blocks, self.slot, self.send, self.recv = blocks, slot, send, recv
        self.nz, self.nc = blocks.shape[:2]
        _, self.c, self.z, _ = place()
        self.local = pltpu.make_async_copy(blocks.at[self.z, self.c], slot(self.z, self.c), local)

    def copies(self):
        for i, step in enumerate(others(self.nz, self.nc)):
            pz, pc = team_peer(step, self.nz, self.nc)
            yield remote(
                self.blocks.at[pz, pc], self.slot(self.z, self.c), self.send.at[i], self.recv.at[i],
                {"z": pz, "core": pc},
            )

    def start(self):
        for copy in self.copies():
            copy.start()
        self.local.start()

    def arrived(self):
        self.local.wait()
        for copy in self.copies():
            copy.wait_recv()

    def finish(self):
        for copy in self.copies():
            copy.wait_send()


def call(kernel, operands, in_spaces, outs, out_spaces, scratch, number):
    return pl.pallas_call(
        kernel,
        out_shape=[jax.ShapeDtypeStruct(s, t) for s, t in outs],
        in_specs=[pl.BlockSpec(memory_space=s) for s in in_spaces],
        out_specs=[pl.BlockSpec(memory_space=s) for s in out_spaces],
        scratch_shapes=scratch,
        compiler_params=pltpu.CompilerParams(
            collective_id=number, has_side_effects=True, vmem_limit_bytes=56 << 20
        ),
    )(*operands)


def first_kernel(dims, n1, table, blocks, n1g, tabg, w_attn, gs, gr, ts, tr, ss, sr, ds, dr, local):
    nx, nc, nz, ny = dims
    x, c, z, y = place()
    greet(*dims)
    swap = Swap(blocks, lambda pz, pc: w_attn.at[x, pc, pz, y], ss, sr, local.at[0])
    rows = Gather(n1, n1g, gs, gr, local.at[1])
    tabs = Gather(table, tabg, ts, tr, local.at[2])
    swap.start()
    tabs.start()
    rows.start()
    swap.arrived()
    spread = Spread(
        lambda px, py: w_attn.at[x, :, :, y], lambda px, py: w_attn.at[px, :, :, py], ds, dr, local.at[3], nx, ny
    )
    for copy in spread.copies():
        copy.start()
    for far in range(1, nz):
        tabs.hop(far)
        rows.hop(far)
    tabs.finish()
    rows.finish()
    swap.finish()
    for copy in spread.copies():
        copy.wait_recv()
    spread.finish()


def first_call(dims, n1, table, blocks):
    nx, nc, nz, ny = dims
    rows, width = n1.shape
    own, cols = blocks.shape[2:]
    peers = nx * ny - 1
    return call(
        functools.partial(first_kernel, dims),
        (n1, table, blocks),
        (VM, VM, pl.ANY),
        [
            ((nz, nc, rows, width), BF),
            ((nz, nc) + table.shape, F32),
            ((nx, nc, nz, ny, own, cols), BF),
        ],
        (pl.ANY, pl.ANY, pl.ANY),
        Gather.SEMS * 2 + [DMA((nz * nc - 1,))] * 2 + [DMA((peers,))] * 2 + [DMA((4,))],
        1,
    )


def middle_kernel(
    dims, part, tokens, cot, mlp_t, down,
    mid, n2g, cotg, w_mlp, w_dn,
    held, came, n2, rs, rr, ns, nr, cs, cr, ms, mr, ws, wr, local,
):
    nx, nc, nz, ny = dims
    x, c, z, y = place()
    greet(*dims)
    reduce = Reduce(part, held, came, rs, rr)
    cots = Gather(cot, cotg, cs, cr, local.at[0])
    gu = Spread(lambda px, py: mlp_t, lambda px, py: w_mlp.at[px, :, :, py], ms, mr, local.at[1], nx, ny)
    dn = Spread(lambda px, py: down, lambda px, py: w_dn.at[px, py], ws, wr, local.at[2], nx, ny)
    reduce.start()
    gu.start()
    dn.start()
    cots.start()
    for k in range(nz - 1):
        reduce.hop(k)
        cots.hop(k + 1)

    def settle(at, total):
        value = tokens[at, :].astype(F32) + total
        mid[at, :] = value
        inverse = lax.rsqrt(jnp.mean(value * value, axis=-1, keepdims=True) + EPSILON)
        n2[at, :] = (value * inverse).astype(BF)

    reduce.last(settle)
    rows = Gather(n2, n2g, ns, nr, local.at[3])
    rows.start()
    for far in range(1, nz):
        rows.hop(far)
    rows.finish()
    cots.finish()
    reduce.finish()
    gu.arrived()
    dn.arrived()
    gu.finish()
    dn.finish()


def middle_call(dims, part, tokens, cot, mlp_t, down):
    nx, nc, nz, ny = dims
    rows, width = tokens.shape
    peers = nx * ny - 1
    return call(
        functools.partial(middle_kernel, dims),
        (part, tokens, cot, mlp_t, down),
        (VM, VM, VM, pl.ANY, pl.ANY),
        [
            ((rows, width), F32),
            ((nz, nc, rows, width), BF),
            ((nz, nc, rows, width), BF),
            ((nx, nc, nz, ny) + mlp_t.shape[2:], BF),
            ((nx, ny) + down.shape, BF),
        ],
        (VM, pl.ANY, pl.ANY, pl.ANY, pl.ANY),
        Reduce.buffers(nz, rows, width)
        + [VM((rows, width), BF)]
        + Reduce.SEMS
        + Gather.SEMS * 2
        + [DMA((peers,))] * 4
        + [DMA((4,))],
        2,
    )


def back_kernel(
    dims, part, mlp_part, mid, cot, grad_mlp, grad_dn,
    dx2, dag, output, gain_part, came_mlp, came_dn,
    held, came, held2, came2, low, rs, rr, os, orr, ds, dr, ms, mr, ws, wr, local,
):
    nx, nc, nz, ny = dims
    x, c, z, y = place()
    greet(*dims)
    reduce = Reduce(part, held, came, rs, rr)
    reduce2 = Reduce(mlp_part, held2, came2, os, orr)
    reduce.start()
    dn = Spread(lambda px, py: grad_dn.at[px, py], lambda px, py: came_dn.at[px, py], ws, wr, local.at[0], nx, ny)
    gu = Spread(
        lambda px, py: grad_mlp.at[px, :, :, py], lambda px, py: came_mlp.at[px, py], ms, mr, local.at[1], nx, ny
    )
    gu.start()
    dn.start()
    for k in range(nz - 1):
        reduce.hop(k)
    gain_part[...] = jnp.zeros_like(gain_part)

    def settle(at, total):
        value = mid[at, :]
        inverse = lax.rsqrt(jnp.mean(value * value, axis=-1, keepdims=True) + EPSILON)
        normed = value * inverse
        gain_part[...] += jnp.sum((total * normed).reshape(ROWS // 8, 8, -1), axis=0)
        gradient = cot[at, :].astype(F32) + inverse * (
            total - normed * jnp.mean(total * normed, axis=-1, keepdims=True)
        )
        dx2[at, :] = gradient
        low[at, :] = gradient.astype(BF)

    reduce.last(settle)
    rows = Gather(low, dag, ds, dr, local.at[2])
    rows.start()
    reduce2.start()
    for k in range(nz - 1):
        rows.hop(k + 1)
        reduce2.hop(k)

    def finish(at, total):
        output[at, :] = (mid[at, :] + total).astype(BF)

    reduce2.last(finish)
    rows.finish()
    reduce.finish()
    reduce2.finish()
    gu.arrived()
    dn.arrived()
    gu.finish()
    dn.finish()


def back_call(dims, part, mlp_part, mid, cot, grad_mlp, grad_dn):
    nx, nc, nz, ny = dims
    rows, width = mid.shape
    peers = nx * ny - 1
    return call(
        functools.partial(back_kernel, dims),
        (part, mlp_part, mid, cot, grad_mlp, grad_dn),
        (VM, VM, VM, VM, pl.ANY, pl.ANY),
        [
            ((rows, width), F32),
            ((nz, nc, rows, width), BF),
            ((rows, width), BF),
            ((8, width), F32),
            ((nx, ny, nc, nz) + grad_mlp.shape[4:], BF),
            ((nx, ny) + grad_dn.shape[2:], BF),
        ],
        (VM, pl.ANY, VM, VM, pl.ANY, pl.ANY),
        Reduce.buffers(nz, rows, width) * 2
        + [VM((rows, width), BF)]
        + Reduce.SEMS * 2
        + Gather.SEMS
        + [DMA((peers,))] * 4
        + [DMA((3,))],
        3,
    )


def last_kernel(
    dims, part, tokens, dx2, grad_attn,
    input_grad, gain_part, attn_g,
    held, came, came_attn, sums, rs, rr, ds, dr, ss, sr, local,
):
    nx, nc, nz, ny = dims
    x, c, z, y = place()
    greet(*dims)
    reduce = Reduce(part, held, came, rs, rr)
    reduce.start()
    spread = Spread(
        lambda px, py: grad_attn.at[px, :, :, py], lambda px, py: came_attn.at[px, py], ds, dr, local.at[0], nx, ny
    )
    spread.start()
    for k in range(nz - 1):
        reduce.hop(k)
    spread.arrived()

    own = sums.shape[2]

    def add(i, carry):
        at = pl.ds(pl.multiple_of(i * ROWS, ROWS), ROWS)
        for pz in range(nz):
            for pc in range(nc):
                total = came_attn[0, 0, pc, pz, at, :].astype(F32)
                for px, py in others(nx, ny):
                    total = total + came_attn[px, py, pc, pz, at, :].astype(F32)
                sums[pz, pc, at, :] = total.astype(BF)
        return carry

    lax.fori_loop(0, own // ROWS, add, 0)
    swap = Swap(sums, lambda pz, pc: attn_g.at[pz, pc], ss, sr, local.at[1])
    swap.start()
    gain_part[...] = jnp.zeros_like(gain_part)

    def settle(at, total):
        value = tokens[at, :].astype(F32)
        inverse = lax.rsqrt(jnp.mean(value * value, axis=-1, keepdims=True) + EPSILON)
        normed = value * inverse
        gain_part[...] += jnp.sum((total * normed).reshape(ROWS // 8, 8, -1), axis=0)
        input_grad[at, :] = dx2[at, :] + inverse * (
            total - normed * jnp.mean(total * normed, axis=-1, keepdims=True)
        )

    reduce.last(settle)
    reduce.finish()
    spread.finish()
    swap.arrived()
    swap.finish()


def last_call(dims, part, tokens, dx2, grad_attn):
    nx, nc, nz, ny = dims
    rows, width = tokens.shape
    own, cols = grad_attn.shape[4:]
    peers = nx * ny - 1
    return call(
        functools.partial(last_kernel, dims),
        (part, tokens, dx2, grad_attn),
        (VM, VM, VM, pl.ANY),
        [((rows, width), F32), ((8, width), F32), ((nz, nc, own, cols), BF)],
        (VM, VM, VM),
        Reduce.buffers(nz, rows, width)
        + [VM((nx, ny, nc, nz, own, cols), BF), VM((nz, nc, own, cols), BF)]
        + Reduce.SEMS
        + [DMA((peers,))] * 2
        + [DMA((nz * nc - 1,))] * 2
        + [DMA((2,))],
        4,
    )


def team_exchange(blocks):
    return lax.all_to_all(blocks, TEAM, 0, 0, tiled=False)


def turn(values):
    half = values.shape[-1] // 2
    return jnp.concatenate([-values[..., half:], values[..., :half]], axis=-1)


def rope_apply(values, cos_table, sin_table):
    return values * cos_table + turn(values) * sin_table


def rope_reverse(gradient, cos_table, sin_table):
    half = gradient.shape[-1] // 2
    scaled = gradient * sin_table
    return gradient * cos_table + jnp.concatenate(
        [scaled[..., half:], -scaled[..., :half]], axis=-1
    )


def shards(
    tokens, positions, doc_start, cotangent, w_query, w_key, w_value, w_out,
    attn_gain, w_gate, w_up, w_down, mlp_gain,
):
    dims = tuple(lax.axis_size(a) for a in ALL)
    nx, nc, nz, ny = dims
    team = nz * nc
    rows, width = tokens.shape
    own = w_query.shape[0]
    heads = HEADS // team
    qcols = heads * HEAD_DIM
    kv_rep = team // KV_HEADS
    ff = w_gate.shape[1]
    piece = w_down.shape[0]
    ffcols = piece * nx * ny
    y_at = lax.axis_index("y")
    core_at = lax.axis_index("core")
    scale = HEAD_DIM ** (-0.5)

    gain_a = attn_gain.astype(F32)[:, None]
    gain_m = mlp_gain.astype(F32)[:, None]

    def by_heads(w):
        return w.reshape(own, team, -1).transpose(1, 0, 2)

    def by_kv(w):
        return jnp.repeat(w.reshape(own, KV_HEADS, HEAD_DIM).transpose(1, 0, 2), kv_rep, axis=0)

    def scaled(w, gain):
        return (w.astype(F32) * gain).astype(BF)

    def by_ff(w):
        w = w.reshape(own, nx, nc, nz, ny, piece).transpose(3, 2, 0, 1, 4, 5)
        return w.reshape(team, own, ffcols)

    attn_blocks = jnp.concatenate(
        [
            by_heads(scaled(w_query, gain_a)),
            by_kv(scaled(w_key, gain_a)),
            by_kv(scaled(w_value, gain_a)),
            by_heads(w_out.T),
        ],
        axis=-1,
    )
    mlp_blocks = jnp.concatenate([by_ff(scaled(w_gate, gain_m)), by_ff(scaled(w_up, gain_m))], axis=-1)
    mlp_t = team_exchange(mlp_blocks).reshape(nz, nc, own, 2 * ffcols).transpose(1, 0, 2, 3)
    xf = tokens.astype(F32)
    inv1 = lax.rsqrt(jnp.mean(xf * xf, axis=-1, keepdims=True) + EPSILON)
    n1 = xf * inv1
    half = HEAD_DIM // 2
    frequency = 10000.0 ** (-2.0 * jnp.arange(half, dtype=F32) / HEAD_DIM)
    angles = positions.astype(F32)[:, None] * frequency[None, :]
    table = jnp.concatenate(
        [
            jnp.cos(angles),
            jnp.sin(angles),
            jnp.broadcast_to(doc_start.astype(F32)[:, None], (rows, HEAD_DIM)),
        ],
        axis=-1,
    )
    n1g, tab, w_attn = first_call(
        dims, n1.astype(BF), table, attn_blocks.reshape(nz, nc, own, attn_blocks.shape[-1])
    )
    n1g = n1g.reshape(team * rows, width)
    tab = tab.reshape(team * rows, table.shape[1])
    w_attn = w_attn.reshape(width, attn_blocks.shape[-1])
    w_qkv = w_attn[:, : qcols + 2 * HEAD_DIM]
    w_out_t = w_attn[:, qcols + 2 * HEAD_DIM :]
    cos_t = jnp.concatenate([tab[:, :half], tab[:, :half]], axis=-1)
    sin_t = jnp.concatenate([tab[:, half : 2 * half], tab[:, half : 2 * half]], axis=-1)
    starts = tab[:, 2 * half].astype(jnp.int32).reshape(nz, nc, rows)

    qkv = dot_plain(n1g, w_qkv)
    total = team * rows
    q = rope_apply(
        qkv[:, :qcols].reshape(total, heads, HEAD_DIM), cos_t[:, None], sin_t[:, None]
    ).astype(BF)
    k = rope_apply(qkv[:, qcols : qcols + HEAD_DIM], cos_t, sin_t).astype(BF)
    v = qkv[:, qcols + HEAD_DIM :].astype(BF)

    kv_own = jnp.concatenate([k, v], axis=-1).reshape(nz, nc, rows, 2 * HEAD_DIM)
    kv_all = lax.all_gather(kv_own, "y", axis=0).transpose(2, 1, 0, 3, 4)
    kv_all = kv_all.reshape(nc, nz * ny * rows, 2 * HEAD_DIM)
    k_all, v_all = kv_all[..., :HEAD_DIM], kv_all[..., HEAD_DIM:]
    qh = q.reshape(nz, nc, rows, heads, HEAD_DIM).transpose(0, 1, 3, 2, 4)

    def block_scores(z):
        keys = (z + 1) * ny * rows
        s = jnp.einsum("chrd,ckd->chrk", qh[z], k_all[:, :keys], preferred_element_type=F32) * scale
        row_at = (z * ny + y_at) * rows + jnp.arange(rows, dtype=jnp.int32)
        cols = jnp.arange(keys, dtype=jnp.int32)
        allowed = (cols[None, None, :] >= starts[z][:, :, None]) & (
            cols[None, None, :] <= row_at[None, :, None]
        )
        s = jnp.where(allowed[:, None], s, MASKED)
        top = jnp.max(s, axis=-1, keepdims=True)
        e = jnp.exp(s - top)
        return e / jnp.sum(e, axis=-1, keepdims=True), keys

    contexts = []
    for z in range(nz):
        p, keys = block_scores(z)
        contexts.append(
            jnp.einsum("chrk,ckd->chrd", p.astype(BF), v_all[:, :keys], preferred_element_type=F32)
        )
    context = jnp.stack(contexts)
    ob = context.transpose(0, 1, 3, 2, 4).reshape(total, qcols).astype(BF)

    part = dot_right_t(ob, w_out_t).astype(BF).reshape(nz, nc, rows, width)
    mid_f, n2g, cotg, w_mlp, w_dn = middle_call(dims, part, tokens, cotangent, mlp_t, w_down)
    n2g = n2g.reshape(total, width)
    cotg = cotg.reshape(total, width)
    w_mlp = w_mlp.reshape(width, 2 * ffcols)
    w_dn = w_dn.reshape(ffcols, width)
    gt = dot_plain(n2g, w_mlp[:, :ffcols])
    up = dot_plain(n2g, w_mlp[:, ffcols:])
    sg = jax.nn.sigmoid(gt)
    hid = (gt * sg * up).astype(BF)
    mlp_out = dot_plain(hid, w_dn).astype(BF).reshape(nz, nc, rows, width)

    dhid = dot_right_t(cotg, w_dn)
    down_part = dot_left_t(hid, cotg).astype(BF)
    dgt = (dhid * up * sg * (1.0 + gt * (1.0 - sg))).astype(BF)
    dup = (dhid * gt * sg).astype(BF)
    dmlp = jnp.concatenate([dgt, dup], axis=-1)
    dn2 = dot_right_t(dmlp, w_mlp).astype(BF).reshape(nz, nc, rows, width)
    mlp_part = dot_left_t(n2g, dmlp).astype(BF).reshape(nx, nc, nz, ny, own, 2 * ffcols)
    dx2, dag, output, gain_m_part, mlp_came, down_came = back_call(
        dims, dn2, mlp_out, mid_f, cotangent, mlp_part, down_part.reshape(nx, ny, piece, width)
    )
    dag = dag.reshape(total, width)
    gain_m_part = gain_m_part.sum(0)
    out_part = dot_left_t(dag, ob)
    dob = dot_plain(dag, w_out_t).astype(BF)

    doh = dob.reshape(nz, nc, rows, heads, HEAD_DIM).transpose(0, 1, 3, 2, 4)
    delta = jnp.sum(doh.astype(F32) * context, axis=-1)
    dqs = []
    dk = jnp.zeros((nc, nz * ny * rows, HEAD_DIM), F32)
    dv = jnp.zeros((nc, nz * ny * rows, HEAD_DIM), F32)
    for z in range(nz):
        p, keys = block_scores(z)
        dv = dv.at[:, :keys].add(
            jnp.einsum("chrk,chrd->ckd", p.astype(BF), doh[z], preferred_element_type=F32)
        )
        dp = jnp.einsum("chrd,ckd->chrk", doh[z], v_all[:, :keys], preferred_element_type=F32)
        ds = (p * (dp - delta[z][..., None])).astype(BF)
        dqs.append(
            jnp.einsum("chrk,ckd->chrd", ds, k_all[:, :keys], preferred_element_type=F32) * scale
        )
        dk = dk.at[:, :keys].add(
            jnp.einsum("chrk,chrd->ckd", ds, qh[z], preferred_element_type=F32) * scale
        )
    dq = jnp.stack(dqs).transpose(0, 1, 3, 2, 4).reshape(total, heads, HEAD_DIM)
    dkv = jnp.concatenate([dk, dv], axis=-1).astype(BF)
    dkv = dkv.reshape(nc, nz, ny, rows, 2 * HEAD_DIM).transpose(2, 1, 0, 3, 4)
    dkv = lax.all_to_all(dkv, "y", 0, 0, tiled=False).astype(F32).sum(0)
    dkv = dkv.reshape(total, 2 * HEAD_DIM)
    dkv = lax.psum(dkv, "core")
    dka = rope_reverse(dkv[:, :HEAD_DIM], cos_t, sin_t)
    dva = dkv[:, HEAD_DIM:]
    dka = jnp.where(core_at == 0, dka, 0.0)
    dva = jnp.where(core_at == 1, dva, 0.0)
    dqa = rope_reverse(dq, cos_t[:, None], sin_t[:, None]).reshape(total, qcols)
    dqkv = jnp.concatenate([dqa, dka, dva], axis=-1).astype(BF)
    dn1 = dot_right_t(dqkv, w_qkv).astype(BF).reshape(nz, nc, rows, width)
    qkv_part = dot_left_t(n1g, dqkv)
    attn_part = jnp.concatenate([qkv_part, out_part], axis=-1).astype(BF)
    attn_part = attn_part.reshape(nx, nc, nz, ny, own, attn_part.shape[-1])
    input_grad, gain_a_part, attn_g = last_call(dims, dn1, tokens, dx2, attn_part)
    gain_a_part = gain_a_part.sum(0)

    attn_g = attn_g.reshape(team, own, attn_g.shape[-1]).astype(F32)
    mlp_g = jnp.sum(mlp_came.astype(F32), axis=(0, 1)).astype(BF).transpose(1, 0, 2, 3)
    mlp_g = team_exchange(mlp_g.reshape(team, own, 2 * ffcols)).astype(F32)
    grad_down = jnp.sum(down_came.astype(F32), axis=(0, 1))
    grad_query = attn_g[:, :, :qcols].transpose(1, 0, 2).reshape(own, HEADS * HEAD_DIM) * gain_a
    kv_g = attn_g[:, :, qcols : qcols + 2 * HEAD_DIM].reshape(KV_HEADS, kv_rep, own, 2 * HEAD_DIM).sum(1)
    grad_key = kv_g[..., :HEAD_DIM].transpose(1, 0, 2).reshape(own, KV_HEADS * HEAD_DIM) * gain_a
    grad_value = kv_g[..., HEAD_DIM:].transpose(1, 0, 2).reshape(own, KV_HEADS * HEAD_DIM) * gain_a
    grad_out = attn_g[:, :, qcols + 2 * HEAD_DIM :].transpose(1, 0, 2).reshape(own, HEADS * HEAD_DIM).T

    def from_ff(g):
        g = g.reshape(nz, nc, own, nx, ny, piece).transpose(2, 3, 1, 0, 4, 5)
        return g.reshape(own, ff) * gain_m

    grad_gate = from_ff(mlp_g[:, :, :ffcols])
    grad_up = from_ff(mlp_g[:, :, ffcols:])
    gains = jnp.stack([gain_a_part, gain_m_part], 0).reshape(2, nx * team * ny, own).transpose(1, 0, 2)
    gains = lax.all_to_all(gains, ALL, 0, 0, tiled=False).sum(0)
    grad_attn_gain = gains[0] / gain_a[:, 0]
    grad_mlp_gain = gains[1] / gain_m[:, 0]
    return (
        output, input_grad, grad_query, grad_key, grad_value, grad_out,
        grad_attn_gain, grad_gate, grad_up, grad_down, grad_mlp_gain,
    )


def solution(mesh):
    fsdp, seq = mesh.shape["fsdp"], mesh.shape["seq"]
    nc, nz = 2, 4
    grid = Mesh(mesh.devices.reshape(fsdp // nc, nc, nz, seq // nz), ALL)
    row, col, vec = P(ALL, None), P(None, ALL), P(ALL)
    in_specs = (row, vec, vec, row, row, row, row, col, vec, row, row, row, vec)
    out_specs = (row, row, row, row, row, col, vec, row, row, row, vec)
    return jax.shard_map(shards, mesh=grid, in_specs=in_specs, out_specs=out_specs, check_vma=False)
```

```python
import functools

import jax
import jax.numpy as jnp
from jax import lax
from jax.experimental import pallas as pl
from jax.experimental.pallas import tpu as pltpu
from jax.sharding import Mesh
from jax.sharding import PartitionSpec as P

HEADS = 32
KV_HEADS = 4
HEAD_DIM = 64
EPSILON = 1e-05
MASKED = -1e30
ALL = ("x", "core", "z", "y")
TEAM = ("z", "core")
DATA = ("x", "y")
BF = jnp.bfloat16
F32 = jnp.float32


def dot_plain(a, b):
    return jnp.dot(a, b, preferred_element_type=F32)


def dot_right_t(a, b):
    return lax.dot_general(a, b, (((1,), (1,)), ((), ())), preferred_element_type=F32)


def dot_left_t(a, b):
    return lax.dot_general(a, b, (((0,), (0,)), ((), ())), preferred_element_type=F32)


MESH = pl.DeviceIdType.MESH
VM = pltpu.VMEM
DMA = pltpu.SemaphoreType.DMA
ROWS = 16


def place():
    return tuple(lax.axis_index(a) for a in ALL)


def others(nx, ny):
    return [(i, j) for i in range(nx) for j in range(ny) if (i, j) != (0, 0)]


def data_peer(step, nx, ny):
    x, _, _, y = place()
    return lax.rem(x + step[0], nx), lax.rem(y + step[1], ny)


def team_peer(step, nz, nc):
    _, c, z, _ = place()
    return lax.rem(z + step[0], nz), lax.rem(c + step[1], nc)


def greet(nx, nc, nz, ny, cross=False):
    barrier = pltpu.get_barrier_semaphore()
    x, c, z, y = place()
    extra = ny - 1 if cross else 0
    for i in range(extra):
        device = {"y": lax.rem(y + 1 + i, ny), "core": 1 - c}
        pl.semaphore_signal(barrier, inc=1, device_id=device, device_id_type=MESH)
    for step in others(nx, ny):
        px, py = data_peer(step, nx, ny)
        pl.semaphore_signal(barrier, inc=1, device_id={"x": px, "y": py}, device_id_type=MESH)
    for step in others(nz, nc):
        pz, pc = team_peer(step, nz, nc)
        pl.semaphore_signal(barrier, inc=1, device_id={"z": pz, "core": pc}, device_id_type=MESH)
    pl.semaphore_wait(barrier, nx * ny - 1 + nz * nc - 1 + extra)


def remote(source, target, send, recv, device):
    return pltpu.make_async_remote_copy(
        src_ref=source, dst_ref=target, send_sem=send, recv_sem=recv,
        device_id=device, device_id_type=MESH,
    )


class Gather:
    SEMS = [DMA((4, 4)), DMA((2, 4))]

    def __init__(self, own, full, send, recv, local):
        self.own, self.full, self.send, self.recv = own, full, send, recv
        self.x, self.c, self.z, self.y = place()
        self.nz = full.shape[0]
        self.local = pltpu.make_async_copy(own, full.at[self.z, self.c], local)

    def copy(self, at, kind):
        slot = self.full.at[at, self.c]
        device = ({"z": self.z + 1}, {"z": self.z - 1}, {"core": 1 - self.c})[kind]
        return remote(
            slot, slot, self.send.at[kind, at], self.recv.at[0 if kind < 2 else 1, at], device
        )

    def start(self):
        self.local.start()
        self.local.wait()
        pl.when(self.z < self.nz - 1)(lambda: self.copy(self.z, 0).start())
        pl.when(self.z > 0)(lambda: self.copy(self.z, 1).start())
        self.copy(self.z, 2).start()

    def hop(self, far):
        @pl.when(self.z - far >= 0)
        def _():
            at = self.z - far
            self.copy(at, 0).wait_recv()
            pl.when(self.z < self.nz - 1)(lambda: self.copy(at, 0).start())
            self.copy(at, 2).start()

        @pl.when(self.z + far < self.nz)
        def _():
            at = self.z + far
            self.copy(at, 1).wait_recv()
            pl.when(self.z > 0)(lambda: self.copy(at, 1).start())
            self.copy(at, 2).start()

    def finish(self):
        for at in range(self.nz):
            pl.when((at <= self.z) & (self.z < self.nz - 1))(lambda at=at: self.copy(at, 0).wait_send())
            pl.when((at >= self.z) & (self.z > 0))(lambda at=at: self.copy(at, 1).wait_send())
            self.copy(at, 2).wait_send()
            self.copy(at, 2).wait_recv()


class Reduce:
    SEMS = [DMA((3, 4)), DMA((3, 4))]

    @staticmethod
    def buffers(nz, rows, width):
        return [VM((nz, rows, width), BF), VM((2, nz, rows, width), BF)]

    def __init__(self, part, held, came, send, recv):
        self.part, self.held, self.came, self.send, self.recv = part, held, came, send, recv
        self.x, self.c, self.z, self.y = place()
        self.nz, _, self.rows, self.width = part.shape

    def across(self, to):
        return remote(
            self.part.at[to, 1 - self.c], self.held.at[to], self.send.at[2, to], self.recv.at[2, to],
            {"core": 1 - self.c},
        )

    def along(self, to, way):
        device = ({"z": self.z + 1}, {"z": self.z - 1})[way]
        return remote(
            self.held.at[to], self.came.at[way, to], self.send.at[way, to], self.recv.at[way, to], device
        )

    def order(self):
        return [a for k in range(self.nz) for a in (self.nz - 1 - k, k)][: self.nz]

    def start(self):
        for to in self.order():
            self.across(to).start()
        zeros = jnp.zeros((ROWS, self.width), BF)
        for way, end in ((0, 0), (1, self.nz - 1)):

            @pl.when(self.z == end)
            def _(way=way):
                def clear(i, carry):
                    for to in range(self.nz):
                        self.came[way, to, pl.ds(pl.multiple_of(i * ROWS, ROWS), ROWS), :] = zeros
                    return carry

                lax.fori_loop(0, self.rows // ROWS, clear, 0)

    def add(self, to, ways, out=None):
        def body(i, carry):
            at = pl.ds(pl.multiple_of(i * ROWS, ROWS), ROWS)
            total = self.part[to, self.c, at, :].astype(F32) + self.held[to, at, :].astype(F32)
            for way in ways:
                total = total + self.came[way, to, at, :].astype(F32)
            if out is None:
                self.held[to, at, :] = total.astype(BF)
            else:
                out(at, total)
            return carry

        lax.fori_loop(0, self.rows // ROWS, body, 0)

    def hop(self, k):
        for way, to in ((0, self.nz - 1 - k), (1, k)):
            active = (self.z < to) if way == 0 else (self.z > to)
            first = (self.z == 0) if way == 0 else (self.z == self.nz - 1)

            @pl.when(active)
            def _(way=way, to=to, first=first):
                self.across(to).wait_recv()
                pl.when(jnp.logical_not(first))(lambda: self.along(to, way).wait_recv())
                self.add(to, (way,))
                self.along(to, way).start()

    def last(self, out):
        self.across(self.z).wait_recv()
        pl.when(self.z > 0)(lambda: self.along(self.z, 0).wait_recv())
        pl.when(self.z < self.nz - 1)(lambda: self.along(self.z, 1).wait_recv())
        self.add(self.z, (0, 1), out)

    def finish(self):
        for to in range(self.nz):
            self.across(to).wait_send()
            pl.when(self.z < to)(lambda to=to: self.along(to, 0).wait_send())
            pl.when(self.z > to)(lambda to=to: self.along(to, 1).wait_send())


class Spread:
    def __init__(self, source, target, send, recv, local, nx, ny):
        self.source, self.target, self.send, self.recv = source, target, send, recv
        self.nx, self.ny = nx, ny
        self.x, _, _, self.y = place()
        self.local = pltpu.make_async_copy(source(self.x, self.y), target(self.x, self.y), local)

    def copies(self):
        for i, step in enumerate(others(self.nx, self.ny)):
            px, py = data_peer(step, self.nx, self.ny)
            yield remote(
                self.source(px, py), self.target(self.x, self.y), self.send.at[i], self.recv.at[i],
                {"x": px, "y": py},
            )

    def start(self):
        for copy in self.copies():
            copy.start()
        self.local.start()

    def arrived(self):
        self.local.wait()
        for copy in self.copies():
            copy.wait_recv()

    def finish(self):
        for copy in self.copies():
            copy.wait_send()


class Swap:
    def __init__(self, blocks, slot, send, recv, local):
        self.blocks, self.slot, self.send, self.recv = blocks, slot, send, recv
        self.nz, self.nc = blocks.shape[:2]
        _, self.c, self.z, _ = place()
        self.local = pltpu.make_async_copy(blocks.at[self.z, self.c], slot(self.z, self.c), local)

    def copies(self):
        for i, step in enumerate(others(self.nz, self.nc)):
            pz, pc = team_peer(step, self.nz, self.nc)
            yield remote(
                self.blocks.at[pz, pc], self.slot(self.z, self.c), self.send.at[i], self.recv.at[i],
                {"z": pz, "core": pc},
            )

    def start(self):
        for copy in self.copies():
            copy.start()
        self.local.start()

    def arrived(self):
        self.local.wait()
        for copy in self.copies():
            copy.wait_recv()

    def finish(self):
        for copy in self.copies():
            copy.wait_send()


def call(kernel, operands, in_spaces, outs, out_spaces, scratch, number):
    return pl.pallas_call(
        kernel,
        out_shape=[jax.ShapeDtypeStruct(s, t) for s, t in outs],
        in_specs=[pl.BlockSpec(memory_space=s) for s in in_spaces],
        out_specs=[pl.BlockSpec(memory_space=s) for s in out_spaces],
        scratch_shapes=scratch,
        compiler_params=pltpu.CompilerParams(
            collective_id=number, has_side_effects=True, vmem_limit_bytes=56 << 20
        ),
    )(*operands)


def first_kernel(dims, n1, table, blocks, n1g, tabg, w_attn, gs, gr, ts, tr, ss, sr, ds, dr, local):
    nx, nc, nz, ny = dims
    x, c, z, y = place()
    greet(*dims)
    swap = Swap(blocks, lambda pz, pc: w_attn.at[x, pc, pz, y], ss, sr, local.at[0])
    rows = Gather(n1, n1g, gs, gr, local.at[1])
    tabs = Gather(table, tabg, ts, tr, local.at[2])
    swap.start()
    tabs.start()
    rows.start()
    swap.arrived()
    spread = Spread(
        lambda px, py: w_attn.at[x, :, :, y], lambda px, py: w_attn.at[px, :, :, py], ds, dr, local.at[3], nx, ny
    )
    for copy in spread.copies():
        copy.start()
    for far in range(1, nz):
        tabs.hop(far)
        rows.hop(far)
    tabs.finish()
    rows.finish()
    swap.finish()
    for copy in spread.copies():
        copy.wait_recv()
    spread.finish()


def first_call(dims, n1, table, blocks):
    nx, nc, nz, ny = dims
    rows, width = n1.shape
    own, cols = blocks.shape[2:]
    peers = nx * ny - 1
    return call(
        functools.partial(first_kernel, dims),
        (n1, table, blocks),
        (VM, VM, pl.ANY),
        [
            ((nz, nc, rows, width), BF),
            ((nz, nc) + table.shape, F32),
            ((nx, nc, nz, ny, own, cols), BF),
        ],
        (pl.ANY, pl.ANY, pl.ANY),
        Gather.SEMS * 2 + [DMA((nz * nc - 1,))] * 2 + [DMA((peers,))] * 2 + [DMA((4,))],
        1,
    )


def middle_kernel(
    dims, part, tokens, cot, mlp_t, down,
    mid, n2g, cotg, w_mlp, w_dn,
    held, came, n2, rs, rr, ns, nr, cs, cr, ms, mr, ws, wr, local,
):
    nx, nc, nz, ny = dims
    x, c, z, y = place()
    greet(*dims)
    reduce = Reduce(part, held, came, rs, rr)
    cots = Gather(cot, cotg, cs, cr, local.at[0])
    gu = Spread(lambda px, py: mlp_t, lambda px, py: w_mlp.at[px, :, :, py], ms, mr, local.at[1], nx, ny)
    dn = Spread(lambda px, py: down, lambda px, py: w_dn.at[px, py], ws, wr, local.at[2], nx, ny)
    reduce.start()
    gu.start()
    dn.start()
    cots.start()
    for k in range(nz - 1):
        reduce.hop(k)
        cots.hop(k + 1)

    def settle(at, total):
        value = tokens[at, :].astype(F32) + total
        mid[at, :] = value
        inverse = lax.rsqrt(jnp.mean(value * value, axis=-1, keepdims=True) + EPSILON)
        n2[at, :] = (value * inverse).astype(BF)

    reduce.last(settle)
    rows = Gather(n2, n2g, ns, nr, local.at[3])
    rows.start()
    for far in range(1, nz):
        rows.hop(far)
    rows.finish()
    cots.finish()
    reduce.finish()
    gu.arrived()
    dn.arrived()
    gu.finish()
    dn.finish()


def middle_call(dims, part, tokens, cot, mlp_t, down):
    nx, nc, nz, ny = dims
    rows, width = tokens.shape
    peers = nx * ny - 1
    return call(
        functools.partial(middle_kernel, dims),
        (part, tokens, cot, mlp_t, down),
        (VM, VM, VM, pl.ANY, pl.ANY),
        [
            ((rows, width), F32),
            ((nz, nc, rows, width), BF),
            ((nz, nc, rows, width), BF),
            ((nx, nc, nz, ny) + mlp_t.shape[2:], BF),
            ((nx, ny) + down.shape, BF),
        ],
        (VM, pl.ANY, pl.ANY, pl.ANY, pl.ANY),
        Reduce.buffers(nz, rows, width)
        + [VM((rows, width), BF)]
        + Reduce.SEMS
        + Gather.SEMS * 2
        + [DMA((peers,))] * 4
        + [DMA((4,))],
        2,
    )


def back_kernel(
    dims, part, mlp_part, mid, cot, grad_mlp, grad_dn,
    dx2, dag, output, gain_part, came_mlp, came_dn,
    held, came, held2, came2, low, rs, rr, os, orr, ds, dr, ms, mr, ws, wr, local,
):
    nx, nc, nz, ny = dims
    x, c, z, y = place()
    greet(*dims)
    reduce = Reduce(part, held, came, rs, rr)
    reduce2 = Reduce(mlp_part, held2, came2, os, orr)
    reduce.start()
    dn = Spread(lambda px, py: grad_dn.at[px, py], lambda px, py: came_dn.at[px, py], ws, wr, local.at[0], nx, ny)
    gu = Spread(
        lambda px, py: grad_mlp.at[px, :, :, py], lambda px, py: came_mlp.at[px, py], ms, mr, local.at[1], nx, ny
    )
    gu.start()
    dn.start()
    for k in range(nz - 1):
        reduce.hop(k)
    gain_part[...] = jnp.zeros_like(gain_part)

    def settle(at, total):
        value = mid[at, :]
        inverse = lax.rsqrt(jnp.mean(value * value, axis=-1, keepdims=True) + EPSILON)
        normed = value * inverse
        gain_part[...] += jnp.sum((total * normed).reshape(ROWS // 8, 8, -1), axis=0)
        gradient = cot[at, :].astype(F32) + inverse * (
            total - normed * jnp.mean(total * normed, axis=-1, keepdims=True)
        )
        dx2[at, :] = gradient
        low[at, :] = gradient.astype(BF)

    reduce.last(settle)
    rows = Gather(low, dag, ds, dr, local.at[2])
    rows.start()
    reduce2.start()
    for k in range(nz - 1):
        rows.hop(k + 1)
        reduce2.hop(k)

    def finish(at, total):
        output[at, :] = (mid[at, :] + total).astype(BF)

    reduce2.last(finish)
    rows.finish()
    reduce.finish()
    reduce2.finish()
    gu.arrived()
    dn.arrived()
    gu.finish()
    dn.finish()


def back_call(dims, part, mlp_part, mid, cot, grad_mlp, grad_dn):
    nx, nc, nz, ny = dims
    rows, width = mid.shape
    peers = nx * ny - 1
    return call(
        functools.partial(back_kernel, dims),
        (part, mlp_part, mid, cot, grad_mlp, grad_dn),
        (VM, VM, VM, VM, pl.ANY, pl.ANY),
        [
            ((rows, width), F32),
            ((nz, nc, rows, width), BF),
            ((rows, width), BF),
            ((8, width), F32),
            ((nx, ny, nc, nz) + grad_mlp.shape[4:], BF),
            ((nx, ny) + grad_dn.shape[2:], BF),
        ],
        (VM, pl.ANY, VM, VM, pl.ANY, pl.ANY),
        Reduce.buffers(nz, rows, width) * 2
        + [VM((rows, width), BF)]
        + Reduce.SEMS * 2
        + Gather.SEMS
        + [DMA((peers,))] * 4
        + [DMA((3,))],
        3,
    )


def last_kernel(
    dims, part, tokens, dx2, grad_attn,
    input_grad, gain_part, attn_g,
    held, came, came_attn, sums, rs, rr, ds, dr, ss, sr, local,
):
    nx, nc, nz, ny = dims
    x, c, z, y = place()
    greet(*dims)
    reduce = Reduce(part, held, came, rs, rr)
    reduce.start()
    spread = Spread(
        lambda px, py: grad_attn.at[px, :, :, py], lambda px, py: came_attn.at[px, py], ds, dr, local.at[0], nx, ny
    )
    spread.start()
    for k in range(nz - 1):
        reduce.hop(k)
    spread.arrived()

    own = sums.shape[2]

    def add(i, carry):
        at = pl.ds(pl.multiple_of(i * ROWS, ROWS), ROWS)
        for pz in range(nz):
            for pc in range(nc):
                total = came_attn[0, 0, pc, pz, at, :].astype(F32)
                for px, py in others(nx, ny):
                    total = total + came_attn[px, py, pc, pz, at, :].astype(F32)
                sums[pz, pc, at, :] = total.astype(BF)
        return carry

    lax.fori_loop(0, own // ROWS, add, 0)
    swap = Swap(sums, lambda pz, pc: attn_g.at[pz, pc], ss, sr, local.at[1])
    swap.start()
    gain_part[...] = jnp.zeros_like(gain_part)

    def settle(at, total):
        value = tokens[at, :].astype(F32)
        inverse = lax.rsqrt(jnp.mean(value * value, axis=-1, keepdims=True) + EPSILON)
        normed = value * inverse
        gain_part[...] += jnp.sum((total * normed).reshape(ROWS // 8, 8, -1), axis=0)
        input_grad[at, :] = dx2[at, :] + inverse * (
            total - normed * jnp.mean(total * normed, axis=-1, keepdims=True)
        )

    reduce.last(settle)
    reduce.finish()
    spread.finish()
    swap.arrived()
    swap.finish()


def last_call(dims, part, tokens, dx2, grad_attn):
    nx, nc, nz, ny = dims
    rows, width = tokens.shape
    own, cols = grad_attn.shape[4:]
    peers = nx * ny - 1
    return call(
        functools.partial(last_kernel, dims),
        (part, tokens, dx2, grad_attn),
        (VM, VM, VM, pl.ANY),
        [((rows, width), F32), ((8, width), F32), ((nz, nc, own, cols), BF)],
        (VM, VM, VM),
        Reduce.buffers(nz, rows, width)
        + [VM((nx, ny, nc, nz, own, cols), BF), VM((nz, nc, own, cols), BF)]
        + Reduce.SEMS
        + [DMA((peers,))] * 2
        + [DMA((nz * nc - 1,))] * 2
        + [DMA((2,))],
        4,
    )


def nt(a, b):
    return lax.dot_general(a, b, (((1,), (1,)), ((), ())), preferred_element_type=F32)


def nn(a, b):
    return jnp.dot(a, b, preferred_element_type=F32)


def lanes(shape):
    return lax.broadcasted_iota(jnp.int32, shape, len(shape) - 1)


def rope_lanes(tab):
    at = lanes(tab.shape)
    cos = jnp.where(at < 32, tab, 0.0)
    sin = jnp.where((at >= 32) & (at < 64), tab, 0.0)
    cos = cos + pltpu.roll(cos, 32, 1)
    cos = cos + pltpu.roll(cos, 64, 1)
    sin = sin - pltpu.roll(sin, 96, 1)
    sin = sin + pltpu.roll(sin, 64, 1)
    return cos, sin


def swap_halves(u):
    return jnp.where(lax.rem(lanes(u.shape), 64) < 32, pltpu.roll(u, 96, 1), pltpu.roll(u, 32, 1))


def two_heads(u):
    first = lanes(u.shape) < 64
    zero = jnp.zeros_like(u)
    return jnp.concatenate([jnp.where(first, u, zero), jnp.where(first, zero, u)], axis=0)


def join_heads(t):
    rows = t.shape[1] // 2
    return jnp.concatenate([t[:64, :rows], t[64:, rows:]], axis=0).T


def bias_of(tab, keys, first_row):
    rows = tab.shape[0]
    starts = tab.T[64:65, :].astype(jnp.int32)
    key = lax.broadcasted_iota(jnp.int32, (keys, rows), 0)
    row = first_row + lax.broadcasted_iota(jnp.int32, (keys, rows), 1)
    bias = jnp.where((key >= starts) & (key <= row), 0.0, MASKED)
    return jnp.concatenate([bias, bias], axis=1)


def attend_kernel(
    dims, n1g, w, tab, mlp_blocks,
    q, kk, vv, stat, ob, part, mlp_t,
    kv, vt, ss, sr, ys, yr, local,
):
    nx, nc, nz, ny = dims
    x, c, z, y = place()
    rows, width = n1g.shape[2:]
    qcols = q.shape[-1]
    pairs = qcols // 128
    greet(*dims)
    swap = Swap(mlp_blocks, lambda pz, pc: mlp_t.at[pc, pz], ss, sr, local.at[0])
    swap.start()

    def project(i, carry):
        res = nn(n1g[i].reshape(nc * rows, width), w[:, : qcols + 128])
        cos, sin = rope_lanes(tab[i].reshape(nc * rows, 128))
        for p in range(pairs):
            u = res[:, p * 128 : p * 128 + 128]
            u = (u * cos + swap_halves(u) * sin) * (HEAD_DIM ** (-0.5))
            q[i, :, :, p * 128 : p * 128 + 128] = u.astype(BF).reshape(nc, rows, 128)
        u = res[:, qcols : qcols + 128]
        u = jnp.where(lanes(u.shape) < 64, u * cos + swap_halves(u) * sin, u).astype(BF)
        for pc in range(nc):
            kv[pc, i, y] = u[pc * rows : (pc + 1) * rows]
        return carry

    lax.fori_loop(0, nz, project, 0)
    sends = []
    for i in range(ny - 1):
        slot = kv.at[:, :, y]
        sends.append(remote(slot, slot, ys.at[i], yr.at[i], {"y": lax.rem(y + 1 + i, ny)}))
    for copy in sends:
        copy.start()
    for copy in sends:
        copy.wait_recv()

    span = ny * rows

    def double(i, carry):
        pc, pz = i // nz, lax.rem(i, nz)
        u = kv[pc, pz].reshape(span, 128).astype(F32)
        r = pltpu.roll(u, 64, 1)
        first = lanes(u.shape) < 64
        at = pl.ds(pl.multiple_of(pz * span, span), span)
        kk[pc, at, :] = jnp.where(first, u, r).astype(BF)
        values = jnp.where(first, r, u)
        vv[pc, at, :] = values.astype(BF)
        vt[pc, :, at] = values.T.astype(BF)
        return carry

    lax.fori_loop(0, nc * nz, double, 0)

    def attend(pc, carry):
        for pz in range(nz):
            keys = (pz + 1) * span
            bias = bias_of(tab[pz, pc], keys, (pz * ny + y) * rows)
            for p in range(pairs):
                q2 = two_heads(q[pz, pc, :, p * 128 : p * 128 + 128])
                s = nt(kk[pc, :keys, :], q2) + bias
                top = jnp.max(s, axis=0, keepdims=True)
                e = jnp.exp(s - top)
                total = jnp.sum(e, axis=0, keepdims=True)
                stat[pz, pc, p : p + 1, :] = top + jnp.log(total)
                weights = (e * (1.0 / total)).astype(BF)
                o = join_heads(nn(vt[pc, :, :keys], weights))
                ob[pz, pc, :, p * 128 : p * 128 + 128] = o.astype(BF)
        return carry

    lax.fori_loop(0, nc, attend, 0)

    def output(i, carry):
        pz, n = i // 4, lax.rem(i, 4)
        at = pl.ds(pl.multiple_of(n * (width // 4), width // 4), width // 4)
        res = nt(ob[pz].reshape(nc * rows, qcols), w[at, qcols + 128 : 2 * qcols + 128])
        part[pz, :, :, at] = res.astype(BF).reshape(nc, rows, width // 4)
        return carry

    lax.fori_loop(0, nz * 4, output, 0)
    for copy in sends:
        copy.wait_send()
    swap.arrived()
    swap.finish()


def attend_call(dims, n1g, w, tab, mlp_blocks):
    nx, nc, nz, ny = dims
    rows, width = n1g.shape[2:]
    qcols = (w.shape[1] - 128) // 2
    keys = nz * ny * rows
    members = nz * nc - 1
    own, cols = mlp_blocks.shape[2:]
    return call(
        functools.partial(attend_kernel, dims),
        (n1g, w, tab, mlp_blocks),
        (VM, VM, VM, pl.ANY),
        [
            ((nz, nc, rows, qcols), BF),
            ((nc, keys, 128), BF),
            ((nc, keys, 128), BF),
            ((nz, nc, 8, 2 * rows), F32),
            ((nz, nc, rows, qcols), BF),
            ((nz, nc, rows, width), BF),
            ((nc, nz, own, cols), BF),
        ],
        (VM, VM, VM, VM, VM, VM, pl.ANY),
        [VM((nc, nz, ny, rows, 128), BF), VM((nc, 128, keys), BF)]
        + [DMA((members,))] * 2
        + [DMA((max(ny - 1, 1),))] * 2
        + [DMA((1,))],
        5,
    )


def attend_back_kernel(
    dims, dag, w, tab, q, kk, vv, stat, mlp_sum,
    dqkv, part, mlp_g,
    do, kt, dk, dv, out, came, ss, sr, ys, yr, local,
):
    nx, nc, nz, ny = dims
    x, c, z, y = place()
    rows, width = dag.shape[2:]
    qcols = q.shape[-1]
    pairs = qcols // 128
    span = ny * rows
    greet(*dims, cross=True)
    swap = Swap(mlp_sum, lambda pz, pc: mlp_g.at[pz, pc], ss, sr, local.at[0])
    swap.start()

    def project(i, carry):
        res = nn(dag[i].reshape(nc * rows, width), w[:, qcols + 128 : 2 * qcols + 128])
        do[i] = res.astype(BF).reshape(nc, rows, qcols)
        return carry

    lax.fori_loop(0, nz, project, 0)

    def turned(i, carry):
        pc, pz = i // nz, lax.rem(i, nz)
        at = pl.ds(pl.multiple_of(pz * span, span), span)
        kt[pc, :, at] = kk[pc, at, :].astype(F32).T.astype(BF)
        return carry

    lax.fori_loop(0, nc * nz, turned, 0)

    def attend(pc, carry):
        for pz in reversed(range(nz)):
            keys = (pz + 1) * span
            bias = bias_of(tab[pz, pc], keys, (pz * ny + y) * rows)
            cos, sin = rope_lanes(tab[pz, pc])
            for p in range(pairs):
                q2 = two_heads(q[pz, pc, :, p * 128 : p * 128 + 128])
                do2 = two_heads(do[pz, pc, :, p * 128 : p * 128 + 128])
                s = nt(kk[pc, :keys, :], q2) + bias
                weights = jnp.exp(s - stat[pz, pc, p : p + 1, :])
                dw = nt(vv[pc, :keys, :], do2)
                dw = weights * dw
                delta = jnp.sum(dw, axis=0, keepdims=True)
                ds = (dw - weights * delta).astype(BF)
                dv_new = nn(weights.astype(BF), do2)
                dk_new = nn(ds, q2)
                if pz == nz - 1 and p == 0:
                    dv[pc, :keys, :] = dv_new
                    dk[pc, :keys, :] = dk_new
                else:
                    dv[pc, :keys, :] += dv_new
                    dk[pc, :keys, :] += dk_new
                u = join_heads(nn(kt[pc, :, :keys], ds)) * (HEAD_DIM ** (-0.5))
                u = u * cos - swap_halves(u) * sin
                dqkv[pz, pc, :, p * 128 : p * 128 + 128] = u.astype(BF)
        return carry

    lax.fori_loop(0, nc, attend, 0)

    def fold(i, carry):
        pc, pz = i // nz, lax.rem(i, nz)
        at = pl.ds(pl.multiple_of(pz * span, span), span)
        key, value = dk[pc, at, :], dv[pc, at, :]
        first = lanes(key.shape) < 64
        both = jnp.where(first, key + pltpu.roll(key, 64, 1), value + pltpu.roll(value, 64, 1))
        both = both.astype(BF)
        for py in range(ny):
            out[pc, py, pz] = both[py * rows : (py + 1) * rows]
        return carry

    lax.fori_loop(0, nc * nz, fold, 0)
    sends = []
    for i, (sy, sc) in enumerate(others(ny, nc)):
        py, pc = lax.rem(y + sy, ny), lax.rem(c + sc, nc)
        sends.append(remote(out.at[pc, py], came.at[i], ys.at[i], yr.at[i], {"y": py, "core": pc}))
    for copy in sends:
        copy.start()
    for copy in sends:
        copy.wait_recv()

    def settle(pz, carry):
        total = out[c, y, pz].astype(F32)
        for i in range(len(sends)):
            total = total + came[i, pz].astype(F32)
        cos, sin = rope_lanes(tab[pz, c])
        first = lanes(total.shape) < 64
        total = jnp.where(first, total * cos - swap_halves(total) * sin, total)
        dqkv[pz, c, :, qcols : qcols + 128] = total.astype(BF)
        dqkv[pz, 1 - c, :, qcols : qcols + 128] = jnp.zeros((rows, 128), BF)
        return carry

    lax.fori_loop(0, nz, settle, 0)

    def output(i, carry):
        pz, n = i // 4, lax.rem(i, 4)
        at = pl.ds(pl.multiple_of(n * (width // 4), width // 4), width // 4)
        res = nt(dqkv[pz].reshape(nc * rows, qcols + 128), w[at, : qcols + 128])
        part[pz, :, :, at] = res.astype(BF).reshape(nc, rows, width // 4)
        return carry

    lax.fori_loop(0, nz * 4, output, 0)
    for copy in sends:
        copy.wait_send()
    swap.arrived()
    swap.finish()


def attend_back_call(dims, dag, w, tab, q, kk, vv, stat, mlp_sum):
    nx, nc, nz, ny = dims
    rows, width = dag.shape[2:]
    qcols = q.shape[-1]
    keys = nz * ny * rows
    members = nz * nc - 1
    near = ny * nc - 1
    own, cols = mlp_sum.shape[2:]
    return call(
        functools.partial(attend_back_kernel, dims),
        (dag, w, tab, q, kk, vv, stat, mlp_sum),
        (VM, VM, VM, VM, VM, VM, VM, pl.ANY),
        [
            ((nz, nc, rows, qcols + 128), BF),
            ((nz, nc, rows, width), BF),
            ((nz, nc, own, cols), BF),
        ],
        (VM, VM, pl.ANY),
        [
            VM((nz, nc, rows, qcols), BF),
            VM((nc, 128, keys), BF),
            VM((nc, keys, 128), F32),
            VM((nc, keys, 128), F32),
            VM((nc, ny, nz, rows, 128), BF),
            VM((near, nz, rows, 128), BF),
        ]
        + [DMA((members,))] * 2
        + [DMA((near,))] * 2
        + [DMA((1,))],
        6,
    )


def shards(
    tokens, positions, doc_start, cotangent, w_query, w_key, w_value, w_out,
    attn_gain, w_gate, w_up, w_down, mlp_gain,
):
    dims = tuple(lax.axis_size(a) for a in ALL)
    nx, nc, nz, ny = dims
    team = nz * nc
    rows, width = tokens.shape
    own = w_query.shape[0]
    heads = HEADS // team
    qcols = heads * HEAD_DIM
    kv_rep = team // KV_HEADS
    ff = w_gate.shape[1]
    piece = w_down.shape[0]
    ffcols = piece * nx * ny

    gain_a = attn_gain.astype(F32)[:, None]
    gain_m = mlp_gain.astype(F32)[:, None]

    def by_heads(w):
        return w.reshape(own, team, -1).transpose(1, 0, 2)

    def by_kv(w):
        return jnp.repeat(w.reshape(own, KV_HEADS, HEAD_DIM).transpose(1, 0, 2), kv_rep, axis=0)

    def scaled(w, gain):
        return (w.astype(F32) * gain).astype(BF)

    def by_ff(w):
        w = w.reshape(own, nx, nc, nz, ny, piece).transpose(3, 2, 0, 1, 4, 5)
        return w.reshape(team, own, ffcols)

    attn_blocks = jnp.concatenate(
        [
            by_heads(scaled(w_query, gain_a)),
            by_kv(scaled(w_key, gain_a)),
            by_kv(scaled(w_value, gain_a)),
            by_heads(w_out.T),
        ],
        axis=-1,
    )
    mlp_blocks = jnp.concatenate([by_ff(scaled(w_gate, gain_m)), by_ff(scaled(w_up, gain_m))], axis=-1)
    xf = tokens.astype(F32)
    inv1 = lax.rsqrt(jnp.mean(xf * xf, axis=-1, keepdims=True) + EPSILON)
    n1 = xf * inv1
    half = HEAD_DIM // 2
    frequency = 10000.0 ** (-2.0 * jnp.arange(half, dtype=F32) / HEAD_DIM)
    angles = positions.astype(F32)[:, None] * frequency[None, :]
    table = jnp.concatenate(
        [
            jnp.cos(angles),
            jnp.sin(angles),
            jnp.broadcast_to(doc_start.astype(F32)[:, None], (rows, HEAD_DIM)),
        ],
        axis=-1,
    )
    n1g, tab, w_attn = first_call(
        dims, n1.astype(BF), table, attn_blocks.reshape(nz, nc, own, attn_blocks.shape[-1])
    )
    w_attn = w_attn.reshape(width, attn_blocks.shape[-1])
    total = team * rows
    q, kk, vv, stat, ob, part, mlp_t = attend_call(
        dims, n1g, w_attn, tab, mlp_blocks.reshape(nz, nc, own, 2 * ffcols)
    )
    mid_f, n2g, cotg, w_mlp, w_dn = middle_call(dims, part, tokens, cotangent, mlp_t, w_down)
    n2g = n2g.reshape(total, width)
    cotg = cotg.reshape(total, width)
    w_mlp = w_mlp.reshape(width, 2 * ffcols)
    w_dn = w_dn.reshape(ffcols, width)
    gt = dot_plain(n2g, w_mlp[:, :ffcols])
    up = dot_plain(n2g, w_mlp[:, ffcols:])
    sg = jax.nn.sigmoid(gt)
    hid = (gt * sg * up).astype(BF)
    mlp_out = dot_plain(hid, w_dn).astype(BF).reshape(nz, nc, rows, width)

    dhid = dot_right_t(cotg, w_dn)
    down_part = dot_left_t(hid, cotg).astype(BF)
    dgt = (dhid * up * sg * (1.0 + gt * (1.0 - sg))).astype(BF)
    dup = (dhid * gt * sg).astype(BF)
    dmlp = jnp.concatenate([dgt, dup], axis=-1)
    dn2 = dot_right_t(dmlp, w_mlp).astype(BF).reshape(nz, nc, rows, width)
    mlp_part = dot_left_t(n2g, dmlp).astype(BF).reshape(nx, nc, nz, ny, own, 2 * ffcols)
    dx2, dag, output, gain_m_part, mlp_came, down_came = back_call(
        dims, dn2, mlp_out, mid_f, cotangent, mlp_part, down_part.reshape(nx, ny, piece, width)
    )
    gain_m_part = gain_m_part.sum(0)
    mlp_sum = jnp.sum(mlp_came.astype(F32), axis=(0, 1)).astype(BF).transpose(1, 0, 2, 3)
    dqkv, dn1, mlp_g = attend_back_call(dims, dag, w_attn, tab, q, kk, vv, stat, mlp_sum)
    out_part = dot_left_t(dag.reshape(total, width), ob.reshape(total, qcols))
    qkv_part = dot_left_t(n1g.reshape(total, width), dqkv.reshape(total, qcols + 128))
    attn_part = jnp.concatenate([qkv_part, out_part], axis=-1).astype(BF)
    attn_part = attn_part.reshape(nx, nc, nz, ny, own, attn_part.shape[-1])
    input_grad, gain_a_part, attn_g = last_call(dims, dn1, tokens, dx2, attn_part)
    gain_a_part = gain_a_part.sum(0)

    attn_g = attn_g.reshape(team, own, attn_g.shape[-1]).astype(F32)
    mlp_g = mlp_g.reshape(team, own, 2 * ffcols).astype(F32)
    grad_down = jnp.sum(down_came.astype(F32), axis=(0, 1))
    grad_query = attn_g[:, :, :qcols].transpose(1, 0, 2).reshape(own, HEADS * HEAD_DIM) * gain_a
    kv_g = attn_g[:, :, qcols : qcols + 2 * HEAD_DIM].reshape(KV_HEADS, kv_rep, own, 2 * HEAD_DIM).sum(1)
    grad_key = kv_g[..., :HEAD_DIM].transpose(1, 0, 2).reshape(own, KV_HEADS * HEAD_DIM) * gain_a
    grad_value = kv_g[..., HEAD_DIM:].transpose(1, 0, 2).reshape(own, KV_HEADS * HEAD_DIM) * gain_a
    grad_out = attn_g[:, :, qcols + 2 * HEAD_DIM :].transpose(1, 0, 2).reshape(own, HEADS * HEAD_DIM).T

    def from_ff(g):
        g = g.reshape(nz, nc, own, nx, ny, piece).transpose(2, 3, 1, 0, 4, 5)
        return g.reshape(own, ff) * gain_m

    grad_gate = from_ff(mlp_g[:, :, :ffcols])
    grad_up = from_ff(mlp_g[:, :, ffcols:])
    gains = jnp.stack([gain_a_part, gain_m_part], 0).reshape(2, nx * team * ny, own).transpose(1, 0, 2)
    gains = lax.all_to_all(gains, ALL, 0, 0, tiled=False).sum(0)
    grad_attn_gain = gains[0] / gain_a[:, 0]
    grad_mlp_gain = gains[1] / gain_m[:, 0]
    return (
        output, input_grad, grad_query, grad_key, grad_value, grad_out,
        grad_attn_gain, grad_gate, grad_up, grad_down, grad_mlp_gain,
    )


def solution(mesh):
    fsdp, seq = mesh.shape["fsdp"], mesh.shape["seq"]
    nc, nz = 2, 4
    grid = Mesh(mesh.devices.reshape(fsdp // nc, nc, nz, seq // nz), ALL)
    row, col, vec = P(ALL, None), P(None, ALL), P(ALL)
    in_specs = (row, vec, vec, row, row, row, row, col, vec, row, row, row, vec)
    out_specs = (row, row, row, row, row, col, vec, row, row, row, vec)
    return jax.shard_map(shards, mesh=grid, in_specs=in_specs, out_specs=out_specs, check_vma=False)
```

```python
import functools

import jax
import jax.numpy as jnp
from jax import lax
from jax.experimental import pallas as pl
from jax.experimental.pallas import tpu as pltpu
from jax.sharding import Mesh
from jax.sharding import PartitionSpec as P

HEADS = 32
KV_HEADS = 4
HEAD_DIM = 64
EPSILON = 1e-05
MASKED = -1e30
ALL = ("x", "core", "z", "y")
TEAM = ("z", "core")
DATA = ("x", "y")
BF = jnp.bfloat16
F32 = jnp.float32


def dot_plain(a, b):
    return jnp.dot(a, b, preferred_element_type=F32)


def dot_right_t(a, b):
    return lax.dot_general(a, b, (((1,), (1,)), ((), ())), preferred_element_type=F32)


def dot_left_t(a, b):
    return lax.dot_general(a, b, (((0,), (0,)), ((), ())), preferred_element_type=F32)


MESH = pl.DeviceIdType.MESH
VM = pltpu.VMEM
DMA = pltpu.SemaphoreType.DMA
ROWS = 16
PARTS = 2
WINDOW = 2


def place():
    return tuple(lax.axis_index(a) for a in ALL)


def others(nx, ny):
    return [(i, j) for i in range(nx) for j in range(ny) if (i, j) != (0, 0)]


def data_peer(step, nx, ny):
    x, _, _, y = place()
    return lax.rem(x + step[0], nx), lax.rem(y + step[1], ny)


def team_peer(step, nz, nc):
    _, c, z, _ = place()
    return lax.rem(z + step[0], nz), lax.rem(c + step[1], nc)


def greet(nx, nc, nz, ny, cross=False):
    barrier = pltpu.get_barrier_semaphore()
    x, c, z, y = place()
    extra = ny - 1 if cross else 0
    for i in range(extra):
        device = {"y": lax.rem(y + 1 + i, ny), "core": 1 - c}
        pl.semaphore_signal(barrier, inc=1, device_id=device, device_id_type=MESH)
    for step in others(nx, ny):
        px, py = data_peer(step, nx, ny)
        pl.semaphore_signal(barrier, inc=1, device_id={"x": px, "y": py}, device_id_type=MESH)
    for step in others(nz, nc):
        pz, pc = team_peer(step, nz, nc)
        pl.semaphore_signal(barrier, inc=1, device_id={"z": pz, "core": pc}, device_id_type=MESH)
    pl.semaphore_wait(barrier, nx * ny - 1 + nz * nc - 1 + extra)


def remote(source, target, send, recv, device):
    return pltpu.make_async_remote_copy(
        src_ref=source, dst_ref=target, send_sem=send, recv_sem=recv,
        device_id=device, device_id_type=MESH,
    )


def piece_of(part, rows):
    return pl.ds(part * (rows // PARTS), rows // PARTS)


class Gather:
    SEMS = [DMA((3, 4, PARTS)), DMA((2, 4, PARTS)), DMA((PARTS,))]

    def __init__(self, own, full, send, recv, local):
        self.own, self.full, self.send, self.recv, self.local = own, full, send, recv, local
        self.x, self.c, self.z, self.y = place()
        self.nz, _, self.rows = full.shape[:3]

    def copy(self, at, kind, part, mine=False):
        rows = piece_of(part, self.rows)
        slot = self.full.at[at, self.c, rows]
        device = ({"z": self.z + 1}, {"z": self.z - 1}, {"core": 1 - self.c})[kind]
        return remote(
            self.own.at[rows] if mine else slot, slot, self.send.at[kind, at, part],
            self.recv.at[0 if kind < 2 else 1, at, part], device,
        )

    def keep(self, part):
        rows = piece_of(part, self.rows)
        return pltpu.make_async_copy(self.own.at[rows], self.full.at[self.z, self.c, rows], self.local.at[part])

    def begin(self, part):
        self.keep(part).start()
        self.copy(self.z, 2, part, True).start()

    def finish(self):
        for part in range(PARTS):
            self.keep(part).wait()
            for at in range(self.nz):
                self.copy(at, 2, part).wait_send()
                self.copy(at, 2, part).wait_recv()


class Reduce:
    SEMS = [DMA((2, 4, PARTS)), DMA((2, 4, PARTS)), DMA((4,)), DMA((4,))]

    @staticmethod
    def buffers(nz, rows, width):
        return [VM((nz, rows, width), BF), VM((2, nz, rows, width), BF)]

    def __init__(self, part, held, came, send, recv, across_send, across_recv):
        self.part, self.held, self.came, self.send, self.recv = part, held, came, send, recv
        self.across_send, self.across_recv = across_send, across_recv
        self.x, self.c, self.z, self.y = place()
        self.nz, _, self.rows, self.width = part.shape

    def across(self, to):
        return remote(
            self.part.at[to, 1 - self.c], self.held.at[to], self.across_send.at[to], self.across_recv.at[to],
            {"core": 1 - self.c},
        )

    def along(self, to, way, part):
        device = ({"z": self.z + 1}, {"z": self.z - 1})[way]
        rows = piece_of(part, self.rows)
        return remote(
            self.held.at[to, rows], self.came.at[way, to, rows], self.send.at[way, to, part],
            self.recv.at[way, to, part], device,
        )

    def start(self):
        for to in [a for k in range(self.nz) for a in (self.nz - 1 - k, k)][: self.nz]:
            self.across(to).start()

    def add(self, to, ways, part, out=None):
        size = self.rows // PARTS

        def body(i, carry):
            at = pl.ds(pl.multiple_of(part * size + i * ROWS, ROWS), ROWS)
            total = self.part[to, self.c, at, :].astype(F32) + self.held[to, at, :].astype(F32)
            for way in ways:
                total = total + self.came[way, to, at, :].astype(F32)
            if out is None:
                self.held[to, at, :] = total.astype(BF)
            else:
                out(at, total)
            return carry

        lax.fori_loop(0, size // ROWS, body, 0)

    def last(self, part, out):
        if part == 0:
            self.across(self.z).wait_recv()
        for at in range(self.nz):

            @pl.when(self.z == at)
            def _(at=at):
                ways = ([0] if at > 0 else []) + ([1] if at < self.nz - 1 else [])
                for way in ways:
                    self.along(at, way, part).wait_recv()
                self.add(at, ways, part, out)

    def finish(self):
        for to in range(self.nz):
            self.across(to).wait_send()


def plan(nz, reduces, gathers):
    last = nz - 1
    rows = []
    for e in range(nz):
        sums = [("R", last - k) for k in range(last) if last - k > e]
        blocks = [("G", e - k) for k in range(e + 1)]
        if reduces and gathers:
            if e == last:
                rows.append([None] + blocks[1:-1] + [None] + blocks[-1:])
            else:
                woven = blocks[:-1] + sums[:1] + blocks[-1:] + sums[1:]
                rows.append(woven)
        elif reduces:
            rows.append([None] * e + sums)
        else:
            rows.append(blocks if e < last else [None] + blocks[1:])
    return rows


def flow(reduce, gather, before=None, work=()):
    work = list(work)
    any_one = reduce or gather
    nz, z = any_one.nz, any_one.z
    table = plan(nz, reduce is not None, gather is not None)
    pending = {(way, e): [] for way in (0, 1) for e in range(nz)}

    def pace(key, make):
        queue = pending[key]
        if len(queue) >= WINDOW:
            queue.pop(0)().wait_send()
        make().start()
        queue.append(make)

    def step(way, e, kind, place_at, part):
        block = place_at if way == 0 else nz - 1 - place_at
        if kind == "R":
            if part == 0:
                reduce.across(block).wait_recv()
            if e > 0:
                reduce.along(block, way, part).wait_recv()
            reduce.add(block, (way,) if e > 0 else (), part)
            pace((way, e), functools.partial(reduce.along, block, way, part))
        else:
            mine = place_at == e
            if not mine:
                gather.copy(block, way, part).wait_recv()
            if e < nz - 1:
                pace((way, e), functools.partial(gather.copy, block, way, part, mine))
            if not mine:
                gather.copy(block, 2, part).start()

    for t in range(max(len(row) for row in table)):
        for part in range(PARTS):
            if t == 0 and before is not None:
                before(part)
            if t == 0 and gather is not None:
                gather.begin(part)
            for way in (0, 1):
                for e in range(nz):
                    op = table[e][t] if t < len(table[e]) else None
                    if op is not None:
                        pl.when(z == (e if way == 0 else nz - 1 - e))(
                            functools.partial(step, way, e, op[0], op[1], part)
                        )
            if work:
                work.pop(0)()
    for item in work:
        item()

    def finish():
        for (way, e), queue in pending.items():
            if queue:

                @pl.when(z == (e if way == 0 else nz - 1 - e))
                def _(queue=queue):
                    for make in queue:
                        make().wait_send()

        for one in (reduce, gather):
            if one is not None:
                one.finish()

    return finish


class Spread:
    def __init__(self, source, target, send, recv, local, nx, ny):
        self.source, self.target, self.send, self.recv = source, target, send, recv
        self.nx, self.ny = nx, ny
        self.x, _, _, self.y = place()
        self.local = pltpu.make_async_copy(source(self.x, self.y), target(self.x, self.y), local)

    def copies(self):
        for i, step in enumerate(others(self.nx, self.ny)):
            px, py = data_peer(step, self.nx, self.ny)
            yield remote(
                self.source(px, py), self.target(self.x, self.y), self.send.at[i], self.recv.at[i],
                {"x": px, "y": py},
            )

    def start(self):
        for copy in self.copies():
            copy.start()
        self.local.start()

    def arrived(self):
        self.local.wait()
        for copy in self.copies():
            copy.wait_recv()

    def finish(self):
        for copy in self.copies():
            copy.wait_send()


class Swap:
    def __init__(self, blocks, slot, send, recv, local):
        self.blocks, self.slot, self.send, self.recv = blocks, slot, send, recv
        self.nz, self.nc = blocks.shape[:2]
        _, self.c, self.z, _ = place()
        self.local = pltpu.make_async_copy(blocks.at[self.z, self.c], slot(self.z, self.c), local)

    def copies(self):
        for i, step in enumerate(others(self.nz, self.nc)):
            pz, pc = team_peer(step, self.nz, self.nc)
            yield remote(
                self.blocks.at[pz, pc], self.slot(self.z, self.c), self.send.at[i], self.recv.at[i],
                {"z": pz, "core": pc},
            )

    def start(self):
        for copy in self.copies():
            copy.start()
        self.local.start()

    def arrived(self):
        self.local.wait()
        for copy in self.copies():
            copy.wait_recv()

    def finish(self):
        for copy in self.copies():
            copy.wait_send()


def call(kernel, operands, in_spaces, outs, out_spaces, scratch, number):
    return pl.pallas_call(
        kernel,
        out_shape=[jax.ShapeDtypeStruct(s, t) for s, t in outs],
        in_specs=[pl.BlockSpec(memory_space=s) for s in in_spaces],
        out_specs=[pl.BlockSpec(memory_space=s) for s in out_spaces],
        scratch_shapes=scratch,
        compiler_params=pltpu.CompilerParams(
            collective_id=number, has_side_effects=True, vmem_limit_bytes=56 << 20
        ),
    )(*operands)


def lanes(shape):
    return lax.broadcasted_iota(jnp.int32, shape, len(shape) - 1)


def by_rows(count, body):
    if count % ROWS or count == ROWS:
        body(slice(0, count))
    else:

        def step(i, carry):
            body(pl.ds(pl.multiple_of(i * ROWS, ROWS), ROWS))
            return carry

        lax.fori_loop(0, count // ROWS, step, 0)


def first_kernel(
    dims, tokens, table, gains, w_query, w_key, w_value, w_out, w_gate, w_up, down,
    n1g, tabg, w_attn, mlp_blocks, w_dn,
    n1, blocks, gs, gr, gl, ts, tr, tl, ss, sr, ds, dr, ws, wr, local,
):
    nx, nc, nz, ny = dims
    x, c, z, y = place()
    own = w_query.shape[0]
    qcols = HEADS // (nz * nc) * HEAD_DIM
    span = w_gate.shape[1] // (nx * nc * nz)
    dn = Spread(lambda px, py: down, lambda px, py: w_dn.at[px, py], ws, wr, local.at[1], nx, ny)
    greet(*dims)

    def pack(at):
        gain = gains[at, 0:1]
        for t in range(nz * nc):
            cols = slice(t * qcols, (t + 1) * qcols)
            blocks[t // nc, t % nc, at, :qcols] = (w_query[at, cols].astype(F32) * gain).astype(BF)
        for pair in range(KV_HEADS // 2):
            cols = slice(pair * 128, pair * 128 + 128)
            key, value = w_key[at, cols].astype(F32) * gain, w_value[at, cols].astype(F32) * gain
            first = lanes(key.shape) < 64
            both = (
                jnp.where(first, key, pltpu.roll(value, 64, 1)),
                jnp.where(first, pltpu.roll(key, 64, 1), value),
            )
            for k in range(2):
                for rep in range(nz * nc // KV_HEADS):
                    t = (pair * 2 + k) * (nz * nc // KV_HEADS) + rep
                    blocks[t // nc, t % nc, at, qcols : qcols + 128] = both[k].astype(BF)

    by_rows(own, pack)
    for t in range(nz * nc):
        turned = w_out[t * qcols : (t + 1) * qcols, :].astype(F32).T
        blocks[t // nc, t % nc, :, qcols + 128 :] = turned.astype(BF)
    swap = Swap(blocks, lambda pz, pc: w_attn.at[x, pc, pz, y], ss, sr, local.at[0])
    swap.start()
    dn.start()

    def norm(at):
        value = tokens[at, :].astype(F32)
        inverse = lax.rsqrt(jnp.mean(value * value, axis=-1, keepdims=True) + EPSILON)
        n1[at, :] = (value * inverse).astype(BF)

    by_rows(tokens.shape[0], norm)
    rows = Gather(n1, n1g, gs, gr, gl)
    tabs = Gather(table, tabg, ts, tr, tl)

    def spread_copies():
        for i, step in enumerate(others(nx, ny)):
            px, py = data_peer(step, nx, ny)
            slot = w_attn.at[x, :, :, y]
            yield remote(slot, slot, ds.at[i], dr.at[i], {"x": px, "y": py})

    def spread():
        swap.arrived()
        for copy in spread_copies():
            copy.start()

    def pack_mlp(at):
        gain = gains[at, 1:2]
        for k, weight in enumerate((w_gate, w_up)):
            for t in range(nz * nc):
                for i in range(nx):
                    chunk = (i * nc + t % nc) * nz + t // nc
                    to = (k * nx + i) * span
                    piece = weight[at, chunk * span : (chunk + 1) * span].astype(F32) * gain
                    mlp_blocks[t // nc, t % nc, at, to : to + span] = piece.astype(BF)

    end = flow(None, rows, None, [spread])
    by_rows(own, pack_mlp)
    end2 = flow(None, tabs)
    end()
    end2()
    swap.finish()
    for copy in spread_copies():
        copy.wait_recv()
    for copy in spread_copies():
        copy.wait_send()
    dn.arrived()
    dn.finish()


def first_call(dims, tokens, table, gains, w_query, w_key, w_value, w_out, w_gate, w_up, down):
    nx, nc, nz, ny = dims
    rows, width = tokens.shape
    own = w_query.shape[0]
    cols = 2 * HEADS // (nz * nc) * HEAD_DIM + 128
    peers = nx * ny - 1
    mlp_cols = 2 * w_gate.shape[1] // (nz * nc)
    return call(
        functools.partial(first_kernel, dims),
        (tokens, table, gains, w_query, w_key, w_value, w_out, w_gate, w_up, down),
        (VM,) * 9 + (pl.ANY,),
        [
            ((nz, nc, rows, width), BF),
            ((nz, nc) + table.shape, F32),
            ((nx, nc, nz, ny, own, cols), BF),
            ((nz, nc, own, mlp_cols), BF),
            ((nx, ny) + down.shape, BF),
        ],
        (pl.ANY, pl.ANY, pl.ANY, VM, pl.ANY),
        [VM((rows, width), BF), VM((nz, nc, own, cols), BF)]
        + Gather.SEMS * 2
        + [DMA((nz * nc - 1,))] * 2
        + [DMA((peers,))] * 4
        + [DMA((2,))],
        1,
    )


def middle_kernel(
    dims, part, tokens, cot, mlp_t,
    mid, n2g, cotg, w_mlp,
    held, came, n2, rs, rr, rxs, rxr, ns, nr, nl, cs, cr, cl, ms, mr, local,
):
    nx, nc, nz, ny = dims
    x, c, z, y = place()
    greet(*dims)
    reduce = Reduce(part, held, came, rs, rr, rxs, rxr)
    cots = Gather(cot, cotg, cs, cr, cl)
    rows = Gather(n2, n2g, ns, nr, nl)
    gu = Spread(lambda px, py: mlp_t, lambda px, py: w_mlp.at[px, :, :, py], ms, mr, local.at[0], nx, ny)
    reduce.start()
    gu.start()
    end = flow(reduce, cots)

    def settle(at, total):
        value = tokens[at, :].astype(F32) + total
        mid[at, :] = value
        inverse = lax.rsqrt(jnp.mean(value * value, axis=-1, keepdims=True) + EPSILON)
        n2[at, :] = (value * inverse).astype(BF)

    end2 = flow(None, rows, lambda part: reduce.last(part, settle))
    end2()
    end()
    gu.arrived()
    gu.finish()


def middle_call(dims, part, tokens, cot, mlp_t):
    nx, nc, nz, ny = dims
    rows, width = tokens.shape
    peers = nx * ny - 1
    return call(
        functools.partial(middle_kernel, dims),
        (part, tokens, cot, mlp_t),
        (VM, VM, VM, pl.ANY),
        [
            ((rows, width), F32),
            ((nz, nc, rows, width), BF),
            ((nz, nc, rows, width), BF),
            ((nx, nc, nz, ny) + mlp_t.shape[2:], BF),
        ],
        (VM, pl.ANY, pl.ANY, pl.ANY),
        Reduce.buffers(nz, rows, width)
        + [VM((rows, width), BF)]
        + Reduce.SEMS
        + Gather.SEMS * 2
        + [DMA((peers,))] * 2
        + [DMA((1,))],
        2,
    )


def back_kernel(
    dims, part, mlp_part, mid, cot, grad_mlp,
    dx2, dag, output, gain_part, came_mlp,
    held, came, held2, came2, low, rs, rr, rxs, rxr, os, orr, oxs, oxr, ds, dr, dl, ms, mr, local,
):
    nx, nc, nz, ny = dims
    x, c, z, y = place()
    greet(*dims)
    reduce = Reduce(part, held, came, rs, rr, rxs, rxr)
    reduce2 = Reduce(mlp_part, held2, came2, os, orr, oxs, oxr)
    rows = Gather(low, dag, ds, dr, dl)
    reduce.start()
    gu = Spread(
        lambda px, py: grad_mlp.at[px, :, :, py], lambda px, py: came_mlp.at[px, py], ms, mr, local.at[0], nx, ny
    )
    gu.start()
    end = flow(reduce, None)
    gain_part[...] = jnp.zeros_like(gain_part)

    def settle(at, total):
        value = mid[at, :]
        inverse = lax.rsqrt(jnp.mean(value * value, axis=-1, keepdims=True) + EPSILON)
        normed = value * inverse
        gain_part[...] += jnp.sum((total * normed).reshape(ROWS // 8, 8, -1), axis=0)
        gradient = cot[at, :].astype(F32) + inverse * (
            total - normed * jnp.mean(total * normed, axis=-1, keepdims=True)
        )
        dx2[at, :] = gradient
        low[at, :] = gradient.astype(BF)

    reduce2.start()
    end2 = flow(reduce2, rows, lambda part: reduce.last(part, settle))

    def finish(at, total):
        output[at, :] = (mid[at, :] + total).astype(BF)

    for part in range(PARTS):
        reduce2.last(part, finish)
    end2()
    end()
    gu.arrived()
    gu.finish()


def back_call(dims, part, mlp_part, mid, cot, grad_mlp):
    nx, nc, nz, ny = dims
    rows, width = mid.shape
    peers = nx * ny - 1
    return call(
        functools.partial(back_kernel, dims),
        (part, mlp_part, mid, cot, grad_mlp),
        (VM, VM, VM, VM, pl.ANY),
        [
            ((rows, width), F32),
            ((nz, nc, rows, width), BF),
            ((rows, width), BF),
            ((8, width), F32),
            ((nx, ny, nc, nz) + grad_mlp.shape[4:], BF),
        ],
        (VM, pl.ANY, VM, VM, pl.ANY),
        Reduce.buffers(nz, rows, width) * 2
        + [VM((rows, width), BF)]
        + Reduce.SEMS * 2
        + Gather.SEMS
        + [DMA((peers,))] * 2
        + [DMA((1,))],
        3,
    )


def last_kernel(
    dims, part, tokens, dx2, gains, mlp_g, came_dn, grad_attn,
    input_grad, gain_part, grad_query, grad_key, grad_value, grad_out, grad_gate, grad_up, grad_down,
    held, came, came_attn, sums, attn_g, rs, rr, rxs, rxr, ds, dr, ss, sr, local,
):
    nx, nc, nz, ny = dims
    x, c, z, y = place()
    own, cols = sums.shape[2:]
    qcols = (cols - 128) // 2
    span = mlp_g.shape[-1] // (2 * nx)
    reduce = Reduce(part, held, came, rs, rr, rxs, rxr)
    spread = Spread(
        lambda px, py: grad_attn.at[px, :, :, py], lambda px, py: came_attn.at[px, py], ds, dr, local.at[0], nx, ny
    )
    swap = Swap(sums, lambda pz, pc: attn_g.at[pz, pc], ss, sr, local.at[1])
    greet(*dims)
    reduce.start()
    spread.start()

    def unpack_mlp(at):
        gain = gains[at, 1:2]
        for k, grad in enumerate((grad_gate, grad_up)):
            for t in range(nz * nc):
                for i in range(nx):
                    chunk = (i * nc + t % nc) * nz + t // nc
                    source = (k * nx + i) * span
                    piece = mlp_g[t // nc, t % nc, at, source : source + span].astype(F32) * gain
                    grad[at, chunk * span : (chunk + 1) * span] = piece

    def down(at):
        total = came_dn[0, 0, at, :].astype(F32)
        for px, py in others(nx, ny):
            total = total + came_dn[px, py, at, :].astype(F32)
        grad_down[at, :] = total

    def add(at):
        for pz in range(nz):
            for pc in range(nc):
                total = came_attn[0, 0, pc, pz, at, :].astype(F32)
                for px, py in others(nx, ny):
                    total = total + came_attn[px, py, pc, pz, at, :].astype(F32)
                sums[pz, pc, at, :] = total.astype(BF)

    def exchange():
        spread.arrived()
        by_rows(own, add)
        swap.start()

    def nothing():
        return None

    work = [
        lambda: by_rows(own, unpack_mlp),
        nothing,
        lambda: by_rows(grad_down.shape[0], down),
        nothing,
        nothing,
        exchange,
    ]
    end = flow(reduce, None, None, work)
    gain_part[...] = jnp.zeros_like(gain_part)

    def settle(at, total):
        value = tokens[at, :].astype(F32)
        inverse = lax.rsqrt(jnp.mean(value * value, axis=-1, keepdims=True) + EPSILON)
        normed = value * inverse
        gain_part[...] += jnp.sum((total * normed).reshape(ROWS // 8, 8, -1), axis=0)
        input_grad[at, :] = dx2[at, :] + inverse * (
            total - normed * jnp.mean(total * normed, axis=-1, keepdims=True)
        )

    for half in range(PARTS):
        reduce.last(half, settle)
    end()
    spread.finish()
    swap.arrived()
    swap.finish()

    def unpack(at):
        gain = gains[at, 0:1]
        heads = []
        for t in range(nz * nc):
            block = attn_g[t // nc, t % nc, at, : qcols + 128].astype(F32) * gain
            grad_query[at, t * qcols : (t + 1) * qcols] = block[:, :qcols]
            if t % (nz * nc // KV_HEADS):
                heads[-1] = heads[-1] + block[:, qcols:]
            else:
                heads.append(block[:, qcols:])
        for pair in range(KV_HEADS // 2):
            one, two = heads[2 * pair], heads[2 * pair + 1]
            first = lanes(one.shape) < 64
            grad_key[at, pair * 128 : pair * 128 + 128] = jnp.where(first, one, pltpu.roll(two, 64, 1))
            grad_value[at, pair * 128 : pair * 128 + 128] = jnp.where(first, pltpu.roll(one, 64, 1), two)

    by_rows(own, unpack)
    for t in range(nz * nc):
        block = attn_g[t // nc, t % nc, :, qcols + 128 :].astype(F32)
        grad_out[t * qcols : (t + 1) * qcols, :] = block.T


def last_call(dims, part, tokens, dx2, gains, mlp_g, came_dn, grad_attn):
    nx, nc, nz, ny = dims
    rows, width = tokens.shape
    own, cols = grad_attn.shape[4:]
    qcols = (cols - 128) // 2
    heads = nz * nc * qcols
    ff = mlp_g.shape[-1] // 2 * nz * nc
    peers = nx * ny - 1
    return call(
        functools.partial(last_kernel, dims),
        (part, tokens, dx2, gains, mlp_g, came_dn, grad_attn),
        (VM,) * 6 + (pl.ANY,),
        [
            ((rows, width), F32),
            ((8, width), F32),
            ((own, heads), F32),
            ((own, KV_HEADS * HEAD_DIM), F32),
            ((own, KV_HEADS * HEAD_DIM), F32),
            ((heads, own), F32),
            ((own, ff), F32),
            ((own, ff), F32),
            (came_dn.shape[2:], F32),
        ],
        (VM,) * 9,
        Reduce.buffers(nz, rows, width)
        + [VM((nx, ny, nc, nz, own, cols), BF), VM((nz, nc, own, cols), BF), VM((nz, nc, own, cols), BF)]
        + Reduce.SEMS
        + [DMA((peers,))] * 2
        + [DMA((nz * nc - 1,))] * 2
        + [DMA((2,))],
        4,
    )


def nt(a, b):
    return lax.dot_general(a, b, (((1,), (1,)), ((), ())), preferred_element_type=F32)


def nn(a, b):
    return jnp.dot(a, b, preferred_element_type=F32)


def rope_lanes(tab):
    at = lanes(tab.shape)
    cos = jnp.where(at < 32, tab, 0.0)
    sin = jnp.where((at >= 32) & (at < 64), tab, 0.0)
    cos = cos + pltpu.roll(cos, 32, 1)
    cos = cos + pltpu.roll(cos, 64, 1)
    sin = sin - pltpu.roll(sin, 96, 1)
    sin = sin + pltpu.roll(sin, 64, 1)
    return cos, sin


def swap_halves(u):
    return jnp.where(lax.rem(lanes(u.shape), 64) < 32, pltpu.roll(u, 96, 1), pltpu.roll(u, 32, 1))


def two_heads(u):
    first = lanes(u.shape) < 64
    zero = jnp.zeros_like(u)
    return jnp.concatenate([jnp.where(first, u, zero), jnp.where(first, zero, u)], axis=0)


def join_heads(t):
    rows = t.shape[1] // 2
    return jnp.concatenate([t[:64, :rows], t[64:, rows:]], axis=0).T


def bias_of(tab, keys, first_row):
    rows = tab.shape[0]
    starts = tab.T[64:65, :].astype(jnp.int32)
    key = lax.broadcasted_iota(jnp.int32, (keys, rows), 0)
    row = first_row + lax.broadcasted_iota(jnp.int32, (keys, rows), 1)
    bias = jnp.where((key >= starts) & (key <= row), 0.0, MASKED)
    return jnp.concatenate([bias, bias], axis=1)


def attend_kernel(
    dims, n1g, w, tab, mlp_blocks,
    q, kk, vv, stat, ob, part, mlp_t,
    kv, vt, ss, sr, ys, yr, local,
):
    nx, nc, nz, ny = dims
    x, c, z, y = place()
    rows, width = n1g.shape[2:]
    qcols = q.shape[-1]
    pairs = qcols // 128
    greet(*dims)
    swap = Swap(mlp_blocks, lambda pz, pc: mlp_t.at[pc, pz], ss, sr, local.at[0])
    swap.start()

    def project(i, carry):
        res = nn(n1g[i].reshape(nc * rows, width), w[:, : qcols + 128])
        cos, sin = rope_lanes(tab[i].reshape(nc * rows, 128))
        for p in range(pairs):
            u = res[:, p * 128 : p * 128 + 128]
            u = (u * cos + swap_halves(u) * sin) * (HEAD_DIM ** (-0.5))
            q[i, :, :, p * 128 : p * 128 + 128] = u.astype(BF).reshape(nc, rows, 128)
        u = res[:, qcols : qcols + 128]
        u = jnp.where(lanes(u.shape) < 64, u * cos + swap_halves(u) * sin, u).astype(BF)
        for pc in range(nc):
            kv[pc, i, y] = u[pc * rows : (pc + 1) * rows]
        return carry

    lax.fori_loop(0, nz, project, 0)
    sends = []
    for i in range(ny - 1):
        slot = kv.at[:, :, y]
        sends.append(remote(slot, slot, ys.at[i], yr.at[i], {"y": lax.rem(y + 1 + i, ny)}))
    for copy in sends:
        copy.start()
    for copy in sends:
        copy.wait_recv()

    span = ny * rows

    def double(i, carry):
        pc, pz = i // nz, lax.rem(i, nz)
        u = kv[pc, pz].reshape(span, 128).astype(F32)
        r = pltpu.roll(u, 64, 1)
        first = lanes(u.shape) < 64
        at = pl.ds(pl.multiple_of(pz * span, span), span)
        kk[pc, at, :] = jnp.where(first, u, r).astype(BF)
        values = jnp.where(first, r, u)
        vv[pc, at, :] = values.astype(BF)
        vt[pc, :, at] = values.T.astype(BF)
        return carry

    lax.fori_loop(0, nc * nz, double, 0)

    def attend(pc, carry):
        for pz in range(nz):
            keys = (pz + 1) * span
            bias = bias_of(tab[pz, pc], keys, (pz * ny + y) * rows)
            for p in range(pairs):
                q2 = two_heads(q[pz, pc, :, p * 128 : p * 128 + 128])
                s = nt(kk[pc, :keys, :], q2) + bias
                top = jnp.max(s, axis=0, keepdims=True)
                e = jnp.exp(s - top)
                total = jnp.sum(e, axis=0, keepdims=True)
                stat[pz, pc, p : p + 1, :] = top + jnp.log(total)
                weights = (e * (1.0 / total)).astype(BF)
                o = join_heads(nn(vt[pc, :, :keys], weights))
                ob[pz, pc, :, p * 128 : p * 128 + 128] = o.astype(BF)
        return carry

    lax.fori_loop(0, nc, attend, 0)

    def output(i, carry):
        pz, n = i // 4, lax.rem(i, 4)
        at = pl.ds(pl.multiple_of(n * (width // 4), width // 4), width // 4)
        res = nt(ob[pz].reshape(nc * rows, qcols), w[at, qcols + 128 : 2 * qcols + 128])
        part[pz, :, :, at] = res.astype(BF).reshape(nc, rows, width // 4)
        return carry

    lax.fori_loop(0, nz * 4, output, 0)
    for copy in sends:
        copy.wait_send()
    swap.arrived()
    swap.finish()


def attend_call(dims, n1g, w, tab, mlp_blocks):
    nx, nc, nz, ny = dims
    rows, width = n1g.shape[2:]
    qcols = (w.shape[1] - 128) // 2
    keys = nz * ny * rows
    members = nz * nc - 1
    own, cols = mlp_blocks.shape[2:]
    return call(
        functools.partial(attend_kernel, dims),
        (n1g, w, tab, mlp_blocks),
        (VM, VM, VM, pl.ANY),
        [
            ((nz, nc, rows, qcols), BF),
            ((nc, keys, 128), BF),
            ((nc, keys, 128), BF),
            ((nz, nc, 8, 2 * rows), F32),
            ((nz, nc, rows, qcols), BF),
            ((nz, nc, rows, width), BF),
            ((nc, nz, own, cols), BF),
        ],
        (VM, VM, VM, VM, VM, VM, pl.ANY),
        [VM((nc, nz, ny, rows, 128), BF), VM((nc, 128, keys), BF)]
        + [DMA((members,))] * 2
        + [DMA((max(ny - 1, 1),))] * 2
        + [DMA((1,))],
        5,
    )


def attend_back_kernel(
    dims, dag, w, tab, q, kk, vv, stat, mlp_sum, grad_dn,
    dqkv, part, mlp_g, came_dn,
    do, kt, dk, dv, out, came, ss, sr, ys, yr, ws, wr, local,
):
    nx, nc, nz, ny = dims
    x, c, z, y = place()
    rows, width = dag.shape[2:]
    qcols = q.shape[-1]
    pairs = qcols // 128
    span = ny * rows
    greet(*dims, cross=True)
    swap = Swap(mlp_sum, lambda pz, pc: mlp_g.at[pz, pc], ss, sr, local.at[0])
    swap.start()
    dn = Spread(lambda px, py: grad_dn.at[px, py], lambda px, py: came_dn.at[px, py], ws, wr, local.at[1], nx, ny)
    dn.start()

    def project(i, carry):
        res = nn(dag[i].reshape(nc * rows, width), w[:, qcols + 128 : 2 * qcols + 128])
        do[i] = res.astype(BF).reshape(nc, rows, qcols)
        return carry

    lax.fori_loop(0, nz, project, 0)

    def turned(i, carry):
        pc, pz = i // nz, lax.rem(i, nz)
        at = pl.ds(pl.multiple_of(pz * span, span), span)
        kt[pc, :, at] = kk[pc, at, :].astype(F32).T.astype(BF)
        return carry

    lax.fori_loop(0, nc * nz, turned, 0)

    def attend(pc, carry):
        for pz in reversed(range(nz)):
            keys = (pz + 1) * span
            bias = bias_of(tab[pz, pc], keys, (pz * ny + y) * rows)
            cos, sin = rope_lanes(tab[pz, pc])
            for p in range(pairs):
                q2 = two_heads(q[pz, pc, :, p * 128 : p * 128 + 128])
                do2 = two_heads(do[pz, pc, :, p * 128 : p * 128 + 128])
                s = nt(kk[pc, :keys, :], q2) + bias
                weights = jnp.exp(s - stat[pz, pc, p : p + 1, :])
                dw = nt(vv[pc, :keys, :], do2)
                dw = weights * dw
                delta = jnp.sum(dw, axis=0, keepdims=True)
                ds = (dw - weights * delta).astype(BF)
                dv_new = nn(weights.astype(BF), do2)
                dk_new = nn(ds, q2)
                if pz == nz - 1 and p == 0:
                    dv[pc, :keys, :] = dv_new
                    dk[pc, :keys, :] = dk_new
                else:
                    dv[pc, :keys, :] += dv_new
                    dk[pc, :keys, :] += dk_new
                u = join_heads(nn(kt[pc, :, :keys], ds)) * (HEAD_DIM ** (-0.5))
                u = u * cos - swap_halves(u) * sin
                dqkv[pz, pc, :, p * 128 : p * 128 + 128] = u.astype(BF)
        return carry

    lax.fori_loop(0, nc, attend, 0)

    def fold(i, carry):
        pc, pz = i // nz, lax.rem(i, nz)
        at = pl.ds(pl.multiple_of(pz * span, span), span)
        key, value = dk[pc, at, :], dv[pc, at, :]
        first = lanes(key.shape) < 64
        both = jnp.where(first, key + pltpu.roll(key, 64, 1), value + pltpu.roll(value, 64, 1))
        both = both.astype(BF)
        for py in range(ny):
            out[pc, py, pz] = both[py * rows : (py + 1) * rows]
        return carry

    lax.fori_loop(0, nc * nz, fold, 0)
    sends = []
    for i, (sy, sc) in enumerate(others(ny, nc)):
        py, pc = lax.rem(y + sy, ny), lax.rem(c + sc, nc)
        sends.append(remote(out.at[pc, py], came.at[i], ys.at[i], yr.at[i], {"y": py, "core": pc}))
    for copy in sends:
        copy.start()
    for copy in sends:
        copy.wait_recv()

    def settle(pz, carry):
        total = out[c, y, pz].astype(F32)
        for i in range(len(sends)):
            total = total + came[i, pz].astype(F32)
        cos, sin = rope_lanes(tab[pz, c])
        first = lanes(total.shape) < 64
        total = jnp.where(first, total * cos - swap_halves(total) * sin, total)
        dqkv[pz, c, :, qcols : qcols + 128] = total.astype(BF)
        dqkv[pz, 1 - c, :, qcols : qcols + 128] = jnp.zeros((rows, 128), BF)
        return carry

    lax.fori_loop(0, nz, settle, 0)

    def output(i, carry):
        pz, n = i // 4, lax.rem(i, 4)
        at = pl.ds(pl.multiple_of(n * (width // 4), width // 4), width // 4)
        res = nt(dqkv[pz].reshape(nc * rows, qcols + 128), w[at, : qcols + 128])
        part[pz, :, :, at] = res.astype(BF).reshape(nc, rows, width // 4)
        return carry

    lax.fori_loop(0, nz * 4, output, 0)
    for copy in sends:
        copy.wait_send()
    swap.arrived()
    swap.finish()
    dn.arrived()
    dn.finish()


def attend_back_call(dims, dag, w, tab, q, kk, vv, stat, mlp_sum, grad_dn):
    nx, nc, nz, ny = dims
    rows, width = dag.shape[2:]
    qcols = q.shape[-1]
    keys = nz * ny * rows
    members = nz * nc - 1
    near = ny * nc - 1
    own, cols = mlp_sum.shape[2:]
    return call(
        functools.partial(attend_back_kernel, dims),
        (dag, w, tab, q, kk, vv, stat, mlp_sum, grad_dn),
        (VM, VM, VM, VM, VM, VM, VM, pl.ANY, pl.ANY),
        [
            ((nz, nc, rows, qcols + 128), BF),
            ((nz, nc, rows, width), BF),
            ((nz, nc, own, cols), BF),
            (grad_dn.shape, BF),
        ],
        (VM, VM, pl.ANY, pl.ANY),
        [
            VM((nz, nc, rows, qcols), BF),
            VM((nc, 128, keys), BF),
            VM((nc, keys, 128), F32),
            VM((nc, keys, 128), F32),
            VM((nc, ny, nz, rows, 128), BF),
            VM((near, nz, rows, 128), BF),
        ]
        + [DMA((members,))] * 2
        + [DMA((near,))] * 2
        + [DMA((nx * ny - 1,))] * 2
        + [DMA((2,))],
        6,
    )


def shards(
    tokens, positions, doc_start, cotangent, w_query, w_key, w_value, w_out,
    attn_gain, w_gate, w_up, w_down, mlp_gain,
):
    dims = tuple(lax.axis_size(a) for a in ALL)
    nx, nc, nz, ny = dims
    team = nz * nc
    rows, width = tokens.shape
    own = w_query.shape[0]
    heads = HEADS // team
    qcols = heads * HEAD_DIM
    piece = w_down.shape[0]
    ffcols = piece * nx * ny

    gains = jnp.stack([attn_gain, mlp_gain], axis=1).astype(F32)
    half = HEAD_DIM // 2
    frequency = 10000.0 ** (-2.0 * jnp.arange(half, dtype=F32) / HEAD_DIM)
    angles = positions.astype(F32)[:, None] * frequency[None, :]
    table = jnp.concatenate(
        [
            jnp.cos(angles),
            jnp.sin(angles),
            jnp.broadcast_to(doc_start.astype(F32)[:, None], (rows, HEAD_DIM)),
        ],
        axis=-1,
    )
    n1g, tab, w_attn, mlp_blocks, w_dn = first_call(
        dims, tokens, table, gains, w_query, w_key, w_value, w_out, w_gate, w_up, w_down
    )
    w_attn = w_attn.reshape(width, w_attn.shape[-1])
    total = team * rows
    q, kk, vv, stat, ob, part, mlp_t = attend_call(dims, n1g, w_attn, tab, mlp_blocks)
    mid_f, n2g, cotg, w_mlp = middle_call(dims, part, tokens, cotangent, mlp_t)
    n2g = n2g.reshape(total, width)
    cotg = cotg.reshape(total, width)
    w_mlp = w_mlp.reshape(width, 2 * ffcols)
    w_dn = w_dn.reshape(ffcols, width)
    gt = dot_plain(n2g, w_mlp[:, :ffcols])
    up = dot_plain(n2g, w_mlp[:, ffcols:])
    sg = jax.nn.sigmoid(gt)
    hid = (gt * sg * up).astype(BF)
    mlp_out = dot_plain(hid, w_dn).astype(BF).reshape(nz, nc, rows, width)

    dhid = dot_right_t(cotg, w_dn)
    down_part = dot_left_t(hid, cotg).astype(BF)
    dgt = (dhid * up * sg * (1.0 + gt * (1.0 - sg))).astype(BF)
    dup = (dhid * gt * sg).astype(BF)
    dmlp = jnp.concatenate([dgt, dup], axis=-1)
    dn2 = dot_right_t(dmlp, w_mlp).astype(BF).reshape(nz, nc, rows, width)
    mlp_part = dot_left_t(n2g, dmlp).astype(BF).reshape(nx, nc, nz, ny, own, 2 * ffcols)
    dx2, dag, output, gain_m_part, mlp_came = back_call(dims, dn2, mlp_out, mid_f, cotangent, mlp_part)
    gain_m_part = gain_m_part.sum(0)
    mlp_sum = jnp.sum(mlp_came.astype(F32), axis=(0, 1)).astype(BF).transpose(1, 0, 2, 3)
    dqkv, dn1, mlp_g, down_came = attend_back_call(
        dims, dag, w_attn, tab, q, kk, vv, stat, mlp_sum, down_part.reshape(nx, ny, piece, width)
    )
    out_part = dot_left_t(dag.reshape(total, width), ob.reshape(total, qcols))
    qkv_part = dot_left_t(n1g.reshape(total, width), dqkv.reshape(total, qcols + 128))
    attn_part = jnp.concatenate([qkv_part, out_part], axis=-1).astype(BF)
    attn_part = attn_part.reshape(nx, nc, nz, ny, own, attn_part.shape[-1])
    (
        input_grad, gain_a_part, grad_query, grad_key, grad_value, grad_out, grad_gate, grad_up, grad_down
    ) = last_call(dims, dn1, tokens, dx2, gains, mlp_g, down_came, attn_part)
    parts = jnp.stack([gain_a_part.sum(0), gain_m_part], 0).reshape(2, nx * team * ny, own)
    parts = lax.all_to_all(parts.transpose(1, 0, 2), ALL, 0, 0, tiled=False).sum(0)
    grad_attn_gain = parts[0] / gains[:, 0]
    grad_mlp_gain = parts[1] / gains[:, 1]
    return (
        output, input_grad, grad_query, grad_key, grad_value, grad_out,
        grad_attn_gain, grad_gate, grad_up, grad_down, grad_mlp_gain,
    )


def solution(mesh):
    fsdp, seq = mesh.shape["fsdp"], mesh.shape["seq"]
    nc, nz = 2, 4
    grid = Mesh(mesh.devices.reshape(fsdp // nc, nc, nz, seq // nz), ALL)
    row, col, vec = P(ALL, None), P(None, ALL), P(ALL)
    in_specs = (row, vec, vec, row, row, row, row, col, vec, row, row, row, vec)
    out_specs = (row, row, row, row, row, col, vec, row, row, row, vec)
    return jax.shard_map(shards, mesh=grid, in_specs=in_specs, out_specs=out_specs, check_vma=False)
```

```python
import functools

import jax
import jax.numpy as jnp
from jax import lax
from jax.experimental import pallas as pl
from jax.experimental.pallas import tpu as pltpu
from jax.sharding import Mesh
from jax.sharding import PartitionSpec as P

HEADS = 32
KV_HEADS = 4
HEAD_DIM = 64
EPSILON = 1e-05
MASKED = -1e30
ALL = ("x", "core", "z", "y")
TEAM = ("z", "core")
DATA = ("x", "y")
BF = jnp.bfloat16
F32 = jnp.float32


MESH = pl.DeviceIdType.MESH
VM = pltpu.VMEM
DMA = pltpu.SemaphoreType.DMA
ROWS = 16
PARTS = 2
WINDOW = 2
KEYS = 1024


def place():
    return tuple(lax.axis_index(a) for a in ALL)


def others(nx, ny):
    return [(i, j) for i in range(nx) for j in range(ny) if (i, j) != (0, 0)]


def data_peer(step, nx, ny):
    x, _, _, y = place()
    return lax.rem(x + step[0], nx), lax.rem(y + step[1], ny)


def team_peer(step, nz, nc):
    _, c, z, _ = place()
    return lax.rem(z + step[0], nz), lax.rem(c + step[1], nc)


def greet(nx, nc, nz, ny, cross=False):
    barrier = pltpu.get_barrier_semaphore()
    x, c, z, y = place()
    extra = ny - 1 if cross else 0
    for i in range(extra):
        device = {"y": lax.rem(y + 1 + i, ny), "core": 1 - c}
        pl.semaphore_signal(barrier, inc=1, device_id=device, device_id_type=MESH)
    for step in others(nx, ny):
        px, py = data_peer(step, nx, ny)
        pl.semaphore_signal(barrier, inc=1, device_id={"x": px, "y": py}, device_id_type=MESH)
    for step in others(nz, nc):
        pz, pc = team_peer(step, nz, nc)
        pl.semaphore_signal(barrier, inc=1, device_id={"z": pz, "core": pc}, device_id_type=MESH)
    pl.semaphore_wait(barrier, nx * ny - 1 + nz * nc - 1 + extra)


def remote(source, target, send, recv, device):
    return pltpu.make_async_remote_copy(
        src_ref=source, dst_ref=target, send_sem=send, recv_sem=recv,
        device_id=device, device_id_type=MESH,
    )


def piece_of(part, rows):
    return pl.ds(part * (rows // PARTS), rows // PARTS)


class Gather:
    SEMS = [DMA((3, 4, PARTS)), DMA((2, 4, PARTS)), DMA((PARTS,))]

    def __init__(self, own, full, send, recv, local):
        self.own, self.full, self.send, self.recv, self.local = own, full, send, recv, local
        self.x, self.c, self.z, self.y = place()
        self.nz, _, self.rows = full.shape[:3]

    def copy(self, at, kind, part, mine=False):
        rows = piece_of(part, self.rows)
        slot = self.full.at[at, self.c, rows]
        device = ({"z": self.z + 1}, {"z": self.z - 1}, {"core": 1 - self.c})[kind]
        return remote(
            self.own.at[rows] if mine else slot, slot, self.send.at[kind, at, part],
            self.recv.at[0 if kind < 2 else 1, at, part], device,
        )

    def keep(self, part):
        rows = piece_of(part, self.rows)
        return pltpu.make_async_copy(self.own.at[rows], self.full.at[self.z, self.c, rows], self.local.at[part])

    def begin(self, part):
        self.keep(part).start()
        self.copy(self.z, 2, part, True).start()

    def finish(self):
        for part in range(PARTS):
            self.keep(part).wait()
            for at in range(self.nz):
                self.copy(at, 2, part).wait_send()
                self.copy(at, 2, part).wait_recv()


class Reduce:
    SEMS = [DMA((2, 4, PARTS)), DMA((2, 4, PARTS)), DMA((4,)), DMA((4,))]

    @staticmethod
    def buffers(nz, rows, width):
        return [VM((nz, rows, width), BF), VM((2, nz - 1, rows, width), BF)]

    def __init__(self, part, held, came, send, recv, across_send, across_recv):
        self.part, self.held, self.came, self.send, self.recv = part, held, came, send, recv
        self.across_send, self.across_recv = across_send, across_recv
        self.x, self.c, self.z, self.y = place()
        self.nz, _, self.rows, self.width = part.shape

    def across(self, to):
        return remote(
            self.part.at[to, 1 - self.c], self.held.at[to], self.across_send.at[to], self.across_recv.at[to],
            {"core": 1 - self.c},
        )

    def along(self, to, way, part):
        device = ({"z": self.z + 1}, {"z": self.z - 1})[way]
        rows = piece_of(part, self.rows)
        return remote(
            self.held.at[to, rows], self.came.at[way, to - 1 + way, rows], self.send.at[way, to, part],
            self.recv.at[way, to, part], device,
        )

    def start(self):
        for to in [a for k in range(self.nz) for a in (self.nz - 1 - k, k)][: self.nz]:
            self.across(to).start()

    def add(self, to, ways, part, out=None):
        size = self.rows // PARTS

        def body(i, carry):
            at = pl.ds(pl.multiple_of(part * size + i * ROWS, ROWS), ROWS)
            total = self.part[to, self.c, at, :].astype(F32) + self.held[to, at, :].astype(F32)
            for way in ways:
                total = total + self.came[way, to - 1 + way, at, :].astype(F32)
            if out is None:
                self.held[to, at, :] = total.astype(BF)
            else:
                out(at, total)
            return carry

        lax.fori_loop(0, size // ROWS, body, 0)

    def last(self, part, out):
        if part == 0:
            self.across(self.z).wait_recv()
        for at in range(self.nz):

            @pl.when(self.z == at)
            def _(at=at):
                ways = ([0] if at > 0 else []) + ([1] if at < self.nz - 1 else [])
                for way in ways:
                    self.along(at, way, part).wait_recv()
                self.add(at, ways, part, out)

    def finish(self):
        for to in range(self.nz):
            self.across(to).wait_send()


def plan(nz, reduces, gathers):
    last = nz - 1
    rows = []
    for e in range(nz):
        sums = [("R", last - k) for k in range(last) if last - k > e]
        blocks = [("G", e - k) for k in range(e + 1)]
        if reduces and gathers:
            if e == last:
                rows.append([None] + blocks[1:-1] + [None] + blocks[-1:])
            else:
                woven = blocks[:-1] + sums[:1] + blocks[-1:] + sums[1:]
                rows.append(woven)
        elif reduces:
            rows.append([None] * e + sums)
        else:
            rows.append(blocks if e < last else [None] + blocks[1:])
    return rows


def flow(reduce, gather, before=None, work=()):
    work = list(work)
    any_one = reduce or gather
    nz, z = any_one.nz, any_one.z
    table = plan(nz, reduce is not None, gather is not None)
    pending = {(way, e): [] for way in (0, 1) for e in range(nz)}

    def pace(key, make):
        queue = pending[key]
        if len(queue) >= WINDOW:
            queue.pop(0)().wait_send()
        make().start()
        queue.append(make)

    def step(way, e, kind, place_at, part):
        block = place_at if way == 0 else nz - 1 - place_at
        if kind == "R":
            if part == 0:
                reduce.across(block).wait_recv()
            if e > 0:
                reduce.along(block, way, part).wait_recv()
            reduce.add(block, (way,) if e > 0 else (), part)
            pace((way, e), functools.partial(reduce.along, block, way, part))
        else:
            mine = place_at == e
            if not mine:
                gather.copy(block, way, part).wait_recv()
            if e < nz - 1:
                pace((way, e), functools.partial(gather.copy, block, way, part, mine))
            if not mine:
                gather.copy(block, 2, part).start()

    for t in range(max(len(row) for row in table)):
        for part in range(PARTS):
            if t == 0 and before is not None:
                before(part)
            if t == 0 and gather is not None:
                gather.begin(part)
            for way in (0, 1):
                for e in range(nz):
                    op = table[e][t] if t < len(table[e]) else None
                    if op is not None:
                        pl.when(z == (e if way == 0 else nz - 1 - e))(
                            functools.partial(step, way, e, op[0], op[1], part)
                        )
            if work:
                work.pop(0)()
    for item in work:
        item()

    def finish():
        for (way, e), queue in pending.items():
            if queue:

                @pl.when(z == (e if way == 0 else nz - 1 - e))
                def _(queue=queue):
                    for make in queue:
                        make().wait_send()

        for one in (reduce, gather):
            if one is not None:
                one.finish()

    return finish


class Spread:
    def __init__(self, source, target, send, recv, local, nx, ny):
        self.source, self.target, self.send, self.recv = source, target, send, recv
        self.nx, self.ny = nx, ny
        self.x, _, _, self.y = place()
        self.own = lambda: pltpu.make_async_copy(source(self.x, self.y), target(self.x, self.y), local)

    def copies(self):
        for i, step in enumerate(others(self.nx, self.ny)):
            px, py = data_peer(step, self.nx, self.ny)
            yield remote(
                self.source(px, py), self.target(self.x, self.y), self.send.at[i], self.recv.at[i],
                {"x": px, "y": py},
            )

    def start(self):
        for copy in self.copies():
            copy.start()
        self.own().start()

    def start_along(self, far):
        for step, copy in zip(others(self.nx, self.ny), self.copies()):
            if step[0] == far:
                copy.start()
        if far == 0:
            self.own().start()

    def arrived(self):
        self.own().wait()
        for copy in self.copies():
            copy.wait_recv()

    def finish(self):
        for copy in self.copies():
            copy.wait_send()


class Swap:
    def __init__(self, source, slot, send, recv, local, nz, nc):
        self.source, self.slot, self.send, self.recv, self.nz, self.nc = source, slot, send, recv, nz, nc
        _, self.c, self.z, _ = place()
        self.own = lambda: pltpu.make_async_copy(source(self.z, self.c), slot(self.z, self.c), local)

    def copies(self):
        for i, step in enumerate(others(self.nz, self.nc)):
            pz, pc = team_peer(step, self.nz, self.nc)
            yield remote(
                self.source(pz, pc), self.slot(self.z, self.c), self.send.at[i], self.recv.at[i],
                {"z": pz, "core": pc},
            )

    def start(self):
        for copy in self.copies():
            copy.start()
        self.own().start()

    def arrived(self):
        self.own().wait()
        for copy in self.copies():
            copy.wait_recv()

    def finish(self):
        for copy in self.copies():
            copy.wait_send()


def call(kernel, operands, in_spaces, outs, out_spaces, scratch, number):
    return pl.pallas_call(
        kernel,
        out_shape=[jax.ShapeDtypeStruct(s, t) for s, t in outs],
        in_specs=[pl.BlockSpec(memory_space=s) for s in in_spaces],
        out_specs=[pl.BlockSpec(memory_space=s) for s in out_spaces],
        scratch_shapes=scratch,
        compiler_params=pltpu.CompilerParams(
            collective_id=number, has_side_effects=True, vmem_limit_bytes=60 << 20
        ),
    )(*operands)


def lanes(shape):
    return lax.broadcasted_iota(jnp.int32, shape, len(shape) - 1)


def by_rows(count, body):
    if count % ROWS or count == ROWS:
        body(slice(0, count))
    else:

        def step(i, carry):
            body(pl.ds(pl.multiple_of(i * ROWS, ROWS), ROWS))
            return carry

        lax.fori_loop(0, count // ROWS, step, 0)


def nt(a, b):
    return lax.dot_general(a, b, (((1,), (1,)), ((), ())), preferred_element_type=F32)


def nn(a, b):
    return jnp.dot(a, b, preferred_element_type=F32)


def tn(a, b):
    return lax.dot_general(a, b, (((0,), (0,)), ((), ())), preferred_element_type=F32)


def rope_lanes(tab):
    at = lanes(tab.shape)
    cos = jnp.where(at < 32, tab, 0.0)
    sin = jnp.where((at >= 32) & (at < 64), tab, 0.0)
    cos = cos + pltpu.roll(cos, 32, 1)
    cos = cos + pltpu.roll(cos, 64, 1)
    sin = sin - pltpu.roll(sin, 96, 1)
    sin = sin + pltpu.roll(sin, 64, 1)
    return cos, sin


def swap_halves(u):
    return jnp.where(lax.rem(lanes(u.shape), 64) < 32, pltpu.roll(u, 96, 1), pltpu.roll(u, 32, 1))


def two_heads(u):
    first = lanes(u.shape) < 64
    zero = jnp.zeros_like(u)
    return jnp.concatenate([jnp.where(first, u, zero), jnp.where(first, zero, u)], axis=0)


def join_heads(t):
    rows = t.shape[1] // 2
    return jnp.concatenate([t[:64, :rows], t[64:, rows:]], axis=0).T


def bias_of(tab, keys, first_row, first_key=0):
    rows = tab.shape[0]
    starts = tab.T[64:65, :].astype(jnp.int32)
    key = first_key + lax.broadcasted_iota(jnp.int32, (keys, rows), 0)
    row = first_row + lax.broadcasted_iota(jnp.int32, (keys, rows), 1)
    bias = jnp.where((key >= starts) & (key <= row), 0.0, MASKED)
    return jnp.concatenate([bias, bias], axis=1)


def forward_kernel(
    dims, tokens, table, gains, w_query, w_key, w_value, w_out_t, w_gate, w_up, down, cot,
    n1g, w_attn, tab, q, kk, vv, stat, ob, mid, n2g, cotg, w_mlp, w_dn,
    n1, blocks, mlp_blocks, mlp_t, kv, vt, part, held, came, n2,
    gs, gr, gl, ts, tr, ss, sr, ds, dr, ws, wr, us, ur, ys, yr, rs, rr, rxs, rxr, cs, cr, cl, ns, nr, nl, ms, mr, local,
):
    nx, nc, nz, ny = dims
    x, c, z, y = place()
    rows, width = tokens.shape
    own = w_query.shape[0]
    qcols = q.shape[-1]
    pairs = qcols // 128
    span = w_gate.shape[1] // (nx * nc * nz)
    keys_span = ny * rows
    dn = Spread(lambda px, py: down, lambda px, py: w_dn.at[px, py], ws, wr, local.at[0], nx, ny)
    swap = Swap(
        lambda pz, pc: blocks.at[pz, pc], lambda pz, pc: w_attn.at[x, pc, pz, y], ss, sr, local.at[1], nz, nc
    )
    tabs = Swap(lambda pz, pc: table, lambda pz, pc: tab.at[pz, pc], ts, tr, local.at[2], nz, nc)
    mlp_swap = Swap(
        lambda pz, pc: mlp_blocks.at[pz, pc], lambda pz, pc: mlp_t.at[pc, pz], us, ur, local.at[3], nz, nc
    )
    gu = Spread(lambda px, py: mlp_t, lambda px, py: w_mlp.at[px, :, :, py], ms, mr, local.at[4], nx, ny)
    first_rows = Gather(n1, n1g, gs, gr, gl)
    reduce = Reduce(part, held, came, rs, rr, rxs, rxr)
    cots = Gather(cot, cotg, cs, cr, cl)
    next_rows = Gather(n2, n2g, ns, nr, nl)
    greet(*dims)

    def pack(at):
        gain = gains[at, 0:1]
        for t in range(nz * nc):
            cols = slice(t * qcols, (t + 1) * qcols)
            blocks[t // nc, t % nc, at, :qcols] = (w_query[at, cols].astype(F32) * gain).astype(BF)
            blocks[t // nc, t % nc, at, qcols + 128 :] = w_out_t[at, cols]
        for pair in range(KV_HEADS // 2):
            cols = slice(pair * 128, pair * 128 + 128)
            key, value = w_key[at, cols].astype(F32) * gain, w_value[at, cols].astype(F32) * gain
            first = lanes(key.shape) < 64
            both = (
                jnp.where(first, key, pltpu.roll(value, 64, 1)),
                jnp.where(first, pltpu.roll(key, 64, 1), value),
            )
            for k in range(2):
                for rep in range(nz * nc // KV_HEADS):
                    t = (pair * 2 + k) * (nz * nc // KV_HEADS) + rep
                    blocks[t // nc, t % nc, at, qcols : qcols + 128] = both[k].astype(BF)

    by_rows(own, pack)
    swap.start()
    tabs.start()
    dn.start()

    def norm(at):
        value = tokens[at, :].astype(F32)
        inverse = lax.rsqrt(jnp.mean(value * value, axis=-1, keepdims=True) + EPSILON)
        n1[at, :] = (value * inverse).astype(BF)

    by_rows(rows, norm)

    def spread_copies():
        for i, step in enumerate(others(nx, ny)):
            px, py = data_peer(step, nx, ny)
            slot = w_attn.at[x, :, :, y]
            yield remote(slot, slot, ds.at[i], dr.at[i], {"x": px, "y": py})

    def spread():
        swap.arrived()
        for copy in spread_copies():
            copy.start()

    def pack_mlp(at):
        gain = gains[at, 1:2]
        for k, weight in enumerate((w_gate, w_up)):
            for t in range(nz * nc):
                for i in range(nx):
                    chunk = (i * nc + t % nc) * nz + t // nc
                    to = (k * nx + i) * span
                    piece = weight[at, chunk * span : (chunk + 1) * span].astype(F32) * gain
                    mlp_blocks[t // nc, t % nc, at, to : to + span] = piece.astype(BF)

    end = flow(None, first_rows, None, [spread, lambda: by_rows(own, pack_mlp)])
    end()
    mlp_swap.start()
    tabs.arrived()
    for copy in spread_copies():
        copy.wait_recv()

    def project(i, carry):
        res = nn(n1g[i].reshape(nc * rows, width), w_attn[..., : qcols + 128].reshape(width, qcols + 128))
        cos, sin = rope_lanes(tab[i].reshape(nc * rows, 128))
        for p in range(pairs):
            u = res[:, p * 128 : p * 128 + 128]
            u = (u * cos + swap_halves(u) * sin) * (HEAD_DIM ** (-0.5))
            q[i, :, :, p * 128 : p * 128 + 128] = u.astype(BF).reshape(nc, rows, 128)
        u = res[:, qcols : qcols + 128]
        u = jnp.where(lanes(u.shape) < 64, u * cos + swap_halves(u) * sin, u).astype(BF)
        for pc in range(nc):
            kv[pc, i, y] = u[pc * rows : (pc + 1) * rows]
        return carry

    lax.fori_loop(0, nz, project, 0)
    sends = []
    for i in range(ny - 1):
        slot = kv.at[:, :, y]
        sends.append(remote(slot, slot, ys.at[i], yr.at[i], {"y": lax.rem(y + 1 + i, ny)}))
    for copy in sends:
        copy.start()
    for copy in sends:
        copy.wait_recv()

    def double(i, carry):
        pc, pz = i // nz, lax.rem(i, nz)
        u = kv[pc, pz].reshape(keys_span, 128).astype(F32)
        r = pltpu.roll(u, 64, 1)
        first = lanes(u.shape) < 64
        at = pl.ds(pl.multiple_of(pz * keys_span, keys_span), keys_span)
        kk[pc, at, :] = jnp.where(first, u, r).astype(BF)
        values = jnp.where(first, r, u)
        vv[pc, at, :] = values.astype(BF)
        vt[pc, :, at] = values.T.astype(BF)
        return carry

    lax.fori_loop(0, nc * nz, double, 0)

    def attend(pc, carry):
        for pz in range(nz):
            keys = (pz + 1) * keys_span
            bias = bias_of(tab[pz, pc], keys, (pz * ny + y) * rows)
            for p in range(pairs):
                q2 = two_heads(q[pz, pc, :, p * 128 : p * 128 + 128])
                s = nt(kk[pc, :keys, :], q2) + bias
                top = jnp.max(s, axis=0, keepdims=True)
                e = jnp.exp(s - top)
                total = jnp.sum(e, axis=0, keepdims=True)
                stat[pz, pc, p : p + 1, :] = top + jnp.log(total)
                weights = (e * (1.0 / total)).astype(BF)
                o = join_heads(nn(vt[pc, :, :keys], weights))
                ob[pz, pc, :, p * 128 : p * 128 + 128] = o.astype(BF)
        return carry

    lax.fori_loop(0, nc, attend, 0)

    def output(i, carry):
        half, odd = i // 2, lax.rem(i, 2)
        pz = odd * half + (1 - odd) * (nz - 1 - half)
        for px in range(nx):
            cols = slice(px * (width // nx), (px + 1) * (width // nx))
            weights = w_attn[px, :, :, :, :, qcols + 128 :].reshape(width // nx, qcols)
            res = nt(ob[pz].reshape(nc * rows, qcols), weights)
            part[pz, :, :, cols] = res.astype(BF).reshape(nc, rows, width // nx)
        reduce.across(pz).start()
        return carry

    lax.fori_loop(0, nz, output, 0)

    def spread_mlp():
        mlp_swap.arrived()
        gu.start()

    end2 = flow(reduce, cots, None, [spread_mlp])

    def settle(at, total):
        value = tokens[at, :].astype(F32) + total
        mid[at, :] = value
        inverse = lax.rsqrt(jnp.mean(value * value, axis=-1, keepdims=True) + EPSILON)
        n2[at, :] = (value * inverse).astype(BF)

    end3 = flow(None, next_rows, lambda half: reduce.last(half, settle))
    end3()
    end2()
    gu.arrived()
    dn.arrived()
    for one in (swap, tabs, mlp_swap, gu, dn):
        one.finish()
    for copy in list(spread_copies()) + sends:
        copy.wait_send()


def forward_call(dims, tokens, table, gains, w_query, w_key, w_value, w_out_t, w_gate, w_up, down, cot):
    nx, nc, nz, ny = dims
    rows, width = tokens.shape
    own = w_query.shape[0]
    qcols = HEADS // (nz * nc) * HEAD_DIM
    cols = 2 * qcols + 128
    peers, members = nx * ny - 1, nz * nc - 1
    mlp_cols = 2 * w_gate.shape[1] // (nz * nc)
    keys = nz * ny * rows
    team_rows = (nz, nc, rows, width)
    return call(
        functools.partial(forward_kernel, dims),
        (tokens, table, gains, w_query, w_key, w_value, w_out_t, w_gate, w_up, down, cot),
        (VM,) * 9 + (pl.ANY, VM),
        [
            (team_rows, BF),
            ((nx, nc, nz, ny, own, cols), BF),
            ((nz, nc) + table.shape, F32),
            ((nz, nc, rows, qcols), BF),
            ((nc, keys, 128), BF),
            ((nc, keys, 128), BF),
            ((nz, nc, 8, 2 * rows), F32),
            ((nz, nc, rows, qcols), BF),
            ((rows, width), F32),
            (team_rows, BF),
            (team_rows, BF),
            ((nx, nc, nz, ny, own, mlp_cols), BF),
            ((nx, ny) + down.shape, BF),
        ],
        (VM,) * 9 + (pl.ANY,) * 4,
        [
            VM((rows, width), BF),
            VM((nz, nc, own, cols), BF),
            VM((nz, nc, own, mlp_cols), BF),
            VM((nc, nz, own, mlp_cols), BF),
            VM((nc, nz, ny, rows, 128), BF),
            VM((nc, 128, keys), BF),
            VM(team_rows, BF),
        ]
        + Reduce.buffers(nz, rows, width)
        + [VM((rows, width), BF)]
        + Gather.SEMS
        + [DMA((members,))] * 4
        + [DMA((peers,))] * 4
        + [DMA((members,))] * 2
        + [DMA((max(ny - 1, 1),))] * 2
        + Reduce.SEMS
        + Gather.SEMS * 2
        + [DMA((peers,))] * 2
        + [DMA((5,))],
        1,
    )


def mlp_kernel(
    dims, n2g, cotg, w_mlp, w_dn, mid, cot,
    dx2, dag, output, came_mlp, came_dn, rest_dn,
    n2v, cotv, wv, wd, hid, hid_t, dmlp, part, mlp_out, grad_mlp, grad_dn,
    held, came, held2, came2, low,
    loads, rs, rr, rxs, rxr, os, orr, oxs, oxr, ds, dr, dl, ms, mr, ws, wr, local,
):
    nx, nc, nz, ny = dims
    x, c, z, y = place()
    rows, width = mid.shape
    ff2 = wv.shape[-1]
    ff = ff2 // 2
    piece = wd.shape[2]
    block = nc * rows
    fetch_w = pltpu.make_async_copy(w_mlp, wv, loads.at[0])
    fetch_d = pltpu.make_async_copy(w_dn, wd, loads.at[1])
    fetch_w.start()

    def fetch(at, k):
        source, target = ((n2g, n2v), (cotg, cotv))[k]
        return pltpu.make_async_copy(source.at[at], target.at[at], loads.at[2 + k * nz + at])

    order = [a for k in range(nz) for a in (nz - 1 - k, k)][:nz]
    for k in range(nz):
        fetch(order[k], 0).start()
        if k == 0:
            fetch_d.start()
        fetch(order[k], 1).start()
    greet(*dims)
    reduce = Reduce(part, held, came, rs, rr, rxs, rxr)
    reduce2 = Reduce(mlp_out, held2, came2, os, orr, oxs, oxr)
    into = Gather(low, dag, ds, dr, dl)
    gu = Spread(
        lambda px, py: grad_mlp.at[px, :, :, py], lambda px, py: came_mlp.at[px, py], ms, mr, local.at[0], nx, ny
    )
    dn = Spread(lambda px, py: grad_dn.at[px, py], lambda px, py: came_dn.at[px, py], ws, wr, local.at[1], nx, ny)
    half_width = width // 2

    def down_rows(cols):
        if piece % ROWS:
            return jnp.concatenate([wd[px, py, :, cols] for px in range(nx) for py in range(ny)], axis=0)
        return wd[:, :, :, cols].reshape(ff, -1)

    def weights(px):
        return wv[px].reshape(width // nx, ff2)

    fetch_w.wait()

    def forward_back(k, carry):
        half = k // 2
        odd = lax.rem(k, 2)
        at = odd * half + (1 - odd) * (nz - 1 - half)
        fetch(at, 0).wait()
        u = nn(n2v[at].reshape(block, width), wv[...].reshape(width, ff2))
        gt, up = u[:, :ff], u[:, ff:]
        sg = jax.nn.sigmoid(gt)
        silu = gt * sg
        value = (silu * up).astype(BF)
        hid[at] = value
        hid_t[:, pl.ds(pl.multiple_of(at * block, block), block)] = value.astype(F32).T.astype(BF)
        pl.when(k == 0)(fetch_d.wait)
        fetch(at, 1).wait()
        dh = nt(cotv[at].reshape(block, width), down_rows(slice(None)))
        dgt = dh * up * sg * (1.0 + gt * (1.0 - sg))
        dmlp[at] = jnp.concatenate([dgt, dh * silu], axis=1).astype(BF)

        for px in range(nx):
            cols = slice(px * (width // nx), (px + 1) * (width // nx))
            res = nt(dmlp[at], weights(px))
            part[at, :, :, cols] = res.astype(BF).reshape(nc, rows, width // nx)
        reduce.across(at).start()
        return carry

    lax.fori_loop(0, 2, forward_back, 0)
    chunk = width // 4

    def down_grad(part_of, target):
        def body(n, carry):
            at = pl.ds(pl.multiple_of(n * chunk, chunk), chunk)
            cols = pl.ds(pl.multiple_of(part_of * half_width + n * chunk, chunk), chunk)
            res = nn(hid_t[...], cotv[:, :, :, cols].reshape(nz * block, chunk)).astype(BF)
            for px in range(nx):
                for py in range(ny):
                    k = (px * ny + py) * piece
                    target[px, py, :, at] = res[k : k + piece]
            return carry

        lax.fori_loop(0, 2, body, 0)

    def mlp_grad(far):
        px = lax.rem(x + far, nx)
        size = width // (nx * 4)

        def body(j, carry):
            cols = pl.ds(pl.multiple_of(px * (width // nx) + j * size, size), size)
            res = tn(n2v[:, :, :, cols].reshape(nz * block, size), dmlp[...].reshape(nz * block, ff2))
            own = grad_mlp.shape[4]
            grad_mlp[px, j // 2, pl.ds(lax.rem(j, 2) * (nz // 2), nz // 2)] = res.astype(BF).reshape(
                nz // 2, ny, own, ff2
            )
            return carry

        lax.fori_loop(0, 4, body, 0)
        gu.start_along(far)

    def mlp_sum(n, carry):
        cols = pl.ds(pl.multiple_of(n * chunk, chunk), chunk)
        res = nn(hid[...].reshape(nz * block, ff), down_rows(cols))
        mlp_out[:, :, :, cols] = res.astype(BF).reshape(nz, nc, rows, chunk)
        return carry

    def down_first():
        down_grad(0, grad_dn)
        dn.start()

    def down_second():
        down_grad(1, rest_dn)

    def sum_all():
        lax.fori_loop(0, 4, mlp_sum, 0)
        reduce2.start()

    def more():
        lax.fori_loop(2, 3, forward_back, 0)

    def most():
        lax.fori_loop(3, nz, forward_back, 0)

    work = [more, most] + [functools.partial(mlp_grad, far) for far in reversed(range(nx))]
    end = flow(reduce, None, None, work + [down_first, down_second, sum_all])

    def settle(at, total):
        value = mid[at, :]
        inverse = lax.rsqrt(jnp.mean(value * value, axis=-1, keepdims=True) + EPSILON)
        normed = value * inverse
        gradient = cot[at, :].astype(F32) + inverse * (
            total - normed * jnp.mean(total * normed, axis=-1, keepdims=True)
        )
        dx2[at, :] = gradient
        low[at, :] = gradient.astype(BF)

    end2 = flow(reduce2, into, lambda part: reduce.last(part, settle))

    def finish(at, total):
        output[at, :] = (mid[at, :] + total).astype(BF)

    for half in range(PARTS):
        reduce2.last(half, finish)
    end2()
    end()
    gu.arrived()
    dn.arrived()
    gu.finish()
    dn.finish()


def mlp_call(dims, n2g, cotg, w_mlp, w_dn, mid, cot):
    nx, nc, nz, ny = dims
    rows, width = mid.shape
    own, ff2 = w_mlp.shape[4:]
    block = nc * rows
    peers = nx * ny - 1
    half_dn = w_dn.shape[:3] + (width // 2,)
    return call(
        functools.partial(mlp_kernel, dims),
        (n2g, cotg, w_mlp, w_dn, mid, cot),
        (pl.ANY, pl.ANY, pl.ANY, pl.ANY, VM, VM),
        [
            ((rows, width), F32),
            ((nz, nc, rows, width), BF),
            ((rows, width), BF),
            ((nx, ny, nc, nz, own, ff2), BF),
            (half_dn, BF),
            (half_dn, BF),
        ],
        (VM, pl.ANY, VM, pl.ANY, pl.ANY, VM),
        [
            VM(n2g.shape, BF),
            VM(cotg.shape, BF),
            VM(w_mlp.shape, BF),
            VM(w_dn.shape, BF),
            VM((nz, block, ff2 // 2), BF),
            VM((ff2 // 2, nz * block), BF),
            VM((nz, block, ff2), BF),
            VM(n2g.shape, BF),
            VM(n2g.shape, BF),
            VM(w_mlp.shape, BF),
            VM(half_dn, BF),
        ]
        + Reduce.buffers(nz, rows, width) * 2
        + [VM((rows, width), BF), DMA((2 + 2 * nz,))]
        + Reduce.SEMS * 2
        + Gather.SEMS
        + [DMA((peers,))] * 4
        + [DMA((2,))],
        3,
    )


def backward_kernel(
    dims, dag, w, tab, q, kk, vv, stat, ob, came_mlp, came_dn, rest_dn, n1g, tokens, dx2, gains,
    w_query, w_key, w_value, w_gate, w_up,
    input_grad, grad_query, grad_key, grad_value, grad_out_t, grad_gate, grad_up, grad_down, grad_gain,
    do, kt, dk, dv, out, near, dqkv, part, team, stage, mlp_sum, mlp_g, rest_came, grad_attn, came_attn, sums, attn_g,
    held, came,
    loads, us, ur, ys, yr, ws, wr, rs, rr, rxs, rxr, ds, dr, ss, sr, local,
):
    nx, nc, nz, ny = dims
    x, c, z, y = place()
    rows, width = tokens.shape
    own = w_query.shape[0]
    qcols = q.shape[-1]
    pairs = qcols // 128
    keys_span = ny * rows
    ff_span = mlp_g.shape[-1] // (2 * nx)
    fetch_dag = pltpu.make_async_copy(dag, team, loads.at[2])
    fetch = pltpu.make_async_copy(n1g, team, loads.at[2])
    fetch_dag.start()
    mlp_swap = Swap(
        lambda pz, pc: mlp_sum.at[pz, pc], lambda pz, pc: mlp_g.at[pz, pc], us, ur, local.at[0], nz, nc
    )
    dn = Spread(lambda px, py: rest_dn.at[px, py], lambda px, py: rest_came.at[px, py], ws, wr, local.at[1], nx, ny)
    reduce = Reduce(part, held, came, rs, rr, rxs, rxr)
    spread = Spread(
        lambda px, py: grad_attn.at[px, :, :, py], lambda px, py: came_attn.at[px, py], ds, dr, local.at[2], nx, ny
    )
    swap = Swap(lambda pz, pc: sums.at[pz, pc], lambda pz, pc: attn_g.at[pz, pc], ss, sr, local.at[3], nz, nc)

    steps = others(nz, nc) + [(0, 0)]

    def load(i):
        pz, pc = team_peer(steps[i], nz, nc)
        return pltpu.make_async_copy(came_mlp.at[:, :, pc, pz], stage.at[i % 2], loads.at[i % 2])

    load(0).start()
    greet(*dims, cross=True)
    dn.start()
    for i, copy in enumerate(list(mlp_swap.copies()) + [mlp_swap.own()]):
        if i + 1 < len(steps):
            load(i + 1).start()
        load(i).wait()
        pz, pc = team_peer(steps[i], nz, nc)

        def add(at, i=i, pz=pz, pc=pc):
            total = stage[i % 2, 0, 0, at, :].astype(F32)
            for px, py in others(nx, ny):
                total = total + stage[i % 2, px, py, at, :].astype(F32)
            mlp_sum[pz, pc, at, :] = total.astype(BF)

        by_rows(own, add)
        copy.start()
    fetch_dag.wait()

    def project(i, carry):
        weights = w[..., qcols + 128 :].reshape(width, qcols)
        do[i] = nn(team[i].reshape(nc * rows, width), weights).astype(BF).reshape(nc, rows, qcols)
        return carry

    lax.fori_loop(0, nz, project, 0)

    def turned(i, carry):
        pc, pz = i // nz, lax.rem(i, nz)
        at = pl.ds(pl.multiple_of(pz * keys_span, keys_span), keys_span)
        kt[pc, :, at] = kk[pc, at, :].astype(F32).T.astype(BF)
        return carry

    lax.fori_loop(0, nc * nz, turned, 0)

    def attend(pc, carry):
        for pz in reversed(range(nz)):
            keys = (pz + 1) * keys_span
            most = KEYS if nz * keys_span <= KEYS else KEYS // 4
            cuts = [slice(a, min(a + most, keys)) for a in range(0, keys, most)]

            def bias_at(i, cuts=cuts, pz=pz):
                cut = cuts[i]
                return bias_of(tab[pz, pc], cut.stop - cut.start, (pz * ny + y) * rows, cut.start)

            only = bias_at(0) if len(cuts) == 1 else None
            cos, sin = rope_lanes(tab[pz, pc])
            for p in range(pairs):
                q2 = two_heads(q[pz, pc, :, p * 128 : p * 128 + 128])
                do2 = two_heads(do[pz, pc, :, p * 128 : p * 128 + 128])

                def scores(i, cuts=cuts, only=only, bias_at=bias_at, q2=q2, do2=do2, p=p, pz=pz):
                    s = nt(kk[pc, cuts[i], :], q2) + (bias_at(i) if only is None else only)
                    weights = jnp.exp(s - stat[pz, pc, p : p + 1, :])
                    return weights, weights * nt(vv[pc, cuts[i], :], do2)

                delta = sum(jnp.sum(scores(i)[1], axis=0, keepdims=True) for i in range(1, len(cuts)))
                u = 0.0
                for i, cut in enumerate(cuts):
                    weights, dw = scores(i)
                    if i == 0:
                        delta = delta + jnp.sum(dw, axis=0, keepdims=True)
                    score_grad = (dw - weights * delta).astype(BF)
                    dv_new = nn(weights.astype(BF), do2)
                    dk_new = nn(score_grad, q2)
                    if pz == nz - 1 and p == 0:
                        dv[pc, cut, :] = dv_new
                        dk[pc, cut, :] = dk_new
                    else:
                        dv[pc, cut, :] += dv_new
                        dk[pc, cut, :] += dk_new
                    u = u + nn(kt[pc, :, cut], score_grad)
                u = join_heads(u) * (HEAD_DIM ** (-0.5))
                u = u * cos - swap_halves(u) * sin
                dqkv[pz, pc, :, p * 128 : p * 128 + 128] = u.astype(BF)
        return carry

    lax.fori_loop(0, nc, attend, 0)

    def fold(i, carry):
        pc, pz = i // nz, lax.rem(i, nz)
        at = pl.ds(pl.multiple_of(pz * keys_span, keys_span), keys_span)
        key, value = dk[pc, at, :], dv[pc, at, :]
        first = lanes(key.shape) < 64
        both = jnp.where(first, key + pltpu.roll(key, 64, 1), value + pltpu.roll(value, 64, 1))
        both = both.astype(BF)
        for py in range(ny):
            out[pc, py, pz] = both[py * rows : (py + 1) * rows]
        return carry

    lax.fori_loop(0, nc * nz, fold, 0)
    sends = []
    for i, (sy, sc) in enumerate(others(ny, nc)):
        py, pc = lax.rem(y + sy, ny), lax.rem(c + sc, nc)
        sends.append(remote(out.at[pc, py], near.at[i], ys.at[i], yr.at[i], {"y": py, "core": pc}))
    for copy in sends:
        copy.start()

    def weight_grad(left, right, first, last):
        def body(j, carry):
            px, k = j // 4, lax.rem(j, 4)
            size = width // (nx * 4)
            cols = pl.ds(pl.multiple_of(j * size, size), size)
            res = tn(left[:, :, :, cols].reshape(nz * nc * rows, size), right.reshape(nz * nc * rows, last - first))
            grad_attn[px, k // 2, pl.ds(lax.rem(k, 2) * (nz // 2), nz // 2), :, :, first:last] = res.astype(
                BF
            ).reshape(nz // 2, ny, own, last - first)
            return carry

        lax.fori_loop(0, nx * 4, body, 0)

    weight_grad(team, ob[...], qcols + 128, 2 * qcols + 128)
    fetch.start()
    for copy in sends:
        copy.wait_recv()

    def settle_kv(pz, carry):
        total = out[c, y, pz].astype(F32)
        for i in range(len(sends)):
            total = total + near[i, pz].astype(F32)
        cos, sin = rope_lanes(tab[pz, c])
        first = lanes(total.shape) < 64
        total = jnp.where(first, total * cos - swap_halves(total) * sin, total)
        dqkv[pz, c, :, qcols : qcols + 128] = total.astype(BF)
        dqkv[pz, 1 - c, :, qcols : qcols + 128] = jnp.zeros((rows, 128), BF)
        return carry

    lax.fori_loop(0, nz, settle_kv, 0)

    def output(i, carry):
        half, odd = i // 2, lax.rem(i, 2)
        pz = odd * half + (1 - odd) * (nz - 1 - half)
        for px in range(nx):
            cols = slice(px * (width // nx), (px + 1) * (width // nx))
            weights = w[px, :, :, :, :, : qcols + 128].reshape(width // nx, qcols + 128)
            res = nt(dqkv[pz].reshape(nc * rows, qcols + 128), weights)
            part[pz, :, :, cols] = res.astype(BF).reshape(nc, rows, width // nx)
        reduce.across(pz).start()
        return carry

    lax.fori_loop(0, nz, output, 0)

    def own_weights():
        fetch.wait()
        weight_grad(team, dqkv[...], 0, qcols + 128)
        spread.start()

    def unpack_mlp(at):
        gain = gains[at, 1:2]
        dots = jnp.zeros(gain.shape, F32)
        for k, (grad, weight) in enumerate(((grad_gate, w_gate), (grad_up, w_up))):
            for t in range(nz * nc):
                for i in range(nx):
                    chunk = (i * nc + t % nc) * nz + t // nc
                    source = (k * nx + i) * ff_span
                    cols = slice(chunk * ff_span, (chunk + 1) * ff_span)
                    value = mlp_g[t // nc, t % nc, at, source : source + ff_span].astype(F32)
                    grad[at, cols] = value * gain
                    dots = dots + jnp.sum(value * weight[at, cols].astype(F32), axis=-1, keepdims=True)
        grad_gain[at, :] = jnp.broadcast_to(dots, (dots.shape[0], 128))

    def unpack_all():
        mlp_swap.arrived()
        by_rows(own, unpack_mlp)

    def down_all():
        dn.arrived()
        half = width // 2

        def down(at):
            for source, cols in ((came_dn, slice(0, half)), (rest_came, slice(half, width))):
                total = source[0, 0, at, :].astype(F32)
                for px, py in others(nx, ny):
                    total = total + source[px, py, at, :].astype(F32)
                grad_down[at, cols] = total

        by_rows(grad_down.shape[0], down)

    def add_attn(at):
        for pz in range(nz):
            for pc in range(nc):
                total = came_attn[0, 0, pc, pz, at, :].astype(F32)
                for px, py in others(nx, ny):
                    total = total + came_attn[px, py, pc, pz, at, :].astype(F32)
                sums[pz, pc, at, :] = total.astype(BF)

    def exchange():
        spread.arrived()
        by_rows(own, add_attn)
        swap.start()

    def nothing():
        return None

    end = flow(reduce, None, None, [own_weights, unpack_all, nothing, down_all, nothing, exchange])

    def settle(at, total):
        value = tokens[at, :].astype(F32)
        inverse = lax.rsqrt(jnp.mean(value * value, axis=-1, keepdims=True) + EPSILON)
        normed = value * inverse
        input_grad[at, :] = dx2[at, :] + inverse * (
            total - normed * jnp.mean(total * normed, axis=-1, keepdims=True)
        )

    for half in range(PARTS):
        reduce.last(half, settle)
    end()
    swap.arrived()

    def unpack(at):
        gain = gains[at, 0:1]
        dots = jnp.zeros(gain.shape, F32)
        heads = []
        for t in range(nz * nc):
            block = attn_g[t // nc, t % nc, at, :].astype(F32)
            cols = slice(t * qcols, (t + 1) * qcols)
            grad_query[at, cols] = block[:, :qcols] * gain
            dots = dots + jnp.sum(block[:, :qcols] * w_query[at, cols].astype(F32), axis=-1, keepdims=True)
            grad_out_t[at, cols] = block[:, qcols + 128 :]
            if t % (nz * nc // KV_HEADS):
                heads[-1] = heads[-1] + block[:, qcols : qcols + 128]
            else:
                heads.append(block[:, qcols : qcols + 128])
        for pair in range(KV_HEADS // 2):
            one, two = heads[2 * pair], heads[2 * pair + 1]
            first = lanes(one.shape) < 64
            cols = slice(pair * 128, pair * 128 + 128)
            key = jnp.where(first, one, pltpu.roll(two, 64, 1))
            value = jnp.where(first, pltpu.roll(one, 64, 1), two)
            grad_key[at, cols] = key * gain
            grad_value[at, cols] = value * gain
            both = key * w_key[at, cols].astype(F32) + value * w_value[at, cols].astype(F32)
            dots = dots + jnp.sum(both, axis=-1, keepdims=True)
        old = grad_gain[at, :]
        grad_gain[at, :] = jnp.where(lanes(old.shape) < 64, dots, old)

    by_rows(own, unpack)
    for one in (mlp_swap, dn, spread, swap):
        one.finish()
    for copy in sends:
        copy.wait_send()


def backward_call(
    dims, dag, w, tab, q, kk, vv, stat, ob, came_mlp, came_dn, rest_dn, n1g, tokens, dx2, gains,
    w_query, w_key, w_value, w_gate, w_up,
):
    nx, nc, nz, ny = dims
    rows, width = tokens.shape
    own = w_query.shape[0]
    qcols = q.shape[-1]
    keys = nz * ny * rows
    peers, members, near = nx * ny - 1, nz * nc - 1, ny * nc - 1
    cols, mlp_cols = w.shape[-1], came_mlp.shape[-1]
    team_rows = (nz, nc, rows, width)
    return call(
        functools.partial(backward_kernel, dims),
        (
            dag, w, tab, q, kk, vv, stat, ob, came_mlp, came_dn, rest_dn, n1g, tokens, dx2, gains,
            w_query, w_key, w_value, w_gate, w_up,
        ),
        (pl.ANY,) + (VM,) * 7 + (pl.ANY, VM, pl.ANY, pl.ANY) + (VM,) * 8,
        [
            ((rows, width), F32),
            (w_query.shape, F32),
            (w_key.shape, F32),
            (w_value.shape, F32),
            (w_query.shape, F32),
            (w_gate.shape, F32),
            (w_up.shape, F32),
            ((came_dn.shape[2], width), F32),
            ((own, 128), F32),
        ],
        (VM,) * 9,
        [
            VM((nz, nc, rows, qcols), BF),
            VM((nc, 128, keys), BF),
            VM((nc, keys, 128), F32),
            VM((nc, keys, 128), F32),
            VM((nc, ny, nz, rows, 128), BF),
            VM((near, nz, rows, 128), BF),
            VM((nz, nc, rows, qcols + 128), BF),
            VM(team_rows, BF),
            VM(team_rows, BF),
            VM((2, nx, ny, own, mlp_cols), BF),
            VM((nz, nc, own, mlp_cols), BF),
            VM((nz, nc, own, mlp_cols), BF),
            VM(rest_dn.shape, BF),
            VM((nx, nc, nz, ny, own, cols), BF),
            VM((nx, ny, nc, nz, own, cols), BF),
            VM((nz, nc, own, cols), BF),
            VM((nz, nc, own, cols), BF),
        ]
        + Reduce.buffers(nz, rows, width)
        + [DMA((3,))]
        + [DMA((members,))] * 2
        + [DMA((near,))] * 2
        + [DMA((peers,))] * 2
        + Reduce.SEMS
        + [DMA((peers,))] * 2
        + [DMA((members,))] * 2
        + [DMA((4,))],
        6,
    )


def shards(
    tokens, positions, doc_start, cotangent, w_query, w_key, w_value, w_out,
    attn_gain, w_gate, w_up, w_down, mlp_gain,
):
    dims = tuple(lax.axis_size(a) for a in ALL)
    rows = tokens.shape[0]

    gains = jnp.stack([attn_gain, mlp_gain], axis=1).astype(F32)
    half = HEAD_DIM // 2
    frequency = 10000.0 ** (-2.0 * jnp.arange(half, dtype=F32) / HEAD_DIM)
    angles = positions.astype(F32)[:, None] * frequency[None, :]
    table = jnp.concatenate(
        [
            jnp.cos(angles),
            jnp.sin(angles),
            jnp.broadcast_to(doc_start.astype(F32)[:, None], (rows, HEAD_DIM)),
        ],
        axis=-1,
    )
    n1g, w_attn, tab, q, kk, vv, stat, ob, mid, n2g, cotg, w_mlp, w_dn = forward_call(
        dims, tokens, table, gains, w_query, w_key, w_value, w_out.T, w_gate, w_up, w_down, cotangent
    )
    dx2, dag, output, came_mlp, came_dn, rest_dn = mlp_call(dims, n2g, cotg, w_mlp, w_dn, mid, cotangent)
    (
        input_grad, grad_query, grad_key, grad_value, grad_out_t, grad_gate, grad_up, grad_down, grad_gain
    ) = backward_call(
        dims, dag, w_attn, tab, q, kk, vv, stat, ob, came_mlp, came_dn, rest_dn, n1g, tokens, dx2, gains,
        w_query, w_key, w_value, w_gate, w_up,
    )
    return (
        output, input_grad, grad_query, grad_key, grad_value, grad_out_t.T, grad_gain[:, 0],
        grad_gate, grad_up, grad_down, grad_gain[:, 64],
    )


def solution(mesh):
    fsdp, seq = mesh.shape["fsdp"], mesh.shape["seq"]
    nc, nz = 2, 4
    grid = Mesh(mesh.devices.reshape(fsdp // nc, nc, nz, seq // nz), ALL)
    row, col, vec = P(ALL, None), P(None, ALL), P(ALL)
    in_specs = (row, vec, vec, row, row, row, row, col, vec, row, row, row, vec)
    out_specs = (row, row, row, row, row, col, vec, row, row, row, vec)
    return jax.shard_map(shards, mesh=grid, in_specs=in_specs, out_specs=out_specs, check_vma=False)
```

```python
import functools

import jax
import jax.numpy as jnp
from jax import lax
from jax.experimental import pallas as pl
from jax.experimental.pallas import tpu as pltpu
from jax.sharding import Mesh
from jax.sharding import PartitionSpec as P

HEADS = 32
KV_HEADS = 4
HEAD_DIM = 64
EPSILON = 1e-05
MASKED = -1e30
ALL = ("x", "core", "z", "y")
TEAM = ("z", "core")
DATA = ("x", "y")
BF = jnp.bfloat16
F32 = jnp.float32


MESH = pl.DeviceIdType.MESH
VM = pltpu.VMEM
DMA = pltpu.SemaphoreType.DMA
ROWS = 16
PARTS = 2
WINDOW = 2
KEYS = 1024


def place():
    return tuple(lax.axis_index(a) for a in ALL)


def others(nx, ny):
    return [(i, j) for i in range(nx) for j in range(ny) if (i, j) != (0, 0)]


def data_peer(step, nx, ny):
    x, _, _, y = place()
    return lax.rem(x + step[0], nx), lax.rem(y + step[1], ny)


def team_peer(step, nz, nc):
    _, c, z, _ = place()
    return lax.rem(z + step[0], nz), lax.rem(c + step[1], nc)


def greet(nx, nc, nz, ny, cross=False):
    barrier = pltpu.get_barrier_semaphore()
    x, c, z, y = place()
    extra = ny - 1 if cross else 0
    for i in range(extra):
        device = {"y": lax.rem(y + 1 + i, ny), "core": 1 - c}
        pl.semaphore_signal(barrier, inc=1, device_id=device, device_id_type=MESH)
    for step in others(nx, ny):
        px, py = data_peer(step, nx, ny)
        pl.semaphore_signal(barrier, inc=1, device_id={"x": px, "y": py}, device_id_type=MESH)
    for step in others(nz, nc):
        pz, pc = team_peer(step, nz, nc)
        pl.semaphore_signal(barrier, inc=1, device_id={"z": pz, "core": pc}, device_id_type=MESH)

    def met():
        pl.semaphore_wait(barrier, nx * ny - 1 + nz * nc - 1 + extra)

    return met


def remote(source, target, send, recv, device):
    return pltpu.make_async_remote_copy(
        src_ref=source, dst_ref=target, send_sem=send, recv_sem=recv,
        device_id=device, device_id_type=MESH,
    )


def piece_of(part, rows):
    return pl.ds(part * (rows // PARTS), rows // PARTS)


class Gather:
    SEMS = [DMA((3, 4, PARTS)), DMA((2, 4, PARTS)), DMA((PARTS,))]

    def __init__(self, own, full, send, recv, local):
        self.own, self.full, self.send, self.recv, self.local = own, full, send, recv, local
        self.x, self.c, self.z, self.y = place()
        self.nz, _, self.rows = full.shape[:3]

    def copy(self, at, kind, part, mine=False):
        rows = piece_of(part, self.rows)
        slot = self.full.at[at, self.c, rows]
        device = ({"z": self.z + 1}, {"z": self.z - 1}, {"core": 1 - self.c})[kind]
        return remote(
            self.own.at[rows] if mine else slot, slot, self.send.at[kind, at, part],
            self.recv.at[0 if kind < 2 else 1, at, part], device,
        )

    def keep(self, part):
        rows = piece_of(part, self.rows)
        return pltpu.make_async_copy(self.own.at[rows], self.full.at[self.z, self.c, rows], self.local.at[part])

    def begin(self, part):
        self.keep(part).start()
        self.copy(self.z, 2, part, True).start()

    def finish(self):
        for part in range(PARTS):
            self.keep(part).wait()
            for at in range(self.nz):
                self.copy(at, 2, part).wait_send()
                self.copy(at, 2, part).wait_recv()


class Reduce:
    SEMS = [DMA((2, 4, PARTS)), DMA((2, 4, PARTS)), DMA((4,)), DMA((4,))]

    @staticmethod
    def buffers(nz, rows, width):
        return [VM((nz, rows, width), BF), VM((2, nz - 1, rows, width), BF)]

    def __init__(self, part, held, came, send, recv, across_send, across_recv):
        self.part, self.held, self.came, self.send, self.recv = part, held, came, send, recv
        self.across_send, self.across_recv = across_send, across_recv
        self.x, self.c, self.z, self.y = place()
        self.nz, _, self.rows, self.width = part.shape

    def across(self, to):
        return remote(
            self.part.at[to, 1 - self.c], self.held.at[to], self.across_send.at[to], self.across_recv.at[to],
            {"core": 1 - self.c},
        )

    def along(self, to, way, part):
        device = ({"z": self.z + 1}, {"z": self.z - 1})[way]
        rows = piece_of(part, self.rows)
        return remote(
            self.held.at[to, rows], self.came.at[way, to - 1 + way, rows], self.send.at[way, to, part],
            self.recv.at[way, to, part], device,
        )

    def start(self):
        for to in [a for k in range(self.nz) for a in (self.nz - 1 - k, k)][: self.nz]:
            self.across(to).start()

    def add(self, to, ways, part, out=None):
        size = self.rows // PARTS

        def body(i, carry):
            at = pl.ds(pl.multiple_of(part * size + i * ROWS, ROWS), ROWS)
            total = self.part[to, self.c, at, :].astype(F32) + self.held[to, at, :].astype(F32)
            for way in ways:
                total = total + self.came[way, to - 1 + way, at, :].astype(F32)
            if out is None:
                self.held[to, at, :] = total.astype(BF)
            else:
                out(at, total)
            return carry

        lax.fori_loop(0, size // ROWS, body, 0)

    def last(self, part, out):
        if part == 0:
            self.across(self.z).wait_recv()
        for at in range(self.nz):

            @pl.when(self.z == at)
            def _(at=at):
                ways = ([0] if at > 0 else []) + ([1] if at < self.nz - 1 else [])
                for way in ways:
                    self.along(at, way, part).wait_recv()
                self.add(at, ways, part, out)

    def finish(self):
        for to in range(self.nz):
            self.across(to).wait_send()


def plan(nz, reduces, gathers):
    last = nz - 1
    rows = []
    for e in range(nz):
        sums = [("R", last - k) for k in range(last) if last - k > e]
        blocks = [("G", e - k) for k in range(e + 1)]
        if reduces and gathers:
            if e == last:
                rows.append([None] + blocks[1:-1] + [None] + blocks[-1:])
            else:
                woven = blocks[:-1] + sums[:1] + blocks[-1:] + sums[1:]
                rows.append(woven)
        elif reduces:
            rows.append([None] * e + sums)
        else:
            rows.append(blocks if e < last else [None] + blocks[1:])
    return rows


def by_need(nz, z, k):
    last = nz - 1
    value = 0
    for at in range(nz):
        when = {to: at + last - to if to > at else last - at + to for to in range(nz) if to != at}
        blocks = sorted(when, key=lambda to: (when[to], to)) + [at]
        value = jnp.where(z == at, blocks[k], value)
    return value


def flow(reduce, gather, before=None, work=()):
    work = list(work)
    any_one = reduce or gather
    nz, z = any_one.nz, any_one.z
    table = plan(nz, reduce is not None, gather is not None)
    pending = {(way, e): [] for way in (0, 1) for e in range(nz)}

    def pace(key, make):
        queue = pending[key]
        if len(queue) >= WINDOW:
            queue.pop(0)().wait_send()
        make().start()
        queue.append(make)

    def step(way, e, kind, place_at, part):
        block = place_at if way == 0 else nz - 1 - place_at
        if kind == "R":
            if part == 0:
                reduce.across(block).wait_recv()
            if e > 0:
                reduce.along(block, way, part).wait_recv()
            reduce.add(block, (way,) if e > 0 else (), part)
            pace((way, e), functools.partial(reduce.along, block, way, part))
        else:
            mine = place_at == e
            if not mine:
                gather.copy(block, way, part).wait_recv()
            if e < nz - 1:
                pace((way, e), functools.partial(gather.copy, block, way, part, mine))
            if not mine:
                gather.copy(block, 2, part).start()

    for t in range(max(len(row) for row in table)):
        for part in range(PARTS):
            if t == 0 and before is not None:
                before(part)
            if t == 0 and gather is not None:
                gather.begin(part)
            for way in (0, 1):
                for e in range(nz):
                    op = table[e][t] if t < len(table[e]) else None
                    if op is not None:
                        pl.when(z == (e if way == 0 else nz - 1 - e))(
                            functools.partial(step, way, e, op[0], op[1], part)
                        )
            if work and (t > 0 or part == PARTS - 1):
                work.pop(0)()
    for item in work:
        item()

    def finish():
        for (way, e), queue in pending.items():
            if queue:

                @pl.when(z == (e if way == 0 else nz - 1 - e))
                def _(queue=queue):
                    for make in queue:
                        make().wait_send()

        for one in (reduce, gather):
            if one is not None:
                one.finish()

    return finish


class Spread:
    def __init__(self, source, target, send, recv, local, nx, ny):
        self.source, self.target, self.send, self.recv = source, target, send, recv
        self.nx, self.ny = nx, ny
        self.x, _, _, self.y = place()
        self.own = lambda: pltpu.make_async_copy(source(self.x, self.y), target(self.x, self.y), local)

    def copies(self):
        for i, step in enumerate(others(self.nx, self.ny)):
            px, py = data_peer(step, self.nx, self.ny)
            yield remote(
                self.source(px, py), self.target(self.x, self.y), self.send.at[i], self.recv.at[i],
                {"x": px, "y": py},
            )

    def start(self):
        for copy in self.copies():
            copy.start()
        self.own().start()

    def start_some(self, first, last):
        for i, copy in enumerate(self.copies()):
            if first <= i < last:
                copy.start()

    def start_along(self, far):
        for step, copy in zip(others(self.nx, self.ny), self.copies()):
            if step[0] == far:
                copy.start()
        if far == 0:
            self.own().start()

    def arrived(self):
        self.own().wait()
        for copy in self.copies():
            copy.wait_recv()

    def finish(self):
        for copy in self.copies():
            copy.wait_send()


class Swap:
    def __init__(self, source, slot, send, recv, local, nz, nc):
        self.source, self.slot, self.send, self.recv, self.nz, self.nc = source, slot, send, recv, nz, nc
        _, self.c, self.z, _ = place()
        self.own = lambda: pltpu.make_async_copy(source(self.z, self.c), slot(self.z, self.c), local)

    def copies(self):
        for i, step in enumerate(others(self.nz, self.nc)):
            pz, pc = team_peer(step, self.nz, self.nc)
            yield remote(
                self.source(pz, pc), self.slot(self.z, self.c), self.send.at[i], self.recv.at[i],
                {"z": pz, "core": pc},
            )

    def start(self):
        for copy in self.copies():
            copy.start()
        self.own().start()

    def arrived(self):
        self.own().wait()
        for copy in self.copies():
            copy.wait_recv()

    def finish(self):
        for copy in self.copies():
            copy.wait_send()


def call(kernel, operands, in_spaces, outs, out_spaces, scratch, number):
    return pl.pallas_call(
        kernel,
        out_shape=[jax.ShapeDtypeStruct(s, t) for s, t in outs],
        in_specs=[pl.BlockSpec(memory_space=s) for s in in_spaces],
        out_specs=[pl.BlockSpec(memory_space=s) for s in out_spaces],
        scratch_shapes=scratch,
        compiler_params=pltpu.CompilerParams(
            collective_id=number, has_side_effects=True, vmem_limit_bytes=60 << 20
        ),
    )(*operands)


def lanes(shape):
    return lax.broadcasted_iota(jnp.int32, shape, len(shape) - 1)


def by_rows(count, body):
    if count % ROWS or count == ROWS:
        body(slice(0, count))
    else:

        def step(i, carry):
            body(pl.ds(pl.multiple_of(i * ROWS, ROWS), ROWS))
            return carry

        lax.fori_loop(0, count // ROWS, step, 0)


def nt(a, b):
    return lax.dot_general(a, b, (((1,), (1,)), ((), ())), preferred_element_type=F32)


def nn(a, b):
    return jnp.dot(a, b, preferred_element_type=F32)


def tn(a, b):
    return lax.dot_general(a, b, (((0,), (0,)), ((), ())), preferred_element_type=F32)


def rope_lanes(tab):
    at = lanes(tab.shape)
    cos = jnp.where(at < 32, tab, 0.0)
    sin = jnp.where((at >= 32) & (at < 64), tab, 0.0)
    cos = cos + pltpu.roll(cos, 32, 1)
    cos = cos + pltpu.roll(cos, 64, 1)
    sin = sin - pltpu.roll(sin, 96, 1)
    sin = sin + pltpu.roll(sin, 64, 1)
    return cos, sin


def swap_halves(u):
    return jnp.where(lax.rem(lanes(u.shape), 64) < 32, pltpu.roll(u, 96, 1), pltpu.roll(u, 32, 1))


def two_heads(u):
    first = lanes(u.shape) < 64
    zero = jnp.zeros_like(u)
    return jnp.concatenate([jnp.where(first, u, zero), jnp.where(first, zero, u)], axis=0)


def join_heads(t):
    rows = t.shape[1] // 2
    return jnp.concatenate([t[:64, :rows], t[64:, rows:]], axis=0).T


def bias_of(tab, keys, first_row, first_key=0):
    rows = tab.shape[0]
    starts = tab.T[64:65, :].astype(jnp.int32)
    key = first_key + lax.broadcasted_iota(jnp.int32, (keys, rows), 0)
    row = first_row + lax.broadcasted_iota(jnp.int32, (keys, rows), 1)
    bias = jnp.where((key >= starts) & (key <= row), 0.0, MASKED)
    return jnp.concatenate([bias, bias], axis=1)


def forward_kernel(
    dims, tokens, table, gains, w_query, w_key, w_value, w_out_t, w_gate, w_up, down, cot,
    n1_out, w_out, tab, q, kk, vv, stat, ob, mid, n2g, cotg, w_mlp, w_dn,
    n1g, w_attn, n1, blocks, mlp_blocks, mlp_t, kv, vt, part, held, came, n2,
    gs, gr, gl, ts, tr, ss, sr, ds, dr, ws, wr, us, ur, ys, yr, rs, rr, rxs, rxr, cs, cr, cl, ns, nr, nl, ms, mr, local,
):
    nx, nc, nz, ny = dims
    x, c, z, y = place()
    rows, width = tokens.shape
    own = w_query.shape[0]
    qcols = q.shape[-1]
    pairs = qcols // 128
    span = w_gate.shape[1] // (nx * nc * nz)
    keys_span = ny * rows
    dn = Spread(lambda px, py: down, lambda px, py: w_dn.at[px, py], ws, wr, local.at[0], nx, ny)
    swap = Swap(
        lambda pz, pc: blocks.at[pz, pc], lambda pz, pc: w_attn.at[x, pc, pz, y], ss, sr, local.at[1], nz, nc
    )
    tabs = Swap(lambda pz, pc: table, lambda pz, pc: tab.at[pz, pc], ts, tr, local.at[2], nz, nc)
    mlp_swap = Swap(
        lambda pz, pc: mlp_blocks.at[pz, pc], lambda pz, pc: mlp_t.at[pc, pz], us, ur, local.at[3], nz, nc
    )
    gu = Spread(lambda px, py: mlp_t, lambda px, py: w_mlp.at[px, :, :, py], ms, mr, local.at[4], nx, ny)
    first_rows = Gather(n1, n1g, gs, gr, gl)
    reduce = Reduce(part, held, came, rs, rr, rxs, rxr)
    cots = Gather(cot, cotg, cs, cr, cl)
    next_rows = Gather(n2, n2g, ns, nr, nl)
    met = greet(*dims)

    def pack(at):
        gain = gains[at, 0:1]
        for t in range(nz * nc):
            cols = slice(t * qcols, (t + 1) * qcols)
            blocks[t // nc, t % nc, at, :qcols] = (w_query[at, cols].astype(F32) * gain).astype(BF)
            blocks[t // nc, t % nc, at, qcols + 128 :] = w_out_t[at, cols]
        for pair in range(KV_HEADS // 2):
            cols = slice(pair * 128, pair * 128 + 128)
            key, value = w_key[at, cols].astype(F32) * gain, w_value[at, cols].astype(F32) * gain
            first = lanes(key.shape) < 64
            both = (
                jnp.where(first, key, pltpu.roll(value, 64, 1)),
                jnp.where(first, pltpu.roll(key, 64, 1), value),
            )
            for k in range(2):
                for rep in range(nz * nc // KV_HEADS):
                    t = (pair * 2 + k) * (nz * nc // KV_HEADS) + rep
                    blocks[t // nc, t % nc, at, qcols : qcols + 128] = both[k].astype(BF)

    def norm(at):
        value = tokens[at, :].astype(F32)
        inverse = lax.rsqrt(jnp.mean(value * value, axis=-1, keepdims=True) + EPSILON)
        n1[at, :] = (value * inverse).astype(BF)

    by_rows(rows, norm)
    by_rows(own, pack)
    met()
    swap.start()
    tabs.start()
    dn.start()

    def spread_copies():
        for i, step in enumerate(others(nx, ny)):
            px, py = data_peer(step, nx, ny)
            slot = w_attn.at[x, :, :, y]
            yield remote(slot, slot, ds.at[i], dr.at[i], {"x": px, "y": py})

    def spread():
        swap.arrived()
        for copy in spread_copies():
            copy.start()

    def pack_mlp(at):
        gain = gains[at, 1:2]
        for k, weight in enumerate((w_gate, w_up)):
            for t in range(nz * nc):
                for i in range(nx):
                    chunk = (i * nc + t % nc) * nz + t // nc
                    to = (k * nx + i) * span
                    piece = weight[at, chunk * span : (chunk + 1) * span].astype(F32) * gain
                    mlp_blocks[t // nc, t % nc, at, to : to + span] = piece.astype(BF)

    end = flow(None, first_rows, None, [spread, lambda: by_rows(own, pack_mlp)])
    end()
    mlp_swap.start()
    keep_rows = pltpu.make_async_copy(n1g, n1_out, local.at[5])
    keep_rows.start()
    tabs.arrived()
    for copy in spread_copies():
        copy.wait_recv()
    keep_weights = pltpu.make_async_copy(w_attn, w_out, local.at[6])
    keep_weights.start()

    def project_kv(i, carry):
        u = nn(n1g[i].reshape(nc * rows, width), w_attn[..., qcols : qcols + 128].reshape(width, 128))
        cos, sin = rope_lanes(tab[i].reshape(nc * rows, 128))
        u = jnp.where(lanes(u.shape) < 64, u * cos + swap_halves(u) * sin, u).astype(BF)
        for pc in range(nc):
            kv[pc, i, y] = u[pc * rows : (pc + 1) * rows]
        return carry

    def project_q(i, carry):
        res = nn(n1g[i].reshape(nc * rows, width), w_attn[..., :qcols].reshape(width, qcols))
        cos, sin = rope_lanes(tab[i].reshape(nc * rows, 128))
        for p in range(pairs):
            u = res[:, p * 128 : p * 128 + 128]
            u = (u * cos + swap_halves(u) * sin) * (HEAD_DIM ** (-0.5))
            q[i, :, :, p * 128 : p * 128 + 128] = u.astype(BF).reshape(nc, rows, 128)
        return carry

    lax.fori_loop(0, nz, project_kv, 0)
    sends = []
    for i in range(ny - 1):
        slot = kv.at[:, :, y]
        sends.append(remote(slot, slot, ys.at[i], yr.at[i], {"y": lax.rem(y + 1 + i, ny)}))
    for copy in sends:
        copy.start()
    lax.fori_loop(0, nz, project_q, 0)
    for copy in sends:
        copy.wait_recv()

    def double(i, carry):
        pc, pz = i // nz, lax.rem(i, nz)
        u = kv[pc, pz].reshape(keys_span, 128).astype(F32)
        r = pltpu.roll(u, 64, 1)
        first = lanes(u.shape) < 64
        at = pl.ds(pl.multiple_of(pz * keys_span, keys_span), keys_span)
        kk[pc, at, :] = jnp.where(first, u, r).astype(BF)
        values = jnp.where(first, r, u)
        vv[pc, at, :] = values.astype(BF)
        vt[pc, :, at] = values.T.astype(BF)
        return carry

    lax.fori_loop(0, nc * nz, double, 0)

    def attend(pc, carry):
        for pz in range(nz):
            keys = (pz + 1) * keys_span
            bias = bias_of(tab[pz, pc], keys, (pz * ny + y) * rows)
            for p in range(pairs):
                q2 = two_heads(q[pz, pc, :, p * 128 : p * 128 + 128])
                s = nt(kk[pc, :keys, :], q2) + bias
                top = jnp.max(s, axis=0, keepdims=True)
                e = jnp.exp(s - top)
                total = jnp.sum(e, axis=0, keepdims=True)
                stat[pz, pc, p : p + 1, :] = top + jnp.log(total)
                weights = (e * (1.0 / total)).astype(BF)
                o = join_heads(nn(vt[pc, :, :keys], weights))
                ob[pz, pc, :, p * 128 : p * 128 + 128] = o.astype(BF)
        return carry

    lax.fori_loop(0, nc, attend, 0)

    def output(i, carry):
        half, odd = i // 2, lax.rem(i, 2)
        pz = odd * half + (1 - odd) * (nz - 1 - half)
        for px in range(nx):
            cols = slice(px * (width // nx), (px + 1) * (width // nx))
            weights = w_attn[px, :, :, :, :, qcols + 128 :].reshape(width // nx, qcols)
            res = nt(ob[pz].reshape(nc * rows, qcols), weights)
            part[pz, :, :, cols] = res.astype(BF).reshape(nc, rows, width // nx)
        reduce.across(pz).start()
        return carry

    lax.fori_loop(0, nz, output, 0)

    def spread_mlp():
        mlp_swap.arrived()
        gu.start()

    end2 = flow(reduce, cots, None, [spread_mlp])

    def settle(at, total):
        value = tokens[at, :].astype(F32) + total
        mid[at, :] = value
        inverse = lax.rsqrt(jnp.mean(value * value, axis=-1, keepdims=True) + EPSILON)
        n2[at, :] = (value * inverse).astype(BF)

    end3 = flow(None, next_rows, lambda half: reduce.last(half, settle))
    end3()
    end2()
    keep_rows.wait()
    keep_weights.wait()
    gu.arrived()
    dn.arrived()
    for one in (swap, tabs, mlp_swap, gu, dn):
        one.finish()
    for copy in list(spread_copies()) + sends:
        copy.wait_send()


def forward_call(dims, tokens, table, gains, w_query, w_key, w_value, w_out_t, w_gate, w_up, down, cot):
    nx, nc, nz, ny = dims
    rows, width = tokens.shape
    own = w_query.shape[0]
    qcols = HEADS // (nz * nc) * HEAD_DIM
    cols = 2 * qcols + 128
    peers, members = nx * ny - 1, nz * nc - 1
    mlp_cols = 2 * w_gate.shape[1] // (nz * nc)
    keys = nz * ny * rows
    team_rows = (nz, nc, rows, width)
    return call(
        functools.partial(forward_kernel, dims),
        (tokens, table, gains, w_query, w_key, w_value, w_out_t, w_gate, w_up, down, cot),
        (VM,) * 9 + (pl.ANY, VM),
        [
            (team_rows, BF),
            ((nx, nc, nz, ny, own, cols), BF),
            ((nz, nc) + table.shape, F32),
            ((nz, nc, rows, qcols), BF),
            ((nc, keys, 128), BF),
            ((nc, keys, 128), BF),
            ((nz, nc, 8, 2 * rows), F32),
            ((nz, nc, rows, qcols), BF),
            ((rows, width), F32),
            (team_rows, BF),
            (team_rows, BF),
            ((nx, nc, nz, ny, own, mlp_cols), BF),
            ((nx, ny) + down.shape, BF),
        ],
        (pl.ANY,) * 2 + (VM,) * 7 + (pl.ANY,) * 4,
        [
            VM(team_rows, BF),
            VM((nx, nc, nz, ny, own, cols), BF),
            VM((rows, width), BF),
            VM((nz, nc, own, cols), BF),
            VM((nz, nc, own, mlp_cols), BF),
            VM((nc, nz, own, mlp_cols), BF),
            VM((nc, nz, ny, rows, 128), BF),
            VM((nc, 128, keys), BF),
            VM(team_rows, BF),
        ]
        + Reduce.buffers(nz, rows, width)
        + [VM((rows, width), BF)]
        + Gather.SEMS
        + [DMA((members,))] * 4
        + [DMA((peers,))] * 4
        + [DMA((members,))] * 2
        + [DMA((max(ny - 1, 1),))] * 2
        + Reduce.SEMS
        + Gather.SEMS * 2
        + [DMA((peers,))] * 2
        + [DMA((7,))],
        1,
    )


def mlp_kernel(
    dims, n2g, cotg, w_mlp, w_dn, mid, cot,
    dx2, dag, output, came_mlp, grad_dn,
    n2v, cotv, wv, wd, hid, hid_t, dmlp, part, mlp_out, grad_mlp,
    held, came, held2, came2, low,
    loads, rs, rr, rxs, rxr, os, orr, oxs, oxr, ds, dr, dl, ms, mr, local,
):
    nx, nc, nz, ny = dims
    x, c, z, y = place()
    rows, width = mid.shape
    ff2 = wv.shape[-1]
    ff = ff2 // 2
    piece = wd.shape[2]
    block = nc * rows
    fetch_w = pltpu.make_async_copy(w_mlp, wv, loads.at[0])
    fetch_d = pltpu.make_async_copy(w_dn, wd, loads.at[1])
    fetch_w.start()

    def fetch(at, k):
        source, target = ((n2g, n2v), (cotg, cotv))[k]
        return pltpu.make_async_copy(source.at[at], target.at[at], loads.at[2 + k * nz + at])

    for k in range(nz):
        fetch(by_need(nz, z, k), 0).start()
        if k == 0:
            fetch_d.start()
        fetch(by_need(nz, z, k), 1).start()
    met = greet(*dims)
    reduce = Reduce(part, held, came, rs, rr, rxs, rxr)
    reduce2 = Reduce(mlp_out, held2, came2, os, orr, oxs, oxr)
    into = Gather(low, dag, ds, dr, dl)
    gu = Spread(
        lambda px, py: grad_mlp.at[px, :, :, py], lambda px, py: came_mlp.at[px, py], ms, mr, local.at[0], nx, ny
    )

    def down_rows(cols):
        if piece % ROWS:
            return jnp.concatenate([wd[px, py, :, cols] for px in range(nx) for py in range(ny)], axis=0)
        return wd[:, :, :, cols].reshape(ff, -1)

    def weights(px):
        return wv[px].reshape(width // nx, ff2)

    fetch_w.wait()

    def forward_back(k):
        at = by_need(nz, z, k)
        fetch(at, 0).wait()
        u = nn(n2v[at].reshape(block, width), wv[...].reshape(width, ff2))
        gt, up = u[:, :ff], u[:, ff:]
        sg = jax.nn.sigmoid(gt)
        silu = gt * sg
        value = (silu * up).astype(BF)
        hid[at] = value
        hid_t[:, pl.ds(pl.multiple_of(at * block, block), block)] = value.astype(F32).T.astype(BF)
        if k == 0:
            fetch_d.wait()
        fetch(at, 1).wait()
        dh = nt(cotv[at].reshape(block, width), down_rows(slice(None)))
        dgt = dh * up * sg * (1.0 + gt * (1.0 - sg))
        dmlp[at] = jnp.concatenate([dgt, dh * silu], axis=1).astype(BF)

        for px in range(nx):
            cols = slice(px * (width // nx), (px + 1) * (width // nx))
            res = nt(dmlp[at], weights(px))
            part[at, :, :, cols] = res.astype(BF).reshape(nc, rows, width // nx)
        if k == 0:
            met()
        reduce.across(at).start()

    forward_back(0)
    chunk = width // 4

    def down_grad(n, carry):
        cols = pl.ds(pl.multiple_of(n * chunk, chunk), chunk)
        res = nn(hid_t[...], cotv[:, :, :, cols].reshape(nz * block, chunk)).astype(BF)
        for px in range(nx):
            for py in range(ny):
                k = (px * ny + py) * piece
                grad_dn[px, py, :, cols] = res[k : k + piece]
        return carry

    def mlp_grad(far):
        px = lax.rem(x + far, nx)
        size = width // (nx * 4)

        def body(j, carry):
            cols = pl.ds(pl.multiple_of(px * (width // nx) + j * size, size), size)
            res = tn(n2v[:, :, :, cols].reshape(nz * block, size), dmlp[...].reshape(nz * block, ff2))
            own = grad_mlp.shape[4]
            grad_mlp[px, j // 2, pl.ds(lax.rem(j, 2) * (nz // 2), nz // 2)] = res.astype(BF).reshape(
                nz // 2, ny, own, ff2
            )
            return carry

        lax.fori_loop(0, 4, body, 0)
        gu.start_along(far)

    def mlp_sum(n, carry):
        cols = pl.ds(pl.multiple_of(n * chunk, chunk), chunk)
        res = nn(hid[...].reshape(nz * block, ff), down_rows(cols))
        mlp_out[:, :, :, cols] = res.astype(BF).reshape(nz, nc, rows, chunk)
        return carry

    def down_first():
        lax.fori_loop(0, 2, down_grad, 0)

    def down_second():
        lax.fori_loop(2, 4, down_grad, 0)

    def sum_all():
        lax.fori_loop(0, 4, mlp_sum, 0)
        reduce2.start()

    work = [functools.partial(forward_back, k) for k in range(1, nz)]
    work += [functools.partial(mlp_grad, far) for far in reversed(range(nx))]
    end = flow(reduce, None, None, work + [sum_all])

    def settle(at, total):
        value = mid[at, :]
        inverse = lax.rsqrt(jnp.mean(value * value, axis=-1, keepdims=True) + EPSILON)
        normed = value * inverse
        gradient = cot[at, :].astype(F32) + inverse * (
            total - normed * jnp.mean(total * normed, axis=-1, keepdims=True)
        )
        dx2[at, :] = gradient
        low[at, :] = gradient.astype(BF)

    end2 = flow(reduce2, into, lambda part: reduce.last(part, settle), [down_first, down_second])

    def finish(at, total):
        output[at, :] = (mid[at, :] + total).astype(BF)

    for half in range(PARTS):
        reduce2.last(half, finish)
    end2()
    end()
    gu.arrived()
    gu.finish()


def mlp_call(dims, n2g, cotg, w_mlp, w_dn, mid, cot):
    nx, nc, nz, ny = dims
    rows, width = mid.shape
    own, ff2 = w_mlp.shape[4:]
    block = nc * rows
    peers = nx * ny - 1
    return call(
        functools.partial(mlp_kernel, dims),
        (n2g, cotg, w_mlp, w_dn, mid, cot),
        (pl.ANY, pl.ANY, pl.ANY, pl.ANY, VM, VM),
        [
            ((rows, width), F32),
            ((nz, nc, rows, width), BF),
            ((rows, width), BF),
            ((nx, ny, nc, nz, own, ff2), BF),
            (w_dn.shape, BF),
        ],
        (VM, pl.ANY, VM, pl.ANY, VM),
        [
            VM(n2g.shape, BF),
            VM(cotg.shape, BF),
            VM(w_mlp.shape, BF),
            VM(w_dn.shape, BF),
            VM((nz, block, ff2 // 2), BF),
            VM((ff2 // 2, nz * block), BF),
            VM((nz, block, ff2), BF),
            VM(n2g.shape, BF),
            VM(n2g.shape, BF),
            VM(w_mlp.shape, BF),
        ]
        + Reduce.buffers(nz, rows, width) * 2
        + [VM((rows, width), BF), DMA((2 + 2 * nz,))]
        + Reduce.SEMS * 2
        + Gather.SEMS
        + [DMA((peers,))] * 2
        + [DMA((1,))],
        3,
    )


def backward_kernel(
    dims, dag, w, tab, q, kk, vv, stat, ob, came_mlp, grad_dn, n1g,
    dn1, raw_gate, raw_up, came_dn, own_o, own_p,
    do, kt, dk, dv, out, near, dqkv, part, team, stage, mlp_sum, mlp_g,
    grad_o, came_o, sums_o, grad_p, came_p, sums_p,
    held, came,
    loads, us, ur, ys, yr, ws, wr, rs, rr, rxs, rxr, ds, dr, ss, sr, es, er, fs, fr, local,
):
    nx, nc, nz, ny = dims
    x, c, z, y = place()
    rows, width = dn1.shape
    own = grad_o.shape[4]
    qcols = q.shape[-1]
    pairs = qcols // 128
    keys_span = ny * rows
    fetch_dag = pltpu.make_async_copy(dag, team, loads.at[2])
    fetch = pltpu.make_async_copy(n1g, team, loads.at[2])
    fetch_dag.start()
    mlp_swap = Swap(
        lambda pz, pc: mlp_sum.at[pz, pc], lambda pz, pc: mlp_g.at[pz, pc], us, ur, local.at[0], nz, nc
    )
    dn = Spread(lambda px, py: grad_dn.at[px, py], lambda px, py: came_dn.at[px, py], ws, wr, local.at[1], nx, ny)
    reduce = Reduce(part, held, came, rs, rr, rxs, rxr)
    spread_o = Spread(
        lambda px, py: grad_o.at[px, :, :, py], lambda px, py: came_o.at[px, py], ds, dr, local.at[2], nx, ny
    )
    swap_o = Swap(lambda pz, pc: sums_o.at[pz, pc], lambda pz, pc: own_o.at[pz, pc], ss, sr, local.at[3], nz, nc)
    spread_p = Spread(
        lambda px, py: grad_p.at[px, :, :, py], lambda px, py: came_p.at[px, py], es, er, local.at[4], nx, ny
    )
    swap_p = Swap(lambda pz, pc: sums_p.at[pz, pc], lambda pz, pc: own_p.at[pz, pc], fs, fr, local.at[5], nz, nc)

    steps = others(nz, nc) + [(0, 0)]

    def load(i):
        pz, pc = team_peer(steps[i], nz, nc)
        return pltpu.make_async_copy(came_mlp.at[:, :, pc, pz], stage.at[i % 2], loads.at[i % 2])

    load(0).start()
    met = greet(*dims, cross=True)

    def turned(i, carry):
        pc, pz = i // nz, lax.rem(i, nz)
        at = pl.ds(pl.multiple_of(pz * keys_span, keys_span), keys_span)
        kt[pc, :, at] = kk[pc, at, :].astype(F32).T.astype(BF)
        return carry

    lax.fori_loop(0, nc * nz, turned, 0)
    early = 2 * (nx * ny - 1) // 3
    for i, copy in enumerate(list(mlp_swap.copies()) + [mlp_swap.own()]):
        if i + 1 < len(steps):
            load(i + 1).start()
        load(i).wait()
        pz, pc = team_peer(steps[i], nz, nc)

        def add(at, i=i, pz=pz, pc=pc):
            total = stage[i % 2, 0, 0, at, :].astype(F32)
            for px, py in others(nx, ny):
                total = total + stage[i % 2, px, py, at, :].astype(F32)
            mlp_sum[pz, pc, at, :] = total.astype(BF)

        by_rows(own, add)
        if i == 0:
            met()
            dn.start_some(0, early)
            dn.own().start()
        copy.start()
    fetch_dag.wait()

    def project(i, carry):
        weights = w[..., qcols + 128 :].reshape(width, qcols)
        do[i] = nn(team[i].reshape(nc * rows, width), weights).astype(BF).reshape(nc, rows, qcols)
        return carry

    lax.fori_loop(0, nz, project, 0)

    def attend(pc, carry):
        for pz in reversed(range(nz)):
            keys = (pz + 1) * keys_span
            most = KEYS if nz * keys_span <= KEYS else KEYS // 4
            cuts = [slice(a, min(a + most, keys)) for a in range(0, keys, most)]

            def bias_at(i, cuts=cuts, pz=pz):
                cut = cuts[i]
                return bias_of(tab[pz, pc], cut.stop - cut.start, (pz * ny + y) * rows, cut.start)

            only = bias_at(0) if len(cuts) == 1 else None
            cos, sin = rope_lanes(tab[pz, pc])
            for p in range(pairs):
                q2 = two_heads(q[pz, pc, :, p * 128 : p * 128 + 128])
                do2 = two_heads(do[pz, pc, :, p * 128 : p * 128 + 128])

                def scores(i, cuts=cuts, only=only, bias_at=bias_at, q2=q2, do2=do2, p=p, pz=pz):
                    s = nt(kk[pc, cuts[i], :], q2) + (bias_at(i) if only is None else only)
                    weights = jnp.exp(s - stat[pz, pc, p : p + 1, :])
                    return weights, weights * nt(vv[pc, cuts[i], :], do2)

                delta = sum(jnp.sum(scores(i)[1], axis=0, keepdims=True) for i in range(1, len(cuts)))
                u = 0.0
                for i, cut in enumerate(cuts):
                    weights, dw = scores(i)
                    if i == 0:
                        delta = delta + jnp.sum(dw, axis=0, keepdims=True)
                    score_grad = (dw - weights * delta).astype(BF)
                    dv_new = nn(weights.astype(BF), do2)
                    dk_new = nn(score_grad, q2)
                    if pz == nz - 1 and p == 0:
                        dv[pc, cut, :] = dv_new
                        dk[pc, cut, :] = dk_new
                    else:
                        dv[pc, cut, :] += dv_new
                        dk[pc, cut, :] += dk_new
                    u = u + nn(kt[pc, :, cut], score_grad)
                u = join_heads(u) * (HEAD_DIM ** (-0.5))
                u = u * cos - swap_halves(u) * sin
                dqkv[pz, pc, :, p * 128 : p * 128 + 128] = u.astype(BF)
        return carry

    lax.fori_loop(0, nc, attend, 0)

    def fold(i, carry):
        pc, pz = i // nz, lax.rem(i, nz)
        at = pl.ds(pl.multiple_of(pz * keys_span, keys_span), keys_span)
        key, value = dk[pc, at, :], dv[pc, at, :]
        first = lanes(key.shape) < 64
        both = jnp.where(first, key + pltpu.roll(key, 64, 1), value + pltpu.roll(value, 64, 1))
        both = both.astype(BF)
        for py in range(ny):
            out[pc, py, pz] = both[py * rows : (py + 1) * rows]
        return carry

    lax.fori_loop(0, nc * nz, fold, 0)
    sends = []
    for i, (sy, sc) in enumerate(others(ny, nc)):
        py, pc = lax.rem(y + sy, ny), lax.rem(c + sc, nc)
        sends.append(remote(out.at[pc, py], near.at[i], ys.at[i], yr.at[i], {"y": py, "core": pc}))
    for copy in sends:
        copy.start()

    def weight_grad(right, target):
        def body(j, carry):
            px, k = j // 4, lax.rem(j, 4)
            size = width // (nx * 4)
            cols = pl.ds(pl.multiple_of(j * size, size), size)
            res = tn(team[:, :, :, cols].reshape(nz * nc * rows, size), right.reshape(nz * nc * rows, -1))
            target[px, k // 2, pl.ds(lax.rem(k, 2) * (nz // 2), nz // 2)] = res.astype(BF).reshape(
                nz // 2, ny, own, -1
            )
            return carry

        lax.fori_loop(0, nx * 4, body, 0)

    weight_grad(ob[...], grad_o)
    fetch.start()
    for copy in sends:
        copy.wait_recv()
    spread_o.start()

    def settle_kv(pz, carry):
        total = out[c, y, pz].astype(F32)
        for i in range(len(sends)):
            total = total + near[i, pz].astype(F32)
        cos, sin = rope_lanes(tab[pz, c])
        first = lanes(total.shape) < 64
        total = jnp.where(first, total * cos - swap_halves(total) * sin, total)
        dqkv[pz, c, :, qcols : qcols + 128] = total.astype(BF)
        dqkv[pz, 1 - c, :, qcols : qcols + 128] = jnp.zeros((rows, 128), BF)
        return carry

    lax.fori_loop(0, nz, settle_kv, 0)

    def output(i, carry):
        half, odd = i // 2, lax.rem(i, 2)
        pz = odd * half + (1 - odd) * (nz - 1 - half)
        for px in range(nx):
            cols = slice(px * (width // nx), (px + 1) * (width // nx))
            weights = w[px, :, :, :, :, : qcols + 128].reshape(width // nx, qcols + 128)
            res = nt(dqkv[pz].reshape(nc * rows, qcols + 128), weights)
            part[pz, :, :, cols] = res.astype(BF).reshape(nc, rows, width // nx)
        reduce.across(pz).start()
        return carry

    lax.fori_loop(0, nz, output, 0)

    def own_weights():
        fetch.wait()
        weight_grad(dqkv[...], grad_p)
        spread_p.start()

    def unpack_mlp(at):
        span = mlp_g.shape[-1] // (2 * nx)
        for k, raw in enumerate((raw_gate, raw_up)):
            for t in range(nz * nc):
                for i in range(nx):
                    chunk = (i * nc + t % nc) * nz + t // nc
                    piece = mlp_g[t // nc, t % nc, at, (k * nx + i) * span : (k * nx + i + 1) * span]
                    raw[at, chunk * span : (chunk + 1) * span] = piece

    def unpack_all():
        mlp_swap.arrived()
        by_rows(own, unpack_mlp)

    def down_rest():
        dn.start_some(early, nx * ny - 1)

    def exchange(spread, arrived, sums, swap):
        spread.arrived()

        def add(at):
            for pz in range(nz):
                for pc in range(nc):
                    total = arrived[0, 0, pc, pz, at, :].astype(F32)
                    for px, py in others(nx, ny):
                        total = total + arrived[px, py, pc, pz, at, :].astype(F32)
                    sums[pz, pc, at, :] = total.astype(BF)

        by_rows(own, add)
        swap.start()

    work = [
        own_weights,
        unpack_all,
        down_rest,
        functools.partial(exchange, spread_o, came_o, sums_o, swap_o),
        functools.partial(exchange, spread_p, came_p, sums_p, swap_p),
    ]
    end = flow(reduce, None, None, work)

    def settle(at, total):
        dn1[at, :] = total

    for half in range(PARTS):
        reduce.last(half, settle)
    end()
    for one in (dn, swap_o, swap_p):
        one.arrived()
    for one in (mlp_swap, dn, spread_o, swap_o, spread_p, swap_p):
        one.finish()
    for copy in sends:
        copy.wait_send()


def backward_call(dims, dag, w, tab, q, kk, vv, stat, ob, came_mlp, grad_dn, n1g):
    nx, nc, nz, ny = dims
    rows, width = dag.shape[2:]
    own, mlp_cols = came_mlp.shape[4:]
    qcols = q.shape[-1]
    keys = nz * ny * rows
    peers, members, near = nx * ny - 1, nz * nc - 1, ny * nc - 1
    team_rows = (nz, nc, rows, width)
    return call(
        functools.partial(backward_kernel, dims),
        (dag, w, tab, q, kk, vv, stat, ob, came_mlp, grad_dn, n1g),
        (pl.ANY,) + (VM,) * 7 + (pl.ANY,) * 3,
        [
            ((rows, width), F32),
            ((own, mlp_cols // 2 * nz * nc), BF),
            ((own, mlp_cols // 2 * nz * nc), BF),
            (grad_dn.shape, BF),
            ((nz, nc, own, qcols), BF),
            ((nz, nc, own, qcols + 128), BF),
        ],
        (VM,) * 3 + (pl.ANY,) * 3,
        [
            VM((nz, nc, rows, qcols), BF),
            VM((nc, 128, keys), BF),
            VM((nc, keys, 128), F32),
            VM((nc, keys, 128), F32),
            VM((nc, ny, nz, rows, 128), BF),
            VM((near, nz, rows, 128), BF),
            VM((nz, nc, rows, qcols + 128), BF),
            VM(team_rows, BF),
            VM(team_rows, BF),
            VM((2, nx, ny, own, mlp_cols), BF),
            VM((nz, nc, own, mlp_cols), BF),
            VM((nz, nc, own, mlp_cols), BF),
        ]
        + [
            VM(shape + (own, n), BF)
            for n in (qcols, qcols + 128)
            for shape in ((nx, nc, nz, ny), (nx, ny, nc, nz), (nz, nc))
        ]
        + Reduce.buffers(nz, rows, width)
        + [DMA((3,))]
        + [DMA((members,))] * 2
        + [DMA((near,))] * 2
        + [DMA((peers,))] * 2
        + Reduce.SEMS
        + ([DMA((peers,))] * 2 + [DMA((members,))] * 2) * 2
        + [DMA((6,))],
        6,
    )


def final_kernel(
    dims, dn1, tokens, dx2, raw_gate, raw_up, came_dn, own_o, own_p, gains, w_query, w_key, w_value, w_gate, w_up,
    input_grad, grad_query, grad_key, grad_value, grad_out_t, grad_gate, grad_up, grad_down, grad_gain,
):
    nx, nc, nz, ny = dims
    team = nz * nc
    value = tokens[...].astype(F32)
    total = dn1[...]
    inverse = lax.rsqrt(jnp.mean(value * value, axis=-1, keepdims=True) + EPSILON)
    normed = value * inverse
    input_grad[...] = dx2[...] + inverse * (total - normed * jnp.mean(total * normed, axis=-1, keepdims=True))

    down = came_dn[0, 0].astype(F32)
    for px, py in others(nx, ny):
        down = down + came_dn[px, py].astype(F32)
    grad_down[...] = down

    gain = gains[:, 1:2]
    both = 0.0
    for raw, weight, grad in ((raw_gate, w_gate, grad_gate), (raw_up, w_up, grad_up)):
        got = raw[...].astype(F32)
        grad[...] = got * gain
        both = both + got * weight[...].astype(F32)
    dots_mlp = jnp.sum(both, axis=-1, keepdims=True)

    gain = gains[:, 0:1]
    qcols = own_o.shape[-1]
    both = 0.0
    heads = []
    for t in range(team):
        block = own_p[t // nc, t % nc].astype(F32)
        cols = slice(t * qcols, (t + 1) * qcols)
        grad_out_t[:, cols] = own_o[t // nc, t % nc].astype(F32)
        grad_query[:, cols] = block[:, :qcols] * gain
        both = both + block[:, :qcols] * w_query[:, cols].astype(F32)
        if t % (team // KV_HEADS):
            heads[-1] = heads[-1] + block[:, qcols:]
        else:
            heads.append(block[:, qcols:])
    dots = jnp.sum(both, axis=-1, keepdims=True)
    for pair in range(KV_HEADS // 2):
        one, two = heads[2 * pair], heads[2 * pair + 1]
        first = lanes(one.shape) < 64
        cols = slice(pair * 128, pair * 128 + 128)
        key = jnp.where(first, one, pltpu.roll(two, 64, 1))
        val = jnp.where(first, pltpu.roll(one, 64, 1), two)
        grad_key[:, cols] = key * gain
        grad_value[:, cols] = val * gain
        both = key * w_key[:, cols].astype(F32) + val * w_value[:, cols].astype(F32)
        dots = dots + jnp.sum(both, axis=-1, keepdims=True)
    shape = grad_gain.shape
    grad_gain[...] = jnp.where(lanes(shape) < 64, dots, dots_mlp)


def final_call(
    dims, dn1, tokens, dx2, raw_gate, raw_up, came_dn, own_o, own_p, gains, w_query, w_key, w_value, w_gate, w_up
):
    own = w_query.shape[0]
    steps = max(own // ROWS, 1)

    def rows_of(shape, axis):
        count = shape[axis]
        each = count if steps == 1 else -(-count // (steps * ROWS)) * ROWS
        block = shape[:axis] + (each,) + shape[axis + 1 :]
        return pl.BlockSpec(block, lambda i: tuple(i if k == axis else 0 for k in range(len(shape))))

    operands = (
        dn1, tokens, dx2, raw_gate, raw_up, came_dn, own_o, own_p, gains, w_query, w_key, w_value, w_gate, w_up
    )
    outs = [
        dn1.shape, w_query.shape, w_key.shape, w_value.shape, w_query.shape, w_gate.shape, w_up.shape,
        came_dn.shape[2:], (own, 128),
    ]
    return pl.pallas_call(
        functools.partial(final_kernel, dims),
        grid=(steps,),
        out_shape=[jax.ShapeDtypeStruct(s, F32) for s in outs],
        in_specs=[rows_of(a.shape, len(a.shape) - 2) for a in operands],
        out_specs=[rows_of(s, 0) for s in outs],
        compiler_params=pltpu.CompilerParams(vmem_limit_bytes=60 << 20),
    )(*operands)


def shards(
    tokens, positions, doc_start, cotangent, w_query, w_key, w_value, w_out,
    attn_gain, w_gate, w_up, w_down, mlp_gain,
):
    dims = tuple(lax.axis_size(a) for a in ALL)
    rows = tokens.shape[0]

    gains = jnp.stack([attn_gain, mlp_gain], axis=1).astype(F32)
    half = HEAD_DIM // 2
    frequency = 10000.0 ** (-2.0 * jnp.arange(half, dtype=F32) / HEAD_DIM)
    angles = positions.astype(F32)[:, None] * frequency[None, :]
    table = jnp.concatenate(
        [
            jnp.cos(angles),
            jnp.sin(angles),
            jnp.broadcast_to(doc_start.astype(F32)[:, None], (rows, HEAD_DIM)),
        ],
        axis=-1,
    )
    n1g, w_attn, tab, q, kk, vv, stat, ob, mid, n2g, cotg, w_mlp, w_dn = forward_call(
        dims, tokens, table, gains, w_query, w_key, w_value, w_out.T, w_gate, w_up, w_down, cotangent
    )
    dx2, dag, output, came_mlp, grad_dn = mlp_call(dims, n2g, cotg, w_mlp, w_dn, mid, cotangent)
    dn1, raw_gate, raw_up, came_dn, own_o, own_p = backward_call(
        dims, dag, w_attn, tab, q, kk, vv, stat, ob, came_mlp, grad_dn, n1g
    )
    (
        input_grad, grad_query, grad_key, grad_value, grad_out_t, grad_gate, grad_up, grad_down, grad_gain
    ) = final_call(
        dims, dn1, tokens, dx2, raw_gate, raw_up, came_dn, own_o, own_p, gains,
        w_query, w_key, w_value, w_gate, w_up,
    )
    return (
        output, input_grad, grad_query, grad_key, grad_value, grad_out_t.T, grad_gain[:, 0],
        grad_gate, grad_up, grad_down, grad_gain[:, 64],
    )


def solution(mesh):
    fsdp, seq = mesh.shape["fsdp"], mesh.shape["seq"]
    nc, nz = 2, 4
    grid = Mesh(mesh.devices.reshape(fsdp // nc, nc, nz, seq // nz), ALL)
    row, col, vec = P(ALL, None), P(None, ALL), P(ALL)
    in_specs = (row, vec, vec, row, row, row, row, col, vec, row, row, row, vec)
    out_specs = (row, row, row, row, row, col, vec, row, row, row, vec)
    return jax.shard_map(shards, mesh=grid, in_specs=in_specs, out_specs=out_specs, check_vma=False)
```

```python
import functools

import jax
import jax.numpy as jnp
import numpy as np
from jax import lax
from jax.experimental import pallas as pl
from jax.experimental.pallas import tpu as pltpu
from jax.sharding import Mesh
from jax.sharding import PartitionSpec as P

HEADS = 32
KV_HEADS = 4
HEAD_DIM = 64
EPSILON = 1e-05
MASKED = -1e30
ALL = ("x", "core", "z", "y")
TEAM = ("z", "core")
DATA = ("x", "y")
BF = jnp.bfloat16
F32 = jnp.float32


MESH = pl.DeviceIdType.MESH
VM = pltpu.VMEM
DMA = pltpu.SemaphoreType.DMA
ROWS = 16
PARTS = 2
WINDOW = 2
KEYS = 1024


def place():
    return tuple(lax.axis_index(a) for a in ALL)


def others(nx, ny):
    return [(i, j) for i in range(nx) for j in range(ny) if (i, j) != (0, 0)]


def data_peer(step, nx, ny):
    x, _, _, y = place()
    return lax.rem(x + step[0], nx), lax.rem(y + step[1], ny)


def team_peer(step, nz, nc):
    _, c, z, _ = place()
    return lax.rem(z + step[0], nz), lax.rem(c + step[1], nc)


def greet(nx, nc, nz, ny, cross=False):
    barrier = pltpu.get_barrier_semaphore()
    x, c, z, y = place()
    extra = ny - 1 if cross else 0
    for i in range(extra):
        device = {"y": lax.rem(y + 1 + i, ny), "core": 1 - c}
        pl.semaphore_signal(barrier, inc=1, device_id=device, device_id_type=MESH)
    for step in others(nx, ny):
        px, py = data_peer(step, nx, ny)
        pl.semaphore_signal(barrier, inc=1, device_id={"x": px, "y": py}, device_id_type=MESH)
    for step in others(nz, nc):
        pz, pc = team_peer(step, nz, nc)
        pl.semaphore_signal(barrier, inc=1, device_id={"z": pz, "core": pc}, device_id_type=MESH)

    def met():
        pl.semaphore_wait(barrier, nx * ny - 1 + nz * nc - 1 + extra)

    return met


def remote(source, target, send, recv, device):
    return pltpu.make_async_remote_copy(
        src_ref=source, dst_ref=target, send_sem=send, recv_sem=recv,
        device_id=device, device_id_type=MESH,
    )


def piece_of(part, rows):
    return pl.ds(part * (rows // PARTS), rows // PARTS)


class Gather:
    SEMS = [DMA((3, 4, PARTS)), DMA((2, 4, PARTS)), DMA((PARTS,))]

    def __init__(self, own, full, send, recv, local):
        self.own, self.full, self.send, self.recv, self.local = own, full, send, recv, local
        self.x, self.c, self.z, self.y = place()
        self.nz, _, self.rows = full.shape[:3]

    def copy(self, at, kind, part, mine=False):
        rows = piece_of(part, self.rows)
        slot = self.full.at[at, self.c, rows]
        device = ({"z": self.z + 1}, {"z": self.z - 1}, {"core": 1 - self.c})[kind]
        return remote(
            self.own.at[rows] if mine else slot, slot, self.send.at[kind, at, part],
            self.recv.at[0 if kind < 2 else 1, at, part], device,
        )

    def keep(self, part):
        rows = piece_of(part, self.rows)
        return pltpu.make_async_copy(self.own.at[rows], self.full.at[self.z, self.c, rows], self.local.at[part])

    def begin(self, part):
        self.keep(part).start()
        self.copy(self.z, 2, part, True).start()

    def finish(self):
        for part in range(PARTS):
            self.keep(part).wait()
            for at in range(self.nz):
                self.copy(at, 2, part).wait_send()
                self.copy(at, 2, part).wait_recv()


class Reduce:
    SEMS = [DMA((2, 4, PARTS)), DMA((2, 4, PARTS)), DMA((4,)), DMA((4,))]

    @staticmethod
    def buffers(nz, rows, width):
        return [VM((nz, rows, width), BF), VM((2, nz - 1, rows, width), BF)]

    def __init__(self, part, held, came, send, recv, across_send, across_recv):
        self.part, self.held, self.came, self.send, self.recv = part, held, came, send, recv
        self.across_send, self.across_recv = across_send, across_recv
        self.x, self.c, self.z, self.y = place()
        self.nz, _, self.rows, self.width = part.shape

    def across(self, to):
        return remote(
            self.part.at[to, 1 - self.c], self.held.at[to], self.across_send.at[to], self.across_recv.at[to],
            {"core": 1 - self.c},
        )

    def along(self, to, way, part):
        device = ({"z": self.z + 1}, {"z": self.z - 1})[way]
        rows = piece_of(part, self.rows)
        return remote(
            self.held.at[to, rows], self.came.at[way, to - 1 + way, rows], self.send.at[way, to, part],
            self.recv.at[way, to, part], device,
        )

    def start(self):
        for to in [a for k in range(self.nz) for a in (self.nz - 1 - k, k)][: self.nz]:
            self.across(to).start()

    def add(self, to, ways, part, out=None):
        size = self.rows // PARTS

        def body(i, carry):
            at = pl.ds(pl.multiple_of(part * size + i * ROWS, ROWS), ROWS)
            total = self.part[to, self.c, at, :].astype(F32) + self.held[to, at, :].astype(F32)
            for way in ways:
                total = total + self.came[way, to - 1 + way, at, :].astype(F32)
            if out is None:
                self.held[to, at, :] = total.astype(BF)
            else:
                out(at, total)
            return carry

        lax.fori_loop(0, size // ROWS, body, 0)

    def last(self, part, out):
        if part == 0:
            self.across(self.z).wait_recv()
        for at in range(self.nz):

            @pl.when(self.z == at)
            def _(at=at):
                ways = ([0] if at > 0 else []) + ([1] if at < self.nz - 1 else [])
                for way in ways:
                    self.along(at, way, part).wait_recv()
                self.add(at, ways, part, out)

    def finish(self):
        for to in range(self.nz):
            self.across(to).wait_send()


def plan(nz, reduces, gathers):
    last = nz - 1
    rows = []
    for e in range(nz):
        sums = [("R", last - k) for k in range(last) if last - k > e]
        blocks = [("G", e - k) for k in range(e + 1)]
        if reduces and gathers:
            if e == last:
                rows.append([None] + blocks[1:-1] + [None] + blocks[-1:])
            else:
                woven = blocks[:-1] + sums[:1] + blocks[-1:] + sums[1:]
                rows.append(woven)
        elif reduces:
            rows.append([None] * e + sums)
        else:
            rows.append(blocks if e < last else [None] + blocks[1:])
    return rows


def by_need(nz, z, k):
    last = nz - 1
    value = 0
    for at in range(nz):
        when = {to: at + last - to if to > at else last - at + to for to in range(nz) if to != at}
        blocks = sorted(when, key=lambda to: (when[to], to)) + [at]
        value = jnp.where(z == at, blocks[k], value)
    return value


def flow(reduce, gather, before=None, work=()):
    work = list(work)
    any_one = reduce or gather
    nz, z = any_one.nz, any_one.z
    table = plan(nz, reduce is not None, gather is not None)
    pending = {(way, e): [] for way in (0, 1) for e in range(nz)}

    def pace(key, make):
        queue = pending[key]
        if len(queue) >= WINDOW:
            queue.pop(0)().wait_send()
        make().start()
        queue.append(make)

    def step(way, e, kind, place_at, part):
        block = place_at if way == 0 else nz - 1 - place_at
        if kind == "R":
            if part == 0:
                reduce.across(block).wait_recv()
            if e > 0:
                reduce.along(block, way, part).wait_recv()
            reduce.add(block, (way,) if e > 0 else (), part)
            pace((way, e), functools.partial(reduce.along, block, way, part))
        else:
            mine = place_at == e
            if not mine:
                gather.copy(block, way, part).wait_recv()
            if e < nz - 1:
                pace((way, e), functools.partial(gather.copy, block, way, part, mine))
            if not mine:
                gather.copy(block, 2, part).start()

    for t in range(max(len(row) for row in table)):
        for part in range(PARTS):
            if t == 0 and before is not None:
                before(part)
            if t == 0 and gather is not None:
                gather.begin(part)
            for way in (0, 1):
                for e in range(nz):
                    op = table[e][t] if t < len(table[e]) else None
                    if op is not None:
                        pl.when(z == (e if way == 0 else nz - 1 - e))(
                            functools.partial(step, way, e, op[0], op[1], part)
                        )
            if work and (t > 0 or part == PARTS - 1):
                work.pop(0)()
    for item in work:
        item()

    def finish():
        for (way, e), queue in pending.items():
            if queue:

                @pl.when(z == (e if way == 0 else nz - 1 - e))
                def _(queue=queue):
                    for make in queue:
                        make().wait_send()

        for one in (reduce, gather):
            if one is not None:
                one.finish()

    return finish


class Spread:
    def __init__(self, source, target, send, recv, local, nx, ny):
        self.source, self.target, self.send, self.recv = source, target, send, recv
        self.nx, self.ny = nx, ny
        self.x, _, _, self.y = place()
        self.own = lambda: pltpu.make_async_copy(source(self.x, self.y), target(self.x, self.y), local)

    def copies(self):
        for i, step in enumerate(others(self.nx, self.ny)):
            px, py = data_peer(step, self.nx, self.ny)
            yield remote(
                self.source(px, py), self.target(self.x, self.y), self.send.at[i], self.recv.at[i],
                {"x": px, "y": py},
            )

    def start(self):
        for copy in self.copies():
            copy.start()
        self.own().start()

    def start_some(self, first, last):
        for i, copy in enumerate(self.copies()):
            if first <= i < last:
                copy.start()

    def start_along(self, far):
        for step, copy in zip(others(self.nx, self.ny), self.copies()):
            if step[0] == far:
                copy.start()
        if far == 0:
            self.own().start()

    def arrived(self):
        self.own().wait()
        for copy in self.copies():
            copy.wait_recv()

    def finish(self):
        for copy in self.copies():
            copy.wait_send()


class Swap:
    def __init__(self, source, slot, send, recv, local, nz, nc):
        self.source, self.slot, self.send, self.recv, self.nz, self.nc = source, slot, send, recv, nz, nc
        _, self.c, self.z, _ = place()
        self.own = lambda: pltpu.make_async_copy(source(self.z, self.c), slot(self.z, self.c), local)

    def copies(self):
        for i, step in enumerate(others(self.nz, self.nc)):
            pz, pc = team_peer(step, self.nz, self.nc)
            yield remote(
                self.source(pz, pc), self.slot(self.z, self.c), self.send.at[i], self.recv.at[i],
                {"z": pz, "core": pc},
            )

    def start(self):
        for copy in self.copies():
            copy.start()
        self.own().start()

    def arrived(self):
        self.own().wait()
        for copy in self.copies():
            copy.wait_recv()

    def finish(self):
        for copy in self.copies():
            copy.wait_send()


def call(kernel, operands, in_spaces, outs, out_spaces, scratch, number):
    return pl.pallas_call(
        kernel,
        out_shape=[jax.ShapeDtypeStruct(s, t) for s, t in outs],
        in_specs=[pl.BlockSpec(memory_space=s) for s in in_spaces],
        out_specs=[pl.BlockSpec(memory_space=s) for s in out_spaces],
        scratch_shapes=scratch,
        compiler_params=pltpu.CompilerParams(
            collective_id=number, has_side_effects=True, vmem_limit_bytes=60 << 20
        ),
    )(*operands)


def lanes(shape):
    return lax.broadcasted_iota(jnp.int32, shape, len(shape) - 1)


def by_rows(count, body):
    if count % ROWS or count == ROWS:
        body(slice(0, count))
    else:

        def step(i, carry):
            body(pl.ds(pl.multiple_of(i * ROWS, ROWS), ROWS))
            return carry

        lax.fori_loop(0, count // ROWS, step, 0)


def nt(a, b):
    return lax.dot_general(a, b, (((1,), (1,)), ((), ())), preferred_element_type=F32)


def nn(a, b):
    return jnp.dot(a, b, preferred_element_type=F32)


def tn(a, b):
    return lax.dot_general(a, b, (((0,), (0,)), ((), ())), preferred_element_type=F32)


def column(row):
    count = row.shape[1]
    down = lax.broadcasted_iota(jnp.int32, (count, count), 0)
    return jnp.sum(jnp.where(down == lanes((count, count)), row, 0.0), axis=1, keepdims=True)


def rope_lanes(tab):
    at = lanes(tab.shape)
    cos = jnp.where(at < 32, tab, 0.0)
    sin = jnp.where((at >= 32) & (at < 64), tab, 0.0)
    cos = cos + pltpu.roll(cos, 32, 1)
    cos = cos + pltpu.roll(cos, 64, 1)
    sin = sin - pltpu.roll(sin, 96, 1)
    sin = sin + pltpu.roll(sin, 64, 1)
    return cos, sin


def swap_halves(u):
    return jnp.where(lax.rem(lanes(u.shape), 64) < 32, pltpu.roll(u, 96, 1), pltpu.roll(u, 32, 1))


def two_heads(u):
    first = lanes(u.shape) < 64
    zero = jnp.zeros_like(u)
    return jnp.concatenate([jnp.where(first, u, zero), jnp.where(first, zero, u)], axis=0)


def join_heads(t):
    rows = t.shape[1] // 2
    return jnp.concatenate([t[:64, :rows], t[64:, rows:]], axis=0).T


def bias_of(tab, keys, first_row, first_key=0):
    rows = tab.shape[0]
    starts = tab.T[64:65, :].astype(jnp.int32)
    key = first_key + lax.broadcasted_iota(jnp.int32, (keys, rows), 0)
    row = first_row + lax.broadcasted_iota(jnp.int32, (keys, rows), 1)
    bias = jnp.where((key >= starts) & (key <= row), 0.0, MASKED)
    return jnp.concatenate([bias, bias], axis=1)


def forward_kernel(
    dims, tokens, positions, starts, gain_a, gain_m, frequency, w_query, w_key, w_value, w_out_t, w_gate, w_up,
    down, cot,
    gains, n1_out, w_out, tab, q, kk, vv, stat, ob, mid, n2g, cotg, w_mlp, w_dn,
    n1g, w_attn, table, n1, blocks, mlp_blocks, mlp_t, kv, vt, part, held, came, n2,
    gs, gr, gl, ts, tr, ss, sr, ds, dr, ws, wr, us, ur, ys, yr, rs, rr, rxs, rxr, cs, cr, cl, ns, nr, nl, ms, mr, local,
):
    nx, nc, nz, ny = dims
    x, c, z, y = place()
    rows, width = tokens.shape
    own = w_query.shape[0]
    qcols = q.shape[-1]
    pairs = qcols // 128
    span = w_gate.shape[1] // (nx * nc * nz)
    keys_span = ny * rows
    dn = Spread(lambda px, py: down, lambda px, py: w_dn.at[px, py], ws, wr, local.at[0], nx, ny)
    swap = Swap(
        lambda pz, pc: blocks.at[pz, pc], lambda pz, pc: w_attn.at[x, pc, pz, y], ss, sr, local.at[1], nz, nc
    )
    tabs = Swap(lambda pz, pc: table, lambda pz, pc: tab.at[pz, pc], ts, tr, local.at[2], nz, nc)
    mlp_swap = Swap(
        lambda pz, pc: mlp_blocks.at[pz, pc], lambda pz, pc: mlp_t.at[pc, pz], us, ur, local.at[3], nz, nc
    )
    gu = Spread(lambda px, py: mlp_t, lambda px, py: w_mlp.at[px, :, :, py], ms, mr, local.at[4], nx, ny)
    first_rows = Gather(n1, n1g, gs, gr, gl)
    reduce = Reduce(part, held, came, rs, rr, rxs, rxr)
    cots = Gather(cot, cotg, cs, cr, cl)
    next_rows = Gather(n2, n2g, ns, nr, nl)
    met = greet(*dims)

    def pack(at):
        gain = gains[at, 0:1]
        for t in range(nz * nc):
            cols = slice(t * qcols, (t + 1) * qcols)
            blocks[t // nc, t % nc, at, :qcols] = (w_query[at, cols].astype(F32) * gain).astype(BF)
            blocks[t // nc, t % nc, at, qcols + 128 :] = w_out_t[at, cols]
        for pair in range(KV_HEADS // 2):
            cols = slice(pair * 128, pair * 128 + 128)
            key, value = w_key[at, cols].astype(F32) * gain, w_value[at, cols].astype(F32) * gain
            first = lanes(key.shape) < 64
            both = (
                jnp.where(first, key, pltpu.roll(value, 64, 1)),
                jnp.where(first, pltpu.roll(key, 64, 1), value),
            )
            for k in range(2):
                for rep in range(nz * nc // KV_HEADS):
                    t = (pair * 2 + k) * (nz * nc // KV_HEADS) + rep
                    blocks[t // nc, t % nc, at, qcols : qcols + 128] = both[k].astype(BF)

    def norm(at):
        value = tokens[at, :].astype(F32)
        inverse = lax.rsqrt(jnp.mean(value * value, axis=-1, keepdims=True) + EPSILON)
        n1[at, :] = (value * inverse).astype(BF)

    first_lanes = lanes((own, 128)) < 64
    gains[...] = jnp.where(first_lanes, column(gain_a[...].astype(F32)), column(gain_m[...].astype(F32)))
    by_rows(rows, norm)
    by_rows(own, pack)
    angle = column(positions[...].astype(F32)) * frequency[...]
    at = lanes(angle.shape)
    doc = jnp.broadcast_to(column(starts[...].astype(F32)), angle.shape)
    table[...] = jnp.where(at < 32, jnp.cos(angle), jnp.where(at < 64, jnp.sin(angle), doc))
    met()
    swap.start()
    tabs.start()
    dn.start()

    def spread_copies():
        for i, step in enumerate(others(nx, ny)):
            px, py = data_peer(step, nx, ny)
            slot = w_attn.at[x, :, :, y]
            yield remote(slot, slot, ds.at[i], dr.at[i], {"x": px, "y": py})

    def spread():
        swap.arrived()
        for copy in spread_copies():
            copy.start()

    def pack_mlp(at):
        gain = gains[at, 64:65]
        for k, weight in enumerate((w_gate, w_up)):
            for t in range(nz * nc):
                for i in range(nx):
                    chunk = (i * nc + t % nc) * nz + t // nc
                    to = (k * nx + i) * span
                    piece = weight[at, chunk * span : (chunk + 1) * span].astype(F32) * gain
                    mlp_blocks[t // nc, t % nc, at, to : to + span] = piece.astype(BF)

    end = flow(None, first_rows, None, [spread, lambda: by_rows(own, pack_mlp)])
    end()
    mlp_swap.start()
    keep_rows = pltpu.make_async_copy(n1g, n1_out, local.at[5])
    keep_rows.start()
    tabs.arrived()
    for copy in spread_copies():
        copy.wait_recv()
    keep_weights = pltpu.make_async_copy(w_attn, w_out, local.at[6])
    keep_weights.start()

    def project_kv(i, carry):
        u = nn(n1g[i].reshape(nc * rows, width), w_attn[..., qcols : qcols + 128].reshape(width, 128))
        cos, sin = rope_lanes(tab[i].reshape(nc * rows, 128))
        u = jnp.where(lanes(u.shape) < 64, u * cos + swap_halves(u) * sin, u).astype(BF)
        for pc in range(nc):
            kv[pc, i, y] = u[pc * rows : (pc + 1) * rows]
        return carry

    def project_q(i, carry):
        res = nn(n1g[i].reshape(nc * rows, width), w_attn[..., :qcols].reshape(width, qcols))
        cos, sin = rope_lanes(tab[i].reshape(nc * rows, 128))
        for p in range(pairs):
            u = res[:, p * 128 : p * 128 + 128]
            u = (u * cos + swap_halves(u) * sin) * (HEAD_DIM ** (-0.5))
            q[i, :, :, p * 128 : p * 128 + 128] = u.astype(BF).reshape(nc, rows, 128)
        return carry

    lax.fori_loop(0, nz, project_kv, 0)
    sends = []
    for i in range(ny - 1):
        slot = kv.at[:, :, y]
        sends.append(remote(slot, slot, ys.at[i], yr.at[i], {"y": lax.rem(y + 1 + i, ny)}))
    for copy in sends:
        copy.start()
    lax.fori_loop(0, nz, project_q, 0)
    for copy in sends:
        copy.wait_recv()

    def double(i, carry):
        pc, pz = i // nz, lax.rem(i, nz)
        u = kv[pc, pz].reshape(keys_span, 128).astype(F32)
        r = pltpu.roll(u, 64, 1)
        first = lanes(u.shape) < 64
        at = pl.ds(pl.multiple_of(pz * keys_span, keys_span), keys_span)
        kk[pc, at, :] = jnp.where(first, u, r).astype(BF)
        values = jnp.where(first, r, u)
        vv[pc, at, :] = values.astype(BF)
        vt[pc, :, at] = values.T.astype(BF)
        return carry

    lax.fori_loop(0, nc * nz, double, 0)

    def attend(pc, carry):
        for pz in range(nz):
            keys = (pz + 1) * keys_span
            bias = bias_of(tab[pz, pc], keys, (pz * ny + y) * rows)
            for p in range(pairs):
                q2 = two_heads(q[pz, pc, :, p * 128 : p * 128 + 128])
                s = nt(kk[pc, :keys, :], q2) + bias
                top = jnp.max(s, axis=0, keepdims=True)
                e = jnp.exp(s - top)
                total = jnp.sum(e, axis=0, keepdims=True)
                stat[pz, pc, p : p + 1, :] = top + jnp.log(total)
                weights = (e * (1.0 / total)).astype(BF)
                o = join_heads(nn(vt[pc, :, :keys], weights))
                ob[pz, pc, :, p * 128 : p * 128 + 128] = o.astype(BF)
        return carry

    lax.fori_loop(0, nc, attend, 0)

    def output(i, carry):
        half, odd = i // 2, lax.rem(i, 2)
        pz = odd * half + (1 - odd) * (nz - 1 - half)
        for px in range(nx):
            cols = slice(px * (width // nx), (px + 1) * (width // nx))
            weights = w_attn[px, :, :, :, :, qcols + 128 :].reshape(width // nx, qcols)
            res = nt(ob[pz].reshape(nc * rows, qcols), weights)
            part[pz, :, :, cols] = res.astype(BF).reshape(nc, rows, width // nx)
        reduce.across(pz).start()
        return carry

    lax.fori_loop(0, nz, output, 0)

    def spread_mlp():
        mlp_swap.arrived()
        gu.start()

    end2 = flow(reduce, cots, None, [spread_mlp])

    def settle(at, total):
        value = tokens[at, :].astype(F32) + total
        mid[at, :] = value
        inverse = lax.rsqrt(jnp.mean(value * value, axis=-1, keepdims=True) + EPSILON)
        n2[at, :] = (value * inverse).astype(BF)

    end3 = flow(None, next_rows, lambda half: reduce.last(half, settle))
    end3()
    end2()
    keep_rows.wait()
    keep_weights.wait()
    gu.arrived()
    dn.arrived()
    for one in (swap, tabs, mlp_swap, gu, dn):
        one.finish()
    for copy in list(spread_copies()) + sends:
        copy.wait_send()


def forward_call(
    dims, tokens, positions, starts, gain_a, gain_m, w_query, w_key, w_value, w_out_t, w_gate, w_up, down, cot
):
    nx, nc, nz, ny = dims
    rows, width = tokens.shape
    own = w_query.shape[0]
    qcols = HEADS // (nz * nc) * HEAD_DIM
    cols = 2 * qcols + 128
    peers, members = nx * ny - 1, nz * nc - 1
    mlp_cols = 2 * w_gate.shape[1] // (nz * nc)
    keys = nz * ny * rows
    team_rows = (nz, nc, rows, width)
    half = HEAD_DIM // 2
    exponents = np.tile(np.arange(half), 128 // half)[None, :] * (-2.0 / HEAD_DIM)
    frequency = jnp.asarray(10000.0**exponents, F32)
    return call(
        functools.partial(forward_kernel, dims),
        (
            tokens, positions, starts, gain_a, gain_m, frequency, w_query, w_key, w_value, w_out_t, w_gate, w_up,
            down, cot,
        ),
        (VM,) * 12 + (pl.ANY, VM),
        [
            ((own, 128), F32),
            (team_rows, BF),
            ((nx, nc, nz, ny, own, cols), BF),
            ((nz, nc, rows, 128), F32),
            ((nz, nc, rows, qcols), BF),
            ((nc, keys, 128), BF),
            ((nc, keys, 128), BF),
            ((nz, nc, 8, 2 * rows), F32),
            ((nz, nc, rows, qcols), BF),
            ((rows, width), F32),
            (team_rows, BF),
            (team_rows, BF),
            ((nx, nc, nz, ny, own, mlp_cols), BF),
            ((nx, ny) + down.shape, BF),
        ],
        (VM,) + (pl.ANY,) * 2 + (VM,) * 7 + (pl.ANY,) * 4,
        [
            VM(team_rows, BF),
            VM((nx, nc, nz, ny, own, cols), BF),
            VM((rows, 128), F32),
            VM((rows, width), BF),
            VM((nz, nc, own, cols), BF),
            VM((nz, nc, own, mlp_cols), BF),
            VM((nc, nz, own, mlp_cols), BF),
            VM((nc, nz, ny, rows, 128), BF),
            VM((nc, 128, keys), BF),
            VM(team_rows, BF),
        ]
        + Reduce.buffers(nz, rows, width)
        + [VM((rows, width), BF)]
        + Gather.SEMS
        + [DMA((members,))] * 4
        + [DMA((peers,))] * 4
        + [DMA((members,))] * 2
        + [DMA((max(ny - 1, 1),))] * 2
        + Reduce.SEMS
        + Gather.SEMS * 2
        + [DMA((peers,))] * 2
        + [DMA((7,))],
        1,
    )


def mlp_kernel(
    dims, n2g, cotg, w_mlp, w_dn, mid, cot,
    dx2, dag, output, came_mlp, grad_dn,
    n2v, cotv, wv, wd, hid, hid_t, dmlp, part, mlp_out, grad_mlp,
    held, came, held2, came2, low,
    loads, rs, rr, rxs, rxr, os, orr, oxs, oxr, ds, dr, dl, ms, mr, local,
):
    nx, nc, nz, ny = dims
    x, c, z, y = place()
    rows, width = mid.shape
    ff2 = wv.shape[-1]
    ff = ff2 // 2
    piece = wd.shape[2]
    block = nc * rows
    fetch_w = pltpu.make_async_copy(w_mlp, wv, loads.at[0])
    fetch_d = pltpu.make_async_copy(w_dn, wd, loads.at[1])
    fetch_w.start()

    def fetch(at, k):
        source, target = ((n2g, n2v), (cotg, cotv))[k]
        return pltpu.make_async_copy(source.at[at], target.at[at], loads.at[2 + k * nz + at])

    for k in range(nz):
        fetch(by_need(nz, z, k), 0).start()
        if k == 0:
            fetch_d.start()
        fetch(by_need(nz, z, k), 1).start()
    met = greet(*dims)
    reduce = Reduce(part, held, came, rs, rr, rxs, rxr)
    reduce2 = Reduce(mlp_out, held2, came2, os, orr, oxs, oxr)
    into = Gather(low, dag, ds, dr, dl)
    gu = Spread(
        lambda px, py: grad_mlp.at[px, :, :, py], lambda px, py: came_mlp.at[px, py], ms, mr, local.at[0], nx, ny
    )

    def down_rows(cols):
        if piece % ROWS:
            return jnp.concatenate([wd[px, py, :, cols] for px in range(nx) for py in range(ny)], axis=0)
        return wd[:, :, :, cols].reshape(ff, -1)

    def weights(px):
        return wv[px].reshape(width // nx, ff2)

    fetch_w.wait()

    def forward_back(k):
        at = by_need(nz, z, k)
        fetch(at, 0).wait()
        u = nn(n2v[at].reshape(block, width), wv[...].reshape(width, ff2))
        gt, up = u[:, :ff], u[:, ff:]
        sg = jax.nn.sigmoid(gt)
        silu = gt * sg
        value = (silu * up).astype(BF)
        hid[at] = value
        hid_t[:, pl.ds(pl.multiple_of(at * block, block), block)] = value.astype(F32).T.astype(BF)
        if k == 0:
            fetch_d.wait()
        fetch(at, 1).wait()
        dh = nt(cotv[at].reshape(block, width), down_rows(slice(None)))
        dgt = dh * up * sg * (1.0 + gt * (1.0 - sg))
        dmlp[at] = jnp.concatenate([dgt, dh * silu], axis=1).astype(BF)

        for px in range(nx):
            cols = slice(px * (width // nx), (px + 1) * (width // nx))
            res = nt(dmlp[at], weights(px))
            part[at, :, :, cols] = res.astype(BF).reshape(nc, rows, width // nx)
        if k == 0:
            met()
        reduce.across(at).start()

    forward_back(0)
    chunk = width // 4

    def down_grad(n, carry):
        cols = pl.ds(pl.multiple_of(n * chunk, chunk), chunk)
        res = nn(hid_t[...], cotv[:, :, :, cols].reshape(nz * block, chunk)).astype(BF)
        for px in range(nx):
            for py in range(ny):
                k = (px * ny + py) * piece
                grad_dn[px, py, :, cols] = res[k : k + piece]
        return carry

    def mlp_grad(far):
        px = lax.rem(x + far, nx)
        size = width // (nx * 4)

        def body(j, carry):
            cols = pl.ds(pl.multiple_of(px * (width // nx) + j * size, size), size)
            res = tn(n2v[:, :, :, cols].reshape(nz * block, size), dmlp[...].reshape(nz * block, ff2))
            own = grad_mlp.shape[4]
            grad_mlp[px, j // 2, pl.ds(lax.rem(j, 2) * (nz // 2), nz // 2)] = res.astype(BF).reshape(
                nz // 2, ny, own, ff2
            )
            return carry

        lax.fori_loop(0, 4, body, 0)
        gu.start_along(far)

    def mlp_sum(n, carry):
        cols = pl.ds(pl.multiple_of(n * chunk, chunk), chunk)
        res = nn(hid[...].reshape(nz * block, ff), down_rows(cols))
        mlp_out[:, :, :, cols] = res.astype(BF).reshape(nz, nc, rows, chunk)
        return carry

    def down_first():
        lax.fori_loop(0, 2, down_grad, 0)

    def down_second():
        lax.fori_loop(2, 4, down_grad, 0)

    def sum_all():
        lax.fori_loop(0, 4, mlp_sum, 0)
        reduce2.start()

    def other_blocks():
        for k in range(2, nz):
            forward_back(k)

    forward_back(1)
    work = [other_blocks] + [functools.partial(mlp_grad, far) for far in reversed(range(nx))]
    end = flow(reduce, None, None, work + [sum_all])

    def settle(at, total):
        value = mid[at, :]
        inverse = lax.rsqrt(jnp.mean(value * value, axis=-1, keepdims=True) + EPSILON)
        normed = value * inverse
        gradient = cot[at, :].astype(F32) + inverse * (
            total - normed * jnp.mean(total * normed, axis=-1, keepdims=True)
        )
        dx2[at, :] = gradient
        low[at, :] = gradient.astype(BF)

    end2 = flow(reduce2, into, lambda part: reduce.last(part, settle), [down_first, down_second])

    def finish(at, total):
        output[at, :] = (mid[at, :] + total).astype(BF)

    for half in range(PARTS):
        reduce2.last(half, finish)
    end2()
    end()
    gu.arrived()
    gu.finish()


def mlp_call(dims, n2g, cotg, w_mlp, w_dn, mid, cot):
    nx, nc, nz, ny = dims
    rows, width = mid.shape
    own, ff2 = w_mlp.shape[4:]
    block = nc * rows
    peers = nx * ny - 1
    return call(
        functools.partial(mlp_kernel, dims),
        (n2g, cotg, w_mlp, w_dn, mid, cot),
        (pl.ANY, pl.ANY, pl.ANY, pl.ANY, VM, VM),
        [
            ((rows, width), F32),
            ((nz, nc, rows, width), BF),
            ((rows, width), BF),
            ((nx, ny, nc, nz, own, ff2), BF),
            (w_dn.shape, BF),
        ],
        (VM, pl.ANY, VM, pl.ANY, VM),
        [
            VM(n2g.shape, BF),
            VM(cotg.shape, BF),
            VM(w_mlp.shape, BF),
            VM(w_dn.shape, BF),
            VM((nz, block, ff2 // 2), BF),
            VM((ff2 // 2, nz * block), BF),
            VM((nz, block, ff2), BF),
            VM(n2g.shape, BF),
            VM(n2g.shape, BF),
            VM(w_mlp.shape, BF),
        ]
        + Reduce.buffers(nz, rows, width) * 2
        + [VM((rows, width), BF), DMA((2 + 2 * nz,))]
        + Reduce.SEMS * 2
        + Gather.SEMS
        + [DMA((peers,))] * 2
        + [DMA((1,))],
        3,
    )


def backward_kernel(
    dims, dag, w, tab, q, kk, vv, stat, ob, came_mlp, grad_dn, n1g,
    dn1, raw_gate, raw_up, came_dn, own_o, own_p,
    do, kt, dk, dv, out, near, dqkv, part, team, stage, mlp_sum, mlp_g,
    grad_o, came_o, sums_o, grad_p, came_p, sums_p,
    held, came,
    loads, us, ur, ys, yr, ws, wr, rs, rr, rxs, rxr, ds, dr, ss, sr, es, er, fs, fr, local,
):
    nx, nc, nz, ny = dims
    x, c, z, y = place()
    rows, width = dn1.shape
    own = grad_o.shape[4]
    qcols = q.shape[-1]
    pairs = qcols // 128
    keys_span = ny * rows
    fetch_dag = pltpu.make_async_copy(dag, team, loads.at[2])
    fetch = pltpu.make_async_copy(n1g, team, loads.at[2])
    fetch_dag.start()
    mlp_swap = Swap(
        lambda pz, pc: mlp_sum.at[pz, pc], lambda pz, pc: mlp_g.at[pz, pc], us, ur, local.at[0], nz, nc
    )
    dn = Spread(lambda px, py: grad_dn.at[px, py], lambda px, py: came_dn.at[px, py], ws, wr, local.at[1], nx, ny)
    reduce = Reduce(part, held, came, rs, rr, rxs, rxr)
    spread_o = Spread(
        lambda px, py: grad_o.at[px, :, :, py], lambda px, py: came_o.at[px, py], ds, dr, local.at[2], nx, ny
    )
    swap_o = Swap(lambda pz, pc: sums_o.at[pz, pc], lambda pz, pc: own_o.at[pz, pc], ss, sr, local.at[3], nz, nc)
    spread_p = Spread(
        lambda px, py: grad_p.at[px, :, :, py], lambda px, py: came_p.at[px, py], es, er, local.at[4], nx, ny
    )
    swap_p = Swap(lambda pz, pc: sums_p.at[pz, pc], lambda pz, pc: own_p.at[pz, pc], fs, fr, local.at[5], nz, nc)

    steps = others(nz, nc) + [(0, 0)]

    def load(i):
        pz, pc = team_peer(steps[i], nz, nc)
        return pltpu.make_async_copy(came_mlp.at[:, :, pc, pz], stage.at[i % 2], loads.at[i % 2])

    load(0).start()
    met = greet(*dims, cross=True)

    def turned(i, carry):
        pc, pz = i // nz, lax.rem(i, nz)
        at = pl.ds(pl.multiple_of(pz * keys_span, keys_span), keys_span)
        kt[pc, :, at] = kk[pc, at, :].astype(F32).T.astype(BF)
        return carry

    lax.fori_loop(0, nc * nz, turned, 0)
    early = 2 * (nx * ny - 1) // 3
    for i, copy in enumerate(list(mlp_swap.copies()) + [mlp_swap.own()]):
        if i + 1 < len(steps):
            load(i + 1).start()
        load(i).wait()
        pz, pc = team_peer(steps[i], nz, nc)

        def add(at, i=i, pz=pz, pc=pc):
            total = stage[i % 2, 0, 0, at, :].astype(F32)
            for px, py in others(nx, ny):
                total = total + stage[i % 2, px, py, at, :].astype(F32)
            mlp_sum[pz, pc, at, :] = total.astype(BF)

        by_rows(own, add)
        if i == 0:
            met()
            dn.start_some(0, early)
            dn.own().start()
        copy.start()
    fetch_dag.wait()

    def project(i, carry):
        weights = w[..., qcols + 128 :].reshape(width, qcols)
        do[i] = nn(team[i].reshape(nc * rows, width), weights).astype(BF).reshape(nc, rows, qcols)
        return carry

    lax.fori_loop(0, nz, project, 0)

    def attend(pc, carry):
        for pz in reversed(range(nz)):
            keys = (pz + 1) * keys_span
            most = KEYS if nz * keys_span <= KEYS else KEYS // 4
            cuts = [slice(a, min(a + most, keys)) for a in range(0, keys, most)]

            def bias_at(i, cuts=cuts, pz=pz):
                cut = cuts[i]
                return bias_of(tab[pz, pc], cut.stop - cut.start, (pz * ny + y) * rows, cut.start)

            only = bias_at(0) if len(cuts) == 1 else None
            cos, sin = rope_lanes(tab[pz, pc])
            for p in range(pairs):
                q2 = two_heads(q[pz, pc, :, p * 128 : p * 128 + 128])
                do2 = two_heads(do[pz, pc, :, p * 128 : p * 128 + 128])

                def scores(i, cuts=cuts, only=only, bias_at=bias_at, q2=q2, do2=do2, p=p, pz=pz):
                    s = nt(kk[pc, cuts[i], :], q2) + (bias_at(i) if only is None else only)
                    weights = jnp.exp(s - stat[pz, pc, p : p + 1, :])
                    return weights, weights * nt(vv[pc, cuts[i], :], do2)

                delta = sum(jnp.sum(scores(i)[1], axis=0, keepdims=True) for i in range(1, len(cuts)))
                u = 0.0
                for i, cut in enumerate(cuts):
                    weights, dw = scores(i)
                    if i == 0:
                        delta = delta + jnp.sum(dw, axis=0, keepdims=True)
                    score_grad = (dw - weights * delta).astype(BF)
                    dv_new = nn(weights.astype(BF), do2)
                    dk_new = nn(score_grad, q2)
                    if pz == nz - 1 and p == 0:
                        dv[pc, cut, :] = dv_new
                        dk[pc, cut, :] = dk_new
                    else:
                        dv[pc, cut, :] += dv_new
                        dk[pc, cut, :] += dk_new
                    u = u + nn(kt[pc, :, cut], score_grad)
                u = join_heads(u) * (HEAD_DIM ** (-0.5))
                u = u * cos - swap_halves(u) * sin
                dqkv[pz, pc, :, p * 128 : p * 128 + 128] = u.astype(BF)
        return carry

    lax.fori_loop(0, nc, attend, 0)

    def fold(i, carry):
        pc, pz = i // nz, lax.rem(i, nz)
        at = pl.ds(pl.multiple_of(pz * keys_span, keys_span), keys_span)
        key, value = dk[pc, at, :], dv[pc, at, :]
        first = lanes(key.shape) < 64
        both = jnp.where(first, key + pltpu.roll(key, 64, 1), value + pltpu.roll(value, 64, 1))
        both = both.astype(BF)
        for py in range(ny):
            out[pc, py, pz] = both[py * rows : (py + 1) * rows]
        return carry

    lax.fori_loop(0, nc * nz, fold, 0)
    sends = []
    for i, (sy, sc) in enumerate(others(ny, nc)):
        py, pc = lax.rem(y + sy, ny), lax.rem(c + sc, nc)
        sends.append(remote(out.at[pc, py], near.at[i], ys.at[i], yr.at[i], {"y": py, "core": pc}))
    for copy in sends:
        copy.start()

    def weight_grad(right, target):
        def body(j, carry):
            px, k = j // 4, lax.rem(j, 4)
            size = width // (nx * 4)
            cols = pl.ds(pl.multiple_of(j * size, size), size)
            res = tn(team[:, :, :, cols].reshape(nz * nc * rows, size), right.reshape(nz * nc * rows, -1))
            target[px, k // 2, pl.ds(lax.rem(k, 2) * (nz // 2), nz // 2)] = res.astype(BF).reshape(
                nz // 2, ny, own, -1
            )
            return carry

        lax.fori_loop(0, nx * 4, body, 0)

    weight_grad(ob[...], grad_o)
    fetch.start()
    for copy in sends:
        copy.wait_recv()
    spread_o.start()

    def settle_kv(pz, carry):
        total = out[c, y, pz].astype(F32)
        for i in range(len(sends)):
            total = total + near[i, pz].astype(F32)
        cos, sin = rope_lanes(tab[pz, c])
        first = lanes(total.shape) < 64
        total = jnp.where(first, total * cos - swap_halves(total) * sin, total)
        dqkv[pz, c, :, qcols : qcols + 128] = total.astype(BF)
        dqkv[pz, 1 - c, :, qcols : qcols + 128] = jnp.zeros((rows, 128), BF)
        return carry

    lax.fori_loop(0, nz, settle_kv, 0)

    def output(i, carry):
        half, odd = i // 2, lax.rem(i, 2)
        pz = odd * half + (1 - odd) * (nz - 1 - half)
        for px in range(nx):
            cols = slice(px * (width // nx), (px + 1) * (width // nx))
            weights = w[px, :, :, :, :, : qcols + 128].reshape(width // nx, qcols + 128)
            res = nt(dqkv[pz].reshape(nc * rows, qcols + 128), weights)
            part[pz, :, :, cols] = res.astype(BF).reshape(nc, rows, width // nx)
        reduce.across(pz).start()
        return carry

    lax.fori_loop(0, nz, output, 0)

    def own_weights():
        fetch.wait()
        weight_grad(dqkv[...], grad_p)
        spread_p.start()

    def unpack_mlp(at):
        span = mlp_g.shape[-1] // (2 * nx)
        for k, raw in enumerate((raw_gate, raw_up)):
            for t in range(nz * nc):
                for i in range(nx):
                    chunk = (i * nc + t % nc) * nz + t // nc
                    piece = mlp_g[t // nc, t % nc, at, (k * nx + i) * span : (k * nx + i + 1) * span]
                    raw[at, chunk * span : (chunk + 1) * span] = piece

    def unpack_all():
        mlp_swap.arrived()
        by_rows(own, unpack_mlp)

    def down_rest():
        dn.start_some(early, nx * ny - 1)

    def exchange(spread, arrived, sums, swap):
        spread.arrived()

        def add(at):
            for pz in range(nz):
                for pc in range(nc):
                    total = arrived[0, 0, pc, pz, at, :].astype(F32)
                    for px, py in others(nx, ny):
                        total = total + arrived[px, py, pc, pz, at, :].astype(F32)
                    sums[pz, pc, at, :] = total.astype(BF)

        by_rows(own, add)
        swap.start()

    work = [
        own_weights,
        unpack_all,
        down_rest,
        functools.partial(exchange, spread_o, came_o, sums_o, swap_o),
        functools.partial(exchange, spread_p, came_p, sums_p, swap_p),
    ]
    end = flow(reduce, None, None, work)

    def settle(at, total):
        dn1[at, :] = total

    for half in range(PARTS):
        reduce.last(half, settle)
    end()
    for one in (dn, swap_o, swap_p):
        one.arrived()
    for one in (mlp_swap, dn, spread_o, swap_o, spread_p, swap_p):
        one.finish()
    for copy in sends:
        copy.wait_send()


def backward_call(dims, dag, w, tab, q, kk, vv, stat, ob, came_mlp, grad_dn, n1g):
    nx, nc, nz, ny = dims
    rows, width = dag.shape[2:]
    own, mlp_cols = came_mlp.shape[4:]
    qcols = q.shape[-1]
    keys = nz * ny * rows
    peers, members, near = nx * ny - 1, nz * nc - 1, ny * nc - 1
    team_rows = (nz, nc, rows, width)
    return call(
        functools.partial(backward_kernel, dims),
        (dag, w, tab, q, kk, vv, stat, ob, came_mlp, grad_dn, n1g),
        (pl.ANY,) + (VM,) * 7 + (pl.ANY,) * 3,
        [
            ((rows, width), F32),
            ((own, mlp_cols // 2 * nz * nc), BF),
            ((own, mlp_cols // 2 * nz * nc), BF),
            (grad_dn.shape, BF),
            ((nz, nc, own, qcols), BF),
            ((nz, nc, own, qcols + 128), BF),
        ],
        (VM,) * 3 + (pl.ANY,) * 3,
        [
            VM((nz, nc, rows, qcols), BF),
            VM((nc, 128, keys), BF),
            VM((nc, keys, 128), F32),
            VM((nc, keys, 128), F32),
            VM((nc, ny, nz, rows, 128), BF),
            VM((near, nz, rows, 128), BF),
            VM((nz, nc, rows, qcols + 128), BF),
            VM(team_rows, BF),
            VM(team_rows, BF),
            VM((2, nx, ny, own, mlp_cols), BF),
            VM((nz, nc, own, mlp_cols), BF),
            VM((nz, nc, own, mlp_cols), BF),
        ]
        + [
            VM(shape + (own, n), BF)
            for n in (qcols, qcols + 128)
            for shape in ((nx, nc, nz, ny), (nx, ny, nc, nz), (nz, nc))
        ]
        + Reduce.buffers(nz, rows, width)
        + [DMA((3,))]
        + [DMA((members,))] * 2
        + [DMA((near,))] * 2
        + [DMA((peers,))] * 2
        + Reduce.SEMS
        + ([DMA((peers,))] * 2 + [DMA((members,))] * 2) * 2
        + [DMA((6,))],
        6,
    )


def final_kernel(
    dims, dn1, tokens, dx2, raw_gate, raw_up, came_dn, own_o, own_p, gains, w_query, w_key, w_value, w_gate, w_up,
    input_grad, grad_query, grad_key, grad_value, grad_out_t, grad_gate, grad_up, grad_down, grad_gain,
):
    nx, nc, nz, ny = dims
    team = nz * nc
    value = tokens[...].astype(F32)
    total = dn1[...]
    inverse = lax.rsqrt(jnp.mean(value * value, axis=-1, keepdims=True) + EPSILON)
    normed = value * inverse
    input_grad[...] = dx2[...] + inverse * (total - normed * jnp.mean(total * normed, axis=-1, keepdims=True))

    down = came_dn[0, 0].astype(F32)
    for px, py in others(nx, ny):
        down = down + came_dn[px, py].astype(F32)
    grad_down[...] = down

    gain = gains[:, 64:65]
    both = 0.0
    for raw, weight, grad in ((raw_gate, w_gate, grad_gate), (raw_up, w_up, grad_up)):
        got = raw[...].astype(F32)
        grad[...] = got * gain
        both = both + got * weight[...].astype(F32)
    dots_mlp = jnp.sum(both, axis=-1, keepdims=True)

    gain = gains[:, 0:1]
    qcols = own_o.shape[-1]
    both = 0.0
    heads = []
    for t in range(team):
        block = own_p[t // nc, t % nc].astype(F32)
        cols = slice(t * qcols, (t + 1) * qcols)
        grad_out_t[:, cols] = own_o[t // nc, t % nc].astype(F32)
        grad_query[:, cols] = block[:, :qcols] * gain
        both = both + block[:, :qcols] * w_query[:, cols].astype(F32)
        if t % (team // KV_HEADS):
            heads[-1] = heads[-1] + block[:, qcols:]
        else:
            heads.append(block[:, qcols:])
    dots = jnp.sum(both, axis=-1, keepdims=True)
    for pair in range(KV_HEADS // 2):
        one, two = heads[2 * pair], heads[2 * pair + 1]
        first = lanes(one.shape) < 64
        cols = slice(pair * 128, pair * 128 + 128)
        key = jnp.where(first, one, pltpu.roll(two, 64, 1))
        val = jnp.where(first, pltpu.roll(one, 64, 1), two)
        grad_key[:, cols] = key * gain
        grad_value[:, cols] = val * gain
        both = key * w_key[:, cols].astype(F32) + val * w_value[:, cols].astype(F32)
        dots = dots + jnp.sum(both, axis=-1, keepdims=True)
    shape = grad_gain.shape
    grad_gain[...] = jnp.where(lanes(shape) < 64, dots, dots_mlp)


def final_call(
    dims, dn1, tokens, dx2, raw_gate, raw_up, came_dn, own_o, own_p, gains, w_query, w_key, w_value, w_gate, w_up
):
    own = w_query.shape[0]
    steps = max(own // ROWS, 1)

    def rows_of(shape, axis):
        count = shape[axis]
        each = count if steps == 1 else -(-count // (steps * ROWS)) * ROWS
        block = shape[:axis] + (each,) + shape[axis + 1 :]
        return pl.BlockSpec(block, lambda i: tuple(i if k == axis else 0 for k in range(len(shape))))

    operands = (
        dn1, tokens, dx2, raw_gate, raw_up, came_dn, own_o, own_p, gains, w_query, w_key, w_value, w_gate, w_up
    )
    outs = [
        dn1.shape, w_query.shape, w_key.shape, w_value.shape, w_query.shape, w_gate.shape, w_up.shape,
        came_dn.shape[2:], (own, 128),
    ]
    return pl.pallas_call(
        functools.partial(final_kernel, dims),
        grid=(steps,),
        out_shape=[jax.ShapeDtypeStruct(s, F32) for s in outs],
        in_specs=[rows_of(a.shape, len(a.shape) - 2) for a in operands],
        out_specs=[rows_of(s, 0) for s in outs],
        compiler_params=pltpu.CompilerParams(vmem_limit_bytes=60 << 20),
    )(*operands)


def shards(
    tokens, positions, doc_start, cotangent, w_query, w_key, w_value, w_out,
    attn_gain, w_gate, w_up, w_down, mlp_gain,
):
    dims = tuple(lax.axis_size(a) for a in ALL)
    gains, n1g, w_attn, tab, q, kk, vv, stat, ob, mid, n2g, cotg, w_mlp, w_dn = forward_call(
        dims, tokens, positions[None], doc_start[None], attn_gain[None], mlp_gain[None],
        w_query, w_key, w_value, w_out.T, w_gate, w_up, w_down, cotangent,
    )
    dx2, dag, output, came_mlp, grad_dn = mlp_call(dims, n2g, cotg, w_mlp, w_dn, mid, cotangent)
    dn1, raw_gate, raw_up, came_dn, own_o, own_p = backward_call(
        dims, dag, w_attn, tab, q, kk, vv, stat, ob, came_mlp, grad_dn, n1g
    )
    (
        input_grad, grad_query, grad_key, grad_value, grad_out_t, grad_gate, grad_up, grad_down, grad_gain
    ) = final_call(
        dims, dn1, tokens, dx2, raw_gate, raw_up, came_dn, own_o, own_p, gains,
        w_query, w_key, w_value, w_gate, w_up,
    )
    return (
        output, input_grad, grad_query, grad_key, grad_value, grad_out_t.T, grad_gain[:, 0],
        grad_gate, grad_up, grad_down, grad_gain[:, 64],
    )


def solution(mesh):
    fsdp, seq = mesh.shape["fsdp"], mesh.shape["seq"]
    nc, nz = 2, 4
    grid = Mesh(mesh.devices.reshape(fsdp // nc, nc, nz, seq // nz), ALL)
    row, col, vec = P(ALL, None), P(None, ALL), P(ALL)
    in_specs = (row, vec, vec, row, row, row, row, col, vec, row, row, row, vec)
    out_specs = (row, row, row, row, row, col, vec, row, row, row, vec)
    return jax.shard_map(shards, mesh=grid, in_specs=in_specs, out_specs=out_specs, check_vma=False)
```

```python
import functools

import jax
import jax.numpy as jnp
import numpy as np
from jax import lax
from jax.experimental import pallas as pl
from jax.experimental.pallas import tpu as pltpu
from jax.sharding import Mesh
from jax.sharding import PartitionSpec as P

HEADS = 32
KV_HEADS = 4
HEAD_DIM = 64
EPSILON = 1e-05
MASKED = -1e30
ALL = ("x", "core", "z", "y")
TEAM = ("z", "core")
DATA = ("x", "y")
BF = jnp.bfloat16
F32 = jnp.float32


MESH = pl.DeviceIdType.MESH
VM = pltpu.VMEM
DMA = pltpu.SemaphoreType.DMA
ROWS = 16
PARTS = 2
WINDOW = 2
KEYS = 1024


def place():
    return tuple(lax.axis_index(a) for a in ALL)


def others(nx, ny):
    return [(i, j) for i in range(nx) for j in range(ny) if (i, j) != (0, 0)]


def data_peer(step, nx, ny):
    x, _, _, y = place()
    return lax.rem(x + step[0], nx), lax.rem(y + step[1], ny)


def team_peer(step, nz, nc):
    _, c, z, _ = place()
    return lax.rem(z + step[0], nz), lax.rem(c + step[1], nc)


def greet(nx, nc, nz, ny, cross=False):
    barrier = pltpu.get_barrier_semaphore()
    x, c, z, y = place()
    extra = ny - 1 if cross else 0
    for i in range(extra):
        device = {"y": lax.rem(y + 1 + i, ny), "core": 1 - c}
        pl.semaphore_signal(barrier, inc=1, device_id=device, device_id_type=MESH)
    for step in others(nx, ny):
        px, py = data_peer(step, nx, ny)
        pl.semaphore_signal(barrier, inc=1, device_id={"x": px, "y": py}, device_id_type=MESH)
    for step in others(nz, nc):
        pz, pc = team_peer(step, nz, nc)
        pl.semaphore_signal(barrier, inc=1, device_id={"z": pz, "core": pc}, device_id_type=MESH)

    def met():
        pl.semaphore_wait(barrier, nx * ny - 1 + nz * nc - 1 + extra)

    return met


def remote(source, target, send, recv, device):
    return pltpu.make_async_remote_copy(
        src_ref=source, dst_ref=target, send_sem=send, recv_sem=recv,
        device_id=device, device_id_type=MESH,
    )


def piece_of(part, rows):
    return pl.ds(part * (rows // PARTS), rows // PARTS)


class Gather:
    SEMS = [DMA((3, 4, PARTS)), DMA((2, 4, PARTS)), DMA((PARTS,))]

    def __init__(self, own, full, send, recv, local):
        self.own, self.full, self.send, self.recv, self.local = own, full, send, recv, local
        self.x, self.c, self.z, self.y = place()
        self.nz, _, self.rows = full.shape[:3]

    def copy(self, at, kind, part, mine=False):
        rows = piece_of(part, self.rows)
        slot = self.full.at[at, self.c, rows]
        device = ({"z": self.z + 1}, {"z": self.z - 1}, {"core": 1 - self.c})[kind]
        return remote(
            self.own.at[rows] if mine else slot, slot, self.send.at[kind, at, part],
            self.recv.at[0 if kind < 2 else 1, at, part], device,
        )

    def keep(self, part):
        rows = piece_of(part, self.rows)
        return pltpu.make_async_copy(self.own.at[rows], self.full.at[self.z, self.c, rows], self.local.at[part])

    def begin(self, part):
        self.keep(part).start()
        self.copy(self.z, 2, part, True).start()

    def finish(self):
        for part in range(PARTS):
            self.keep(part).wait()
            for at in range(self.nz):
                self.copy(at, 2, part).wait_send()
                self.copy(at, 2, part).wait_recv()


class Reduce:
    SEMS = [DMA((2, 4, PARTS)), DMA((2, 4, PARTS)), DMA((4,)), DMA((4,))]

    @staticmethod
    def buffers(nz, rows, width):
        return [VM((nz, rows, width), BF), VM((2, nz - 1, rows, width), BF)]

    def __init__(self, part, held, came, send, recv, across_send, across_recv):
        self.part, self.held, self.came, self.send, self.recv = part, held, came, send, recv
        self.across_send, self.across_recv = across_send, across_recv
        self.x, self.c, self.z, self.y = place()
        self.nz, _, self.rows, self.width = part.shape

    def across(self, to):
        return remote(
            self.part.at[to, 1 - self.c], self.held.at[to], self.across_send.at[to], self.across_recv.at[to],
            {"core": 1 - self.c},
        )

    def along(self, to, way, part):
        device = ({"z": self.z + 1}, {"z": self.z - 1})[way]
        rows = piece_of(part, self.rows)
        return remote(
            self.held.at[to, rows], self.came.at[way, to - 1 + way, rows], self.send.at[way, to, part],
            self.recv.at[way, to, part], device,
        )

    def start(self):
        for to in [a for k in range(self.nz) for a in (self.nz - 1 - k, k)][: self.nz]:
            self.across(to).start()

    def add(self, to, ways, part, out=None):
        size = self.rows // PARTS

        def body(i, carry):
            at = pl.ds(pl.multiple_of(part * size + i * ROWS, ROWS), ROWS)
            total = self.part[to, self.c, at, :].astype(F32) + self.held[to, at, :].astype(F32)
            for way in ways:
                total = total + self.came[way, to - 1 + way, at, :].astype(F32)
            if out is None:
                self.held[to, at, :] = total.astype(BF)
            else:
                out(at, total)
            return carry

        lax.fori_loop(0, size // ROWS, body, 0)

    def last(self, part, out):
        if part == 0:
            self.across(self.z).wait_recv()
        for at in range(self.nz):

            @pl.when(self.z == at)
            def _(at=at):
                ways = ([0] if at > 0 else []) + ([1] if at < self.nz - 1 else [])
                for way in ways:
                    self.along(at, way, part).wait_recv()
                self.add(at, ways, part, out)

    def finish(self):
        for to in range(self.nz):
            self.across(to).wait_send()


def plan(nz, reduces, gathers):
    last = nz - 1
    rows = []
    for e in range(nz):
        sums = [("R", last - k) for k in range(last) if last - k > e]
        blocks = [("G", e - k) for k in range(e + 1)]
        if reduces and gathers:
            if e == last:
                rows.append([None] + blocks[1:-1] + [None] + blocks[-1:])
            else:
                woven = blocks[:-1] + sums[:1] + blocks[-1:] + sums[1:]
                rows.append(woven)
        elif reduces:
            rows.append([None] * e + sums)
        else:
            rows.append(blocks if e < last else [None] + blocks[1:])
    return rows


def by_need(nz, z, k):
    last = nz - 1
    value = 0
    for at in range(nz):
        when = {to: at + last - to if to > at else last - at + to for to in range(nz) if to != at}
        blocks = sorted(when, key=lambda to: (when[to], to)) + [at]
        value = jnp.where(z == at, blocks[k], value)
    return value


def flow(reduce, gather, before=None, work=()):
    work = list(work)
    any_one = reduce or gather
    nz, z = any_one.nz, any_one.z
    table = plan(nz, reduce is not None, gather is not None)
    pending = {(way, e): [] for way in (0, 1) for e in range(nz)}

    def pace(key, make):
        queue = pending[key]
        if len(queue) >= WINDOW:
            queue.pop(0)().wait_send()
        make().start()
        queue.append(make)

    def step(way, e, kind, place_at, part):
        block = place_at if way == 0 else nz - 1 - place_at
        if kind == "R":
            if part == 0:
                reduce.across(block).wait_recv()
            if e > 0:
                reduce.along(block, way, part).wait_recv()
            reduce.add(block, (way,) if e > 0 else (), part)
            pace((way, e), functools.partial(reduce.along, block, way, part))
        else:
            mine = place_at == e
            if not mine:
                gather.copy(block, way, part).wait_recv()
            if e < nz - 1:
                pace((way, e), functools.partial(gather.copy, block, way, part, mine))
            if not mine:
                gather.copy(block, 2, part).start()

    for t in range(max(len(row) for row in table)):
        for part in range(PARTS):
            if t == 0 and before is not None:
                before(part)
            if t == 0 and gather is not None:
                gather.begin(part)
            for way in (0, 1):
                for e in range(nz):
                    op = table[e][t] if t < len(table[e]) else None
                    if op is not None:
                        pl.when(z == (e if way == 0 else nz - 1 - e))(
                            functools.partial(step, way, e, op[0], op[1], part)
                        )
            if work and (t > 0 or part == PARTS - 1):
                work.pop(0)()
    for item in work:
        item()

    def finish():
        for (way, e), queue in pending.items():
            if queue:

                @pl.when(z == (e if way == 0 else nz - 1 - e))
                def _(queue=queue):
                    for make in queue:
                        make().wait_send()

        for one in (reduce, gather):
            if one is not None:
                one.finish()

    return finish


class Spread:
    def __init__(self, source, target, send, recv, local, nx, ny):
        self.source, self.target, self.send, self.recv = source, target, send, recv
        self.nx, self.ny = nx, ny
        self.x, _, _, self.y = place()
        self.own = lambda: pltpu.make_async_copy(source(self.x, self.y), target(self.x, self.y), local)

    def copies(self):
        for i, step in enumerate(others(self.nx, self.ny)):
            px, py = data_peer(step, self.nx, self.ny)
            yield remote(
                self.source(px, py), self.target(self.x, self.y), self.send.at[i], self.recv.at[i],
                {"x": px, "y": py},
            )

    def start(self):
        for copy in self.copies():
            copy.start()
        self.own().start()

    def start_some(self, first, last):
        for i, copy in enumerate(self.copies()):
            if first <= i < last:
                copy.start()

    def start_along(self, far):
        for step, copy in zip(others(self.nx, self.ny), self.copies()):
            if step[0] == far:
                copy.start()
        if far == 0:
            self.own().start()

    def arrived(self):
        self.own().wait()
        for copy in self.copies():
            copy.wait_recv()

    def finish(self):
        for copy in self.copies():
            copy.wait_send()


class Swap:
    def __init__(self, source, slot, send, recv, local, nz, nc):
        self.source, self.slot, self.send, self.recv, self.nz, self.nc = source, slot, send, recv, nz, nc
        _, self.c, self.z, _ = place()
        self.own = lambda: pltpu.make_async_copy(source(self.z, self.c), slot(self.z, self.c), local)

    def copies(self):
        for i, step in enumerate(others(self.nz, self.nc)):
            pz, pc = team_peer(step, self.nz, self.nc)
            yield remote(
                self.source(pz, pc), self.slot(self.z, self.c), self.send.at[i], self.recv.at[i],
                {"z": pz, "core": pc},
            )

    def start(self):
        for copy in self.copies():
            copy.start()
        self.own().start()

    def arrived(self):
        self.own().wait()
        for copy in self.copies():
            copy.wait_recv()

    def finish(self):
        for copy in self.copies():
            copy.wait_send()


def call(kernel, operands, in_spaces, outs, out_spaces, scratch, number):
    return pl.pallas_call(
        kernel,
        out_shape=[jax.ShapeDtypeStruct(s, t) for s, t in outs],
        in_specs=[pl.BlockSpec(memory_space=s) for s in in_spaces],
        out_specs=[pl.BlockSpec(memory_space=s) for s in out_spaces],
        scratch_shapes=scratch,
        compiler_params=pltpu.CompilerParams(
            collective_id=number, has_side_effects=True, vmem_limit_bytes=60 << 20
        ),
    )(*operands)


def lanes(shape):
    return lax.broadcasted_iota(jnp.int32, shape, len(shape) - 1)


def by_rows(count, body):
    if count % ROWS or count == ROWS:
        body(slice(0, count))
    else:

        def step(i, carry):
            body(pl.ds(pl.multiple_of(i * ROWS, ROWS), ROWS))
            return carry

        lax.fori_loop(0, count // ROWS, step, 0)


def nt(a, b):
    return lax.dot_general(a, b, (((1,), (1,)), ((), ())), preferred_element_type=F32)


def nn(a, b):
    return jnp.dot(a, b, preferred_element_type=F32)


def tn(a, b):
    return lax.dot_general(a, b, (((0,), (0,)), ((), ())), preferred_element_type=F32)


def column(row):
    count = row.shape[1]
    down = lax.broadcasted_iota(jnp.int32, (count, count), 0)
    return jnp.sum(jnp.where(down == lanes((count, count)), row, 0.0), axis=1, keepdims=True)


def rope_lanes(tab):
    at = lanes(tab.shape)
    cos = jnp.where(at < 32, tab, 0.0)
    sin = jnp.where((at >= 32) & (at < 64), tab, 0.0)
    cos = cos + pltpu.roll(cos, 32, 1)
    cos = cos + pltpu.roll(cos, 64, 1)
    sin = sin - pltpu.roll(sin, 96, 1)
    sin = sin + pltpu.roll(sin, 64, 1)
    return cos, sin


def swap_halves(u):
    return jnp.where(lax.rem(lanes(u.shape), 64) < 32, pltpu.roll(u, 96, 1), pltpu.roll(u, 32, 1))


def two_heads(u):
    first = lanes(u.shape) < 64
    zero = jnp.zeros_like(u)
    return jnp.concatenate([jnp.where(first, u, zero), jnp.where(first, zero, u)], axis=0)


def join_heads(t):
    rows = t.shape[1] // 2
    return jnp.concatenate([t[:64, :rows], t[64:, rows:]], axis=0).T


def bias_of(tab, keys, first_row, first_key=0):
    rows = tab.shape[0]
    starts = tab.T[64:65, :].astype(jnp.int32)
    key = first_key + lax.broadcasted_iota(jnp.int32, (keys, rows), 0)
    row = first_row + lax.broadcasted_iota(jnp.int32, (keys, rows), 1)
    bias = jnp.where((key >= starts) & (key <= row), 0.0, MASKED)
    return jnp.concatenate([bias, bias], axis=1)


def forward_kernel(
    dims, tokens, positions, starts, gain_a, gain_m, frequency, w_query, w_key, w_value, w_out_t, w_gate, w_up,
    down, cot,
    gains, n1_out, w_out, tab, q, kk, vv, stat, ob, mid, n2g, cotg, w_mlp, w_dn,
    n1g, w_attn, table, n1, blocks, mlp_blocks, mlp_t, kv, vt, part, held, came, n2,
    gs, gr, gl, ts, tr, ss, sr, ds, dr, ws, wr, us, ur, ys, yr, rs, rr, rxs, rxr, cs, cr, cl, ns, nr, nl, ms, mr, local,
):
    nx, nc, nz, ny = dims
    x, c, z, y = place()
    rows, width = tokens.shape
    own = w_query.shape[0]
    qcols = q.shape[-1]
    pairs = qcols // 128
    span = w_gate.shape[1] // (nx * nc * nz)
    keys_span = ny * rows
    dn = Spread(lambda px, py: down, lambda px, py: w_dn.at[px, py], ws, wr, local.at[0], nx, ny)
    swap = Swap(
        lambda pz, pc: blocks.at[pz, pc], lambda pz, pc: w_attn.at[x, pc, pz, y], ss, sr, local.at[1], nz, nc
    )
    tabs = Swap(lambda pz, pc: table, lambda pz, pc: tab.at[pz, pc], ts, tr, local.at[2], nz, nc)
    mlp_swap = Swap(
        lambda pz, pc: mlp_blocks.at[pz, pc], lambda pz, pc: mlp_t.at[pc, pz], us, ur, local.at[3], nz, nc
    )
    gu = Spread(lambda px, py: mlp_t, lambda px, py: w_mlp.at[px, :, :, py], ms, mr, local.at[4], nx, ny)
    first_rows = Gather(n1, n1g, gs, gr, gl)
    reduce = Reduce(part, held, came, rs, rr, rxs, rxr)
    cots = Gather(cot, cotg, cs, cr, cl)
    next_rows = Gather(n2, n2g, ns, nr, nl)
    met = greet(*dims)

    def pack(at):
        gain = gains[at, 0:1]
        for t in range(nz * nc):
            cols = slice(t * qcols, (t + 1) * qcols)
            blocks[t // nc, t % nc, at, :qcols] = (w_query[at, cols].astype(F32) * gain).astype(BF)
            blocks[t // nc, t % nc, at, qcols + 128 :] = w_out_t[at, cols]
        for pair in range(KV_HEADS // 2):
            cols = slice(pair * 128, pair * 128 + 128)
            key, value = w_key[at, cols].astype(F32) * gain, w_value[at, cols].astype(F32) * gain
            first = lanes(key.shape) < 64
            both = (
                jnp.where(first, key, pltpu.roll(value, 64, 1)),
                jnp.where(first, pltpu.roll(key, 64, 1), value),
            )
            for k in range(2):
                for rep in range(nz * nc // KV_HEADS):
                    t = (pair * 2 + k) * (nz * nc // KV_HEADS) + rep
                    blocks[t // nc, t % nc, at, qcols : qcols + 128] = both[k].astype(BF)

    def norm(at):
        value = tokens[at, :].astype(F32)
        inverse = lax.rsqrt(jnp.mean(value * value, axis=-1, keepdims=True) + EPSILON)
        n1[at, :] = (value * inverse).astype(BF)

    first_lanes = lanes((own, 128)) < 64
    gains[...] = jnp.where(first_lanes, column(gain_a[...].astype(F32)), column(gain_m[...].astype(F32)))
    by_rows(rows, norm)
    by_rows(own, pack)
    angle = column(positions[...].astype(F32)) * frequency[...]
    at = lanes(angle.shape)
    doc = jnp.broadcast_to(column(starts[...].astype(F32)), angle.shape)
    table[...] = jnp.where(at < 32, jnp.cos(angle), jnp.where(at < 64, jnp.sin(angle), doc))
    met()
    swap.start()
    tabs.start()
    dn.start()

    def spread_copies():
        for i, step in enumerate(others(nx, ny)):
            px, py = data_peer(step, nx, ny)
            slot = w_attn.at[x, :, :, y]
            yield remote(slot, slot, ds.at[i], dr.at[i], {"x": px, "y": py})

    def spread():
        swap.arrived()
        for copy in spread_copies():
            copy.start()

    def pack_mlp(at):
        gain = gains[at, 64:65]
        for k, weight in enumerate((w_gate, w_up)):
            for t in range(nz * nc):
                for i in range(nx):
                    chunk = (i * nc + t % nc) * nz + t // nc
                    to = (k * nx + i) * span
                    piece = weight[at, chunk * span : (chunk + 1) * span].astype(F32) * gain
                    mlp_blocks[t // nc, t % nc, at, to : to + span] = piece.astype(BF)

    end = flow(None, first_rows, None, [spread, lambda: by_rows(own, pack_mlp)])
    end()
    mlp_swap.start()
    keep_rows = pltpu.make_async_copy(n1g, n1_out, local.at[5])
    keep_rows.start()
    tabs.arrived()
    for copy in spread_copies():
        copy.wait_recv()
    keep_weights = pltpu.make_async_copy(w_attn, w_out, local.at[6])
    keep_weights.start()

    def project_kv(i, carry):
        u = nn(n1g[i].reshape(nc * rows, width), w_attn[..., qcols : qcols + 128].reshape(width, 128))
        cos, sin = rope_lanes(tab[i].reshape(nc * rows, 128))
        u = jnp.where(lanes(u.shape) < 64, u * cos + swap_halves(u) * sin, u).astype(BF)
        for pc in range(nc):
            kv[pc, i, y] = u[pc * rows : (pc + 1) * rows]
        return carry

    def project_q(i, carry):
        res = nn(n1g[i].reshape(nc * rows, width), w_attn[..., :qcols].reshape(width, qcols))
        cos, sin = rope_lanes(tab[i].reshape(nc * rows, 128))
        for p in range(pairs):
            u = res[:, p * 128 : p * 128 + 128]
            u = (u * cos + swap_halves(u) * sin) * (HEAD_DIM ** (-0.5))
            q[i, :, :, p * 128 : p * 128 + 128] = u.astype(BF).reshape(nc, rows, 128)
        return carry

    lax.fori_loop(0, nz, project_kv, 0)
    sends = []
    for i in range(ny - 1):
        slot = kv.at[:, :, y]
        sends.append(remote(slot, slot, ys.at[i], yr.at[i], {"y": lax.rem(y + 1 + i, ny)}))
    for copy in sends:
        copy.start()
    lax.fori_loop(0, nz, project_q, 0)
    for copy in sends:
        copy.wait_recv()

    def double(i, carry):
        pc, pz = i // nz, lax.rem(i, nz)
        u = kv[pc, pz].reshape(keys_span, 128).astype(F32)
        r = pltpu.roll(u, 64, 1)
        first = lanes(u.shape) < 64
        at = pl.ds(pl.multiple_of(pz * keys_span, keys_span), keys_span)
        kk[pc, at, :] = jnp.where(first, u, r).astype(BF)
        values = jnp.where(first, r, u)
        vv[pc, at, :] = values.astype(BF)
        vt[pc, :, at] = values.T.astype(BF)
        return carry

    lax.fori_loop(0, nc * nz, double, 0)

    def attend(pc, carry):
        for pz in range(nz):
            keys = (pz + 1) * keys_span
            bias = bias_of(tab[pz, pc], keys, (pz * ny + y) * rows)
            for p in range(pairs):
                q2 = two_heads(q[pz, pc, :, p * 128 : p * 128 + 128])
                s = nt(kk[pc, :keys, :], q2) + bias
                top = jnp.max(s, axis=0, keepdims=True)
                e = jnp.exp(s - top)
                total = jnp.sum(e, axis=0, keepdims=True)
                stat[pz, pc, p : p + 1, :] = top + jnp.log(total)
                weights = (e * (1.0 / total)).astype(BF)
                o = join_heads(nn(vt[pc, :, :keys], weights))
                ob[pz, pc, :, p * 128 : p * 128 + 128] = o.astype(BF)
        return carry

    lax.fori_loop(0, nc, attend, 0)

    def output(i, carry):
        half, odd = i // 2, lax.rem(i, 2)
        pz = odd * half + (1 - odd) * (nz - 1 - half)
        for px in range(nx):
            cols = slice(px * (width // nx), (px + 1) * (width // nx))
            weights = w_attn[px, :, :, :, :, qcols + 128 :].reshape(width // nx, qcols)
            res = nt(ob[pz].reshape(nc * rows, qcols), weights)
            part[pz, :, :, cols] = res.astype(BF).reshape(nc, rows, width // nx)
        reduce.across(pz).start()
        return carry

    lax.fori_loop(0, nz, output, 0)

    def spread_mlp():
        mlp_swap.arrived()
        gu.start()

    end2 = flow(reduce, cots, None, [spread_mlp])

    def settle(at, total):
        value = tokens[at, :].astype(F32) + total
        mid[at, :] = value
        inverse = lax.rsqrt(jnp.mean(value * value, axis=-1, keepdims=True) + EPSILON)
        n2[at, :] = (value * inverse).astype(BF)

    end3 = flow(None, next_rows, lambda half: reduce.last(half, settle))
    end3()
    end2()
    keep_rows.wait()
    keep_weights.wait()
    gu.arrived()
    dn.arrived()
    for one in (swap, tabs, mlp_swap, gu, dn):
        one.finish()
    for copy in list(spread_copies()) + sends:
        copy.wait_send()


def forward_call(
    dims, tokens, positions, starts, gain_a, gain_m, w_query, w_key, w_value, w_out_t, w_gate, w_up, down, cot
):
    nx, nc, nz, ny = dims
    rows, width = tokens.shape
    own = w_query.shape[0]
    qcols = HEADS // (nz * nc) * HEAD_DIM
    cols = 2 * qcols + 128
    peers, members = nx * ny - 1, nz * nc - 1
    mlp_cols = 2 * w_gate.shape[1] // (nz * nc)
    keys = nz * ny * rows
    team_rows = (nz, nc, rows, width)
    half = HEAD_DIM // 2
    exponents = np.tile(np.arange(half), 128 // half)[None, :] * (-2.0 / HEAD_DIM)
    frequency = jnp.asarray(10000.0**exponents, F32)
    return call(
        functools.partial(forward_kernel, dims),
        (
            tokens, positions, starts, gain_a, gain_m, frequency, w_query, w_key, w_value, w_out_t, w_gate, w_up,
            down, cot,
        ),
        (VM,) * 12 + (pl.ANY, VM),
        [
            ((own, 128), F32),
            (team_rows, BF),
            ((nx, nc, nz, ny, own, cols), BF),
            ((nz, nc, rows, 128), F32),
            ((nz, nc, rows, qcols), BF),
            ((nc, keys, 128), BF),
            ((nc, keys, 128), BF),
            ((nz, nc, 8, 2 * rows), F32),
            ((nz, nc, rows, qcols), BF),
            ((rows, width), F32),
            (team_rows, BF),
            (team_rows, BF),
            ((nx, nc, nz, ny, own, mlp_cols), BF),
            ((nx, ny) + down.shape, BF),
        ],
        (VM,) + (pl.ANY,) * 2 + (VM,) * 7 + (pl.ANY,) * 4,
        [
            VM(team_rows, BF),
            VM((nx, nc, nz, ny, own, cols), BF),
            VM((rows, 128), F32),
            VM((rows, width), BF),
            VM((nz, nc, own, cols), BF),
            VM((nz, nc, own, mlp_cols), BF),
            VM((nc, nz, own, mlp_cols), BF),
            VM((nc, nz, ny, rows, 128), BF),
            VM((nc, 128, keys), BF),
            VM(team_rows, BF),
        ]
        + Reduce.buffers(nz, rows, width)
        + [VM((rows, width), BF)]
        + Gather.SEMS
        + [DMA((members,))] * 4
        + [DMA((peers,))] * 4
        + [DMA((members,))] * 2
        + [DMA((max(ny - 1, 1),))] * 2
        + Reduce.SEMS
        + Gather.SEMS * 2
        + [DMA((peers,))] * 2
        + [DMA((7,))],
        1,
    )


def mlp_kernel(
    dims, n2g, cotg, w_mlp, w_dn, mid, cot,
    dx2, dag, output, came_mlp, grad_dn,
    n2v, cotv, wv, wd, hid, hid_t, dmlp, part, mlp_out, grad_mlp,
    held, came, held2, came2, low,
    loads, rs, rr, rxs, rxr, os, orr, oxs, oxr, ds, dr, dl, ms, mr, local,
):
    nx, nc, nz, ny = dims
    x, c, z, y = place()
    rows, width = mid.shape
    ff2 = wv.shape[-1]
    ff = ff2 // 2
    piece = wd.shape[2]
    block = nc * rows
    fetch_w = pltpu.make_async_copy(w_mlp, wv, loads.at[0])
    fetch_d = pltpu.make_async_copy(w_dn, wd, loads.at[1])
    fetch_w.start()

    def fetch(at, k):
        source, target = ((n2g, n2v), (cotg, cotv))[k]
        return pltpu.make_async_copy(source.at[at], target.at[at], loads.at[2 + k * nz + at])

    for k in range(nz):
        fetch(by_need(nz, z, k), 0).start()
        if k == 0:
            fetch_d.start()
        fetch(by_need(nz, z, k), 1).start()
    met = greet(*dims)
    reduce = Reduce(part, held, came, rs, rr, rxs, rxr)
    reduce2 = Reduce(mlp_out, held2, came2, os, orr, oxs, oxr)
    into = Gather(low, dag, ds, dr, dl)
    gu = Spread(
        lambda px, py: grad_mlp.at[px, :, :, py], lambda px, py: came_mlp.at[px, py], ms, mr, local.at[0], nx, ny
    )

    def down_rows(cols):
        if piece % ROWS:
            return jnp.concatenate([wd[px, py, :, cols] for px in range(nx) for py in range(ny)], axis=0)
        return wd[:, :, :, cols].reshape(ff, -1)

    def weights(px):
        return wv[px].reshape(width // nx, ff2)

    fetch_w.wait()

    def forward_back(k):
        at = by_need(nz, z, k)
        fetch(at, 0).wait()
        u = nn(n2v[at].reshape(block, width), wv[...].reshape(width, ff2))
        gt, up = u[:, :ff], u[:, ff:]
        sg = jax.nn.sigmoid(gt)
        silu = gt * sg
        value = (silu * up).astype(BF)
        hid[at] = value
        hid_t[:, pl.ds(pl.multiple_of(at * block, block), block)] = value.astype(F32).T.astype(BF)
        if k == 0:
            fetch_d.wait()
        fetch(at, 1).wait()
        dh = nt(cotv[at].reshape(block, width), down_rows(slice(None)))
        dgt = dh * up * sg * (1.0 + gt * (1.0 - sg))
        dmlp[at] = jnp.concatenate([dgt, dh * silu], axis=1).astype(BF)

        for px in range(nx):
            cols = slice(px * (width // nx), (px + 1) * (width // nx))
            res = nt(dmlp[at], weights(px))
            part[at, :, :, cols] = res.astype(BF).reshape(nc, rows, width // nx)
        if k == 0:
            met()
        reduce.across(at).start()

    forward_back(0)
    chunk = width // 4

    def down_grad(n, carry):
        cols = pl.ds(pl.multiple_of(n * chunk, chunk), chunk)
        res = nn(hid_t[...], cotv[:, :, :, cols].reshape(nz * block, chunk)).astype(BF)
        for px in range(nx):
            for py in range(ny):
                k = (px * ny + py) * piece
                grad_dn[px, py, :, cols] = res[k : k + piece]
        return carry

    def mlp_grad(far):
        px = lax.rem(x + far, nx)
        size = width // (nx * 4)

        def body(j, carry):
            cols = pl.ds(pl.multiple_of(px * (width // nx) + j * size, size), size)
            res = tn(n2v[:, :, :, cols].reshape(nz * block, size), dmlp[...].reshape(nz * block, ff2))
            own = grad_mlp.shape[4]
            grad_mlp[px, j // 2, pl.ds(lax.rem(j, 2) * (nz // 2), nz // 2)] = res.astype(BF).reshape(
                nz // 2, ny, own, ff2
            )
            return carry

        lax.fori_loop(0, 4, body, 0)
        gu.start_along(far)

    def mlp_sum(n, carry):
        cols = pl.ds(pl.multiple_of(n * chunk, chunk), chunk)
        res = nn(hid[...].reshape(nz * block, ff), down_rows(cols))
        mlp_out[:, :, :, cols] = res.astype(BF).reshape(nz, nc, rows, chunk)
        return carry

    def down_first():
        lax.fori_loop(0, 2, down_grad, 0)

    def down_second():
        lax.fori_loop(2, 4, down_grad, 0)

    def sum_all():
        lax.fori_loop(0, 4, mlp_sum, 0)
        reduce2.start()

    def other_blocks():
        for k in range(2, nz):
            forward_back(k)

    forward_back(1)
    work = [other_blocks] + [functools.partial(mlp_grad, far) for far in reversed(range(nx))]
    end = flow(reduce, None, None, work + [sum_all])

    def settle(at, total):
        value = mid[at, :]
        inverse = lax.rsqrt(jnp.mean(value * value, axis=-1, keepdims=True) + EPSILON)
        normed = value * inverse
        gradient = cot[at, :].astype(F32) + inverse * (
            total - normed * jnp.mean(total * normed, axis=-1, keepdims=True)
        )
        dx2[at, :] = gradient
        low[at, :] = gradient.astype(BF)

    end2 = flow(reduce2, into, lambda part: reduce.last(part, settle), [down_first, down_second])

    def finish(at, total):
        output[at, :] = (mid[at, :] + total).astype(BF)

    for half in range(PARTS):
        reduce2.last(half, finish)
    end2()
    end()
    gu.arrived()
    gu.finish()


def mlp_call(dims, n2g, cotg, w_mlp, w_dn, mid, cot):
    nx, nc, nz, ny = dims
    rows, width = mid.shape
    own, ff2 = w_mlp.shape[4:]
    block = nc * rows
    peers = nx * ny - 1
    return call(
        functools.partial(mlp_kernel, dims),
        (n2g, cotg, w_mlp, w_dn, mid, cot),
        (pl.ANY, pl.ANY, pl.ANY, pl.ANY, VM, VM),
        [
            ((rows, width), F32),
            ((nz, nc, rows, width), BF),
            ((rows, width), BF),
            ((nx, ny, nc, nz, own, ff2), BF),
            (w_dn.shape, BF),
        ],
        (VM, pl.ANY, VM, pl.ANY, VM),
        [
            VM(n2g.shape, BF),
            VM(cotg.shape, BF),
            VM(w_mlp.shape, BF),
            VM(w_dn.shape, BF),
            VM((nz, block, ff2 // 2), BF),
            VM((ff2 // 2, nz * block), BF),
            VM((nz, block, ff2), BF),
            VM(n2g.shape, BF),
            VM(n2g.shape, BF),
            VM(w_mlp.shape, BF),
        ]
        + Reduce.buffers(nz, rows, width) * 2
        + [VM((rows, width), BF), DMA((2 + 2 * nz,))]
        + Reduce.SEMS * 2
        + Gather.SEMS
        + [DMA((peers,))] * 2
        + [DMA((1,))],
        3,
    )


def backward_kernel(
    dims, dag, w_in, tab_in, q_in, kk_in, vv_in, stat_in, ob_in, came_mlp, grad_dn, n1g,
    dn1, raw_gate, raw_up, came_dn, own_o, own_p,
    w, tab, q, kk, vv, stat, ob, do, kt, dk, dv, out, near, dqkv, part, team, stage, mlp_sum, mlp_g,
    grad_o, came_o, sums_o, grad_p, came_p, sums_p,
    held, came,
    ins, loads, us, ur, ys, yr, ws, wr, rs, rr, rxs, rxr, ds, dr, ss, sr, es, er, fs, fr, local,
):
    nx, nc, nz, ny = dims
    x, c, z, y = place()
    rows, width = dn1.shape
    own = grad_o.shape[4]
    qcols = q.shape[-1]
    pairs = qcols // 128
    keys_span = ny * rows
    fetch_dag = pltpu.make_async_copy(dag, team, loads.at[2])
    fetch = pltpu.make_async_copy(n1g, team, loads.at[2])
    pairs_in = zip((w_in, kk_in, q_in, tab_in, stat_in, vv_in, ob_in), (w, kk, q, tab, stat, vv, ob))
    fetch_rest = [pltpu.make_async_copy(a, b, ins.at[i]) for i, (a, b) in enumerate(pairs_in)]
    mlp_swap = Swap(
        lambda pz, pc: mlp_sum.at[pz, pc], lambda pz, pc: mlp_g.at[pz, pc], us, ur, local.at[0], nz, nc
    )
    dn = Spread(lambda px, py: grad_dn.at[px, py], lambda px, py: came_dn.at[px, py], ws, wr, local.at[1], nx, ny)
    reduce = Reduce(part, held, came, rs, rr, rxs, rxr)
    spread_o = Spread(
        lambda px, py: grad_o.at[px, :, :, py], lambda px, py: came_o.at[px, py], ds, dr, local.at[2], nx, ny
    )
    swap_o = Swap(lambda pz, pc: sums_o.at[pz, pc], lambda pz, pc: own_o.at[pz, pc], ss, sr, local.at[3], nz, nc)
    spread_p = Spread(
        lambda px, py: grad_p.at[px, :, :, py], lambda px, py: came_p.at[px, py], es, er, local.at[4], nx, ny
    )
    swap_p = Swap(lambda pz, pc: sums_p.at[pz, pc], lambda pz, pc: own_p.at[pz, pc], fs, fr, local.at[5], nz, nc)

    steps = others(nz, nc) + [(0, 0)]

    def load(i):
        pz, pc = team_peer(steps[i], nz, nc)
        return pltpu.make_async_copy(came_mlp.at[:, :, pc, pz], stage.at[i % 2], loads.at[i % 2])

    load(0).start()
    fetch_dag.start()
    for copy in fetch_rest:
        copy.start()
    met = greet(*dims, cross=True)
    early = 2 * (nx * ny - 1) // 3
    for i, copy in enumerate(list(mlp_swap.copies()) + [mlp_swap.own()]):
        if i + 1 < len(steps):
            load(i + 1).start()
        load(i).wait()
        pz, pc = team_peer(steps[i], nz, nc)

        def add(at, i=i, pz=pz, pc=pc):
            total = stage[i % 2, 0, 0, at, :].astype(F32)
            for px, py in others(nx, ny):
                total = total + stage[i % 2, px, py, at, :].astype(F32)
            mlp_sum[pz, pc, at, :] = total.astype(BF)

        by_rows(own, add)
        if i == 0:
            met()
            dn.start_some(0, early)
            dn.own().start()
        copy.start()
    fetch_dag.wait()
    for copy in fetch_rest:
        copy.wait()

    def turned(i, carry):
        pc, pz = i // nz, lax.rem(i, nz)
        at = pl.ds(pl.multiple_of(pz * keys_span, keys_span), keys_span)
        kt[pc, :, at] = kk[pc, at, :].astype(F32).T.astype(BF)
        return carry

    lax.fori_loop(0, nc * nz, turned, 0)

    def project(i, carry):
        weights = w[..., qcols + 128 :].reshape(width, qcols)
        do[i] = nn(team[i].reshape(nc * rows, width), weights).astype(BF).reshape(nc, rows, qcols)
        return carry

    lax.fori_loop(0, nz, project, 0)

    def attend(pc, carry):
        for pz in reversed(range(nz)):
            keys = (pz + 1) * keys_span
            most = KEYS if nz * keys_span <= KEYS else KEYS // 4
            cuts = [slice(a, min(a + most, keys)) for a in range(0, keys, most)]

            def bias_at(i, cuts=cuts, pz=pz):
                cut = cuts[i]
                return bias_of(tab[pz, pc], cut.stop - cut.start, (pz * ny + y) * rows, cut.start)

            only = bias_at(0) if len(cuts) == 1 else None
            cos, sin = rope_lanes(tab[pz, pc])
            for p in range(pairs):
                q2 = two_heads(q[pz, pc, :, p * 128 : p * 128 + 128])
                do2 = two_heads(do[pz, pc, :, p * 128 : p * 128 + 128])

                def scores(i, cuts=cuts, only=only, bias_at=bias_at, q2=q2, do2=do2, p=p, pz=pz):
                    s = nt(kk[pc, cuts[i], :], q2) + (bias_at(i) if only is None else only)
                    weights = jnp.exp(s - stat[pz, pc, p : p + 1, :])
                    return weights, weights * nt(vv[pc, cuts[i], :], do2)

                delta = sum(jnp.sum(scores(i)[1], axis=0, keepdims=True) for i in range(1, len(cuts)))
                u = 0.0
                for i, cut in enumerate(cuts):
                    weights, dw = scores(i)
                    if i == 0:
                        delta = delta + jnp.sum(dw, axis=0, keepdims=True)
                    score_grad = (dw - weights * delta).astype(BF)
                    dv_new = nn(weights.astype(BF), do2)
                    dk_new = nn(score_grad, q2)
                    if pz == nz - 1 and p == 0:
                        dv[pc, cut, :] = dv_new
                        dk[pc, cut, :] = dk_new
                    else:
                        dv[pc, cut, :] += dv_new
                        dk[pc, cut, :] += dk_new
                    u = u + nn(kt[pc, :, cut], score_grad)
                u = join_heads(u) * (HEAD_DIM ** (-0.5))
                u = u * cos - swap_halves(u) * sin
                dqkv[pz, pc, :, p * 128 : p * 128 + 128] = u.astype(BF)
        return carry

    lax.fori_loop(0, nc, attend, 0)

    def fold(i, carry):
        pc, pz = i // nz, lax.rem(i, nz)
        at = pl.ds(pl.multiple_of(pz * keys_span, keys_span), keys_span)
        key, value = dk[pc, at, :], dv[pc, at, :]
        first = lanes(key.shape) < 64
        both = jnp.where(first, key + pltpu.roll(key, 64, 1), value + pltpu.roll(value, 64, 1))
        both = both.astype(BF)
        for py in range(ny):
            out[pc, py, pz] = both[py * rows : (py + 1) * rows]
        return carry

    lax.fori_loop(0, nc * nz, fold, 0)
    sends = []
    for i, (sy, sc) in enumerate(others(ny, nc)):
        py, pc = lax.rem(y + sy, ny), lax.rem(c + sc, nc)
        sends.append(remote(out.at[pc, py], near.at[i], ys.at[i], yr.at[i], {"y": py, "core": pc}))
    for copy in sends:
        copy.start()

    def weight_grad(right, target):
        def body(j, carry):
            px, k = j // 4, lax.rem(j, 4)
            size = width // (nx * 4)
            cols = pl.ds(pl.multiple_of(j * size, size), size)
            res = tn(team[:, :, :, cols].reshape(nz * nc * rows, size), right.reshape(nz * nc * rows, -1))
            target[px, k // 2, pl.ds(lax.rem(k, 2) * (nz // 2), nz // 2)] = res.astype(BF).reshape(
                nz // 2, ny, own, -1
            )
            return carry

        lax.fori_loop(0, nx * 4, body, 0)

    weight_grad(ob[...], grad_o)
    fetch.start()
    for copy in sends:
        copy.wait_recv()
    spread_o.start()

    def settle_kv(pz, carry):
        total = out[c, y, pz].astype(F32)
        for i in range(len(sends)):
            total = total + near[i, pz].astype(F32)
        cos, sin = rope_lanes(tab[pz, c])
        first = lanes(total.shape) < 64
        total = jnp.where(first, total * cos - swap_halves(total) * sin, total)
        dqkv[pz, c, :, qcols : qcols + 128] = total.astype(BF)
        dqkv[pz, 1 - c, :, qcols : qcols + 128] = jnp.zeros((rows, 128), BF)
        return carry

    lax.fori_loop(0, nz, settle_kv, 0)

    def output(i, carry):
        half, odd = i // 2, lax.rem(i, 2)
        pz = odd * half + (1 - odd) * (nz - 1 - half)
        for px in range(nx):
            cols = slice(px * (width // nx), (px + 1) * (width // nx))
            weights = w[px, :, :, :, :, : qcols + 128].reshape(width // nx, qcols + 128)
            res = nt(dqkv[pz].reshape(nc * rows, qcols + 128), weights)
            part[pz, :, :, cols] = res.astype(BF).reshape(nc, rows, width // nx)
        reduce.across(pz).start()
        return carry

    lax.fori_loop(0, nz, output, 0)

    def own_weights():
        fetch.wait()
        weight_grad(dqkv[...], grad_p)
        spread_p.start()

    def unpack_mlp(at):
        span = mlp_g.shape[-1] // (2 * nx)
        for k, raw in enumerate((raw_gate, raw_up)):
            for t in range(nz * nc):
                for i in range(nx):
                    chunk = (i * nc + t % nc) * nz + t // nc
                    piece = mlp_g[t // nc, t % nc, at, (k * nx + i) * span : (k * nx + i + 1) * span]
                    raw[at, chunk * span : (chunk + 1) * span] = piece

    def unpack_all():
        mlp_swap.arrived()
        by_rows(own, unpack_mlp)

    def down_rest():
        dn.start_some(early, nx * ny - 1)

    def exchange(spread, arrived, sums, swap):
        spread.arrived()

        def add(at):
            for pz in range(nz):
                for pc in range(nc):
                    total = arrived[0, 0, pc, pz, at, :].astype(F32)
                    for px, py in others(nx, ny):
                        total = total + arrived[px, py, pc, pz, at, :].astype(F32)
                    sums[pz, pc, at, :] = total.astype(BF)

        by_rows(own, add)
        swap.start()

    work = [
        own_weights,
        unpack_all,
        down_rest,
        functools.partial(exchange, spread_o, came_o, sums_o, swap_o),
        functools.partial(exchange, spread_p, came_p, sums_p, swap_p),
    ]
    end = flow(reduce, None, None, work)

    def settle(at, total):
        dn1[at, :] = total

    for half in range(PARTS):
        reduce.last(half, settle)
    end()
    for one in (dn, swap_o, swap_p):
        one.arrived()
    for one in (mlp_swap, dn, spread_o, swap_o, spread_p, swap_p):
        one.finish()
    for copy in sends:
        copy.wait_send()


def backward_call(dims, dag, w, tab, q, kk, vv, stat, ob, came_mlp, grad_dn, n1g):
    nx, nc, nz, ny = dims
    rows, width = dag.shape[2:]
    own, mlp_cols = came_mlp.shape[4:]
    qcols = q.shape[-1]
    keys = nz * ny * rows
    peers, members, near = nx * ny - 1, nz * nc - 1, ny * nc - 1
    team_rows = (nz, nc, rows, width)
    return call(
        functools.partial(backward_kernel, dims),
        (dag, w, tab, q, kk, vv, stat, ob, came_mlp, grad_dn, n1g),
        (pl.ANY,) * 11,
        [
            ((rows, width), F32),
            ((own, mlp_cols // 2 * nz * nc), BF),
            ((own, mlp_cols // 2 * nz * nc), BF),
            (grad_dn.shape, BF),
            ((nz, nc, own, qcols), BF),
            ((nz, nc, own, qcols + 128), BF),
        ],
        (VM,) * 3 + (pl.ANY,) * 3,
        [VM(a.shape, a.dtype) for a in (w, tab, q, kk, vv, stat, ob)]
        + [
            VM((nz, nc, rows, qcols), BF),
            VM((nc, 128, keys), BF),
            VM((nc, keys, 128), F32),
            VM((nc, keys, 128), F32),
            VM((nc, ny, nz, rows, 128), BF),
            VM((near, nz, rows, 128), BF),
            VM((nz, nc, rows, qcols + 128), BF),
            VM(team_rows, BF),
            VM(team_rows, BF),
            VM((2, nx, ny, own, mlp_cols), BF),
            VM((nz, nc, own, mlp_cols), BF),
            VM((nz, nc, own, mlp_cols), BF),
        ]
        + [
            VM(shape + (own, n), BF)
            for n in (qcols, qcols + 128)
            for shape in ((nx, nc, nz, ny), (nx, ny, nc, nz), (nz, nc))
        ]
        + Reduce.buffers(nz, rows, width)
        + [DMA((7,)), DMA((3,))]
        + [DMA((members,))] * 2
        + [DMA((near,))] * 2
        + [DMA((peers,))] * 2
        + Reduce.SEMS
        + ([DMA((peers,))] * 2 + [DMA((members,))] * 2) * 2
        + [DMA((6,))],
        6,
    )


def final_kernel(
    dims, low, dn1, tokens, dx2, raw_gate, raw_up, came_dn, own_o, own_p, gains, w_query, w_key, w_value, w_gate, w_up,
    output, input_grad, grad_query, grad_key, grad_value, grad_out_t, grad_gate, grad_up, grad_down, grad_gain,
):
    nx, nc, nz, ny = dims
    team = nz * nc
    output[...] = low[...]
    value = tokens[...].astype(F32)
    total = dn1[...]
    inverse = lax.rsqrt(jnp.mean(value * value, axis=-1, keepdims=True) + EPSILON)
    normed = value * inverse
    input_grad[...] = dx2[...] + inverse * (total - normed * jnp.mean(total * normed, axis=-1, keepdims=True))

    down = came_dn[0, 0].astype(F32)
    for px, py in others(nx, ny):
        down = down + came_dn[px, py].astype(F32)
    grad_down[...] = down

    gain = gains[:, 64:65]
    both = 0.0
    for raw, weight, grad in ((raw_gate, w_gate, grad_gate), (raw_up, w_up, grad_up)):
        got = raw[...].astype(F32)
        grad[...] = got * gain
        both = both + got * weight[...].astype(F32)
    dots_mlp = jnp.sum(both, axis=-1, keepdims=True)

    gain = gains[:, 0:1]
    qcols = own_o.shape[-1]
    both = 0.0
    heads = []
    for t in range(team):
        block = own_p[t // nc, t % nc].astype(F32)
        cols = slice(t * qcols, (t + 1) * qcols)
        grad_out_t[:, cols] = own_o[t // nc, t % nc].astype(F32)
        grad_query[:, cols] = block[:, :qcols] * gain
        both = both + block[:, :qcols] * w_query[:, cols].astype(F32)
        if t % (team // KV_HEADS):
            heads[-1] = heads[-1] + block[:, qcols:]
        else:
            heads.append(block[:, qcols:])
    dots = jnp.sum(both, axis=-1, keepdims=True)
    for pair in range(KV_HEADS // 2):
        one, two = heads[2 * pair], heads[2 * pair + 1]
        first = lanes(one.shape) < 64
        cols = slice(pair * 128, pair * 128 + 128)
        key = jnp.where(first, one, pltpu.roll(two, 64, 1))
        val = jnp.where(first, pltpu.roll(one, 64, 1), two)
        grad_key[:, cols] = key * gain
        grad_value[:, cols] = val * gain
        both = key * w_key[:, cols].astype(F32) + val * w_value[:, cols].astype(F32)
        dots = dots + jnp.sum(both, axis=-1, keepdims=True)
    shape = grad_gain.shape
    grad_gain[...] = jnp.where(lanes(shape) < 64, dots, dots_mlp)


def final_call(
    dims, low, dn1, tokens, dx2, raw_gate, raw_up, came_dn, own_o, own_p, gains,
    w_query, w_key, w_value, w_gate, w_up,
):
    own = w_query.shape[0]
    steps = max(own // ROWS, 1)

    def rows_of(shape, axis):
        count = shape[axis]
        each = count if steps == 1 else -(-count // (steps * ROWS)) * ROWS
        block = shape[:axis] + (each,) + shape[axis + 1 :]
        return pl.BlockSpec(block, lambda i: tuple(i if k == axis else 0 for k in range(len(shape))))

    operands = (
        low, dn1, tokens, dx2, raw_gate, raw_up, came_dn, own_o, own_p, gains, w_query, w_key, w_value, w_gate, w_up
    )
    outs = [
        low.shape, dn1.shape, w_query.shape, w_key.shape, w_value.shape, w_query.shape, w_gate.shape, w_up.shape,
        came_dn.shape[2:], (own, 128),
    ]
    return pl.pallas_call(
        functools.partial(final_kernel, dims),
        grid=(steps,),
        out_shape=[jax.ShapeDtypeStruct(s, BF if i == 0 else F32) for i, s in enumerate(outs)],
        in_specs=[rows_of(a.shape, len(a.shape) - 2) for a in operands],
        out_specs=[rows_of(s, 0) for s in outs],
        compiler_params=pltpu.CompilerParams(vmem_limit_bytes=60 << 20),
    )(*operands)


def shards(
    tokens, positions, doc_start, cotangent, w_query, w_key, w_value, w_out,
    attn_gain, w_gate, w_up, w_down, mlp_gain,
):
    dims = tuple(lax.axis_size(a) for a in ALL)
    gains, n1g, w_attn, tab, q, kk, vv, stat, ob, mid, n2g, cotg, w_mlp, w_dn = forward_call(
        dims, tokens, positions[None], doc_start[None], attn_gain[None], mlp_gain[None],
        w_query, w_key, w_value, w_out.T, w_gate, w_up, w_down, cotangent,
    )
    dx2, dag, output, came_mlp, grad_dn = mlp_call(dims, n2g, cotg, w_mlp, w_dn, mid, cotangent)
    dn1, raw_gate, raw_up, came_dn, own_o, own_p = backward_call(
        dims, dag, w_attn, tab, q, kk, vv, stat, ob, came_mlp, grad_dn, n1g
    )
    (
        output, input_grad, grad_query, grad_key, grad_value, grad_out_t, grad_gate, grad_up, grad_down, grad_gain
    ) = final_call(
        dims, output, dn1, tokens, dx2, raw_gate, raw_up, came_dn, own_o, own_p, gains,
        w_query, w_key, w_value, w_gate, w_up,
    )
    return (
        output, input_grad, grad_query, grad_key, grad_value, grad_out_t.T, grad_gain[:, 0],
        grad_gate, grad_up, grad_down, grad_gain[:, 64],
    )


def solution(mesh):
    fsdp, seq = mesh.shape["fsdp"], mesh.shape["seq"]
    nc, nz = 2, 4
    grid = Mesh(mesh.devices.reshape(fsdp // nc, nc, nz, seq // nz), ALL)
    row, col, vec = P(ALL, None), P(None, ALL), P(ALL)
    in_specs = (row, vec, vec, row, row, row, row, col, vec, row, row, row, vec)
    out_specs = (row, row, row, row, row, col, vec, row, row, row, vec)
    return jax.shard_map(shards, mesh=grid, in_specs=in_specs, out_specs=out_specs, check_vma=False)
```

```python
import functools

import jax
import jax.numpy as jnp
import numpy as np
from jax import lax
from jax.experimental import pallas as pl
from jax.experimental.pallas import tpu as pltpu
from jax.sharding import Mesh
from jax.sharding import PartitionSpec as P

HEADS = 32
KV_HEADS = 4
HEAD_DIM = 64
EPSILON = 1e-05
MASKED = -1e30
ALL = ("x", "core", "z", "y")
TEAM = ("z", "core")
DATA = ("x", "y")
BF = jnp.bfloat16
F32 = jnp.float32


MESH = pl.DeviceIdType.MESH
VM = pltpu.VMEM
DMA = pltpu.SemaphoreType.DMA
ROWS = 16
PARTS = 2
WINDOW = 2
KEYS = 1024


def place():
    return tuple(lax.axis_index(a) for a in ALL)


def others(nx, ny):
    return [(i, j) for i in range(nx) for j in range(ny) if (i, j) != (0, 0)]


def data_peer(step, nx, ny):
    x, _, _, y = place()
    return lax.rem(x + step[0], nx), lax.rem(y + step[1], ny)


def team_peer(step, nz, nc):
    _, c, z, _ = place()
    return lax.rem(z + step[0], nz), lax.rem(c + step[1], nc)


def greet(nx, nc, nz, ny, cross=False):
    barrier = pltpu.get_barrier_semaphore()
    x, c, z, y = place()
    extra = ny - 1 if cross else 0
    for i in range(extra):
        device = {"y": lax.rem(y + 1 + i, ny), "core": 1 - c}
        pl.semaphore_signal(barrier, inc=1, device_id=device, device_id_type=MESH)
    for step in others(nx, ny):
        px, py = data_peer(step, nx, ny)
        pl.semaphore_signal(barrier, inc=1, device_id={"x": px, "y": py}, device_id_type=MESH)
    for step in others(nz, nc):
        pz, pc = team_peer(step, nz, nc)
        pl.semaphore_signal(barrier, inc=1, device_id={"z": pz, "core": pc}, device_id_type=MESH)

    def met():
        pl.semaphore_wait(barrier, nx * ny - 1 + nz * nc - 1 + extra)

    return met


def remote(source, target, send, recv, device):
    return pltpu.make_async_remote_copy(
        src_ref=source, dst_ref=target, send_sem=send, recv_sem=recv,
        device_id=device, device_id_type=MESH,
    )


def piece_of(part, rows):
    return pl.ds(part * (rows // PARTS), rows // PARTS)


class Gather:
    SEMS = [DMA((3, 4, PARTS)), DMA((2, 4, PARTS)), DMA((PARTS,))]

    def __init__(self, own, full, send, recv, local):
        self.own, self.full, self.send, self.recv, self.local = own, full, send, recv, local
        self.x, self.c, self.z, self.y = place()
        self.nz, _, self.rows = full.shape[:3]

    def copy(self, at, kind, part, mine=False):
        rows = piece_of(part, self.rows)
        slot = self.full.at[at, self.c, rows]
        device = ({"z": self.z + 1}, {"z": self.z - 1}, {"core": 1 - self.c})[kind]
        return remote(
            self.own.at[rows] if mine else slot, slot, self.send.at[kind, at, part],
            self.recv.at[0 if kind < 2 else 1, at, part], device,
        )

    def keep(self, part):
        rows = piece_of(part, self.rows)
        return pltpu.make_async_copy(self.own.at[rows], self.full.at[self.z, self.c, rows], self.local.at[part])

    def begin(self, part):
        self.keep(part).start()
        self.copy(self.z, 2, part, True).start()

    def finish(self):
        for part in range(PARTS):
            self.keep(part).wait()
            for at in range(self.nz):
                self.copy(at, 2, part).wait_send()
                self.copy(at, 2, part).wait_recv()


class Reduce:
    SEMS = [DMA((2, 4, PARTS)), DMA((2, 4, PARTS)), DMA((4,)), DMA((4,))]

    @staticmethod
    def buffers(nz, rows, width):
        return [VM((nz, rows, width), BF), VM((2, nz - 1, rows, width), BF)]

    def __init__(self, part, held, came, send, recv, across_send, across_recv):
        self.part, self.held, self.came, self.send, self.recv = part, held, came, send, recv
        self.across_send, self.across_recv = across_send, across_recv
        self.x, self.c, self.z, self.y = place()
        self.nz, _, self.rows, self.width = part.shape

    def across(self, to):
        return remote(
            self.part.at[to, 1 - self.c], self.held.at[to], self.across_send.at[to], self.across_recv.at[to],
            {"core": 1 - self.c},
        )

    def along(self, to, way, part):
        device = ({"z": self.z + 1}, {"z": self.z - 1})[way]
        rows = piece_of(part, self.rows)
        return remote(
            self.held.at[to, rows], self.came.at[way, to - 1 + way, rows], self.send.at[way, to, part],
            self.recv.at[way, to, part], device,
        )

    def start(self):
        for to in [a for k in range(self.nz) for a in (self.nz - 1 - k, k)][: self.nz]:
            self.across(to).start()

    def add(self, to, ways, part, out=None):
        size = self.rows // PARTS

        def body(i, carry):
            at = pl.ds(pl.multiple_of(part * size + i * ROWS, ROWS), ROWS)
            total = self.part[to, self.c, at, :].astype(F32) + self.held[to, at, :].astype(F32)
            for way in ways:
                total = total + self.came[way, to - 1 + way, at, :].astype(F32)
            if out is None:
                self.held[to, at, :] = total.astype(BF)
            else:
                out(at, total)
            return carry

        lax.fori_loop(0, size // ROWS, body, 0)

    def last(self, part, out):
        if part == 0:
            self.across(self.z).wait_recv()
        for at in range(self.nz):

            @pl.when(self.z == at)
            def _(at=at):
                ways = ([0] if at > 0 else []) + ([1] if at < self.nz - 1 else [])
                for way in ways:
                    self.along(at, way, part).wait_recv()
                self.add(at, ways, part, out)

    def finish(self):
        for to in range(self.nz):
            self.across(to).wait_send()


def plan(nz, reduces, gathers):
    last = nz - 1
    rows = []
    for e in range(nz):
        sums = [("R", last - k) for k in range(last) if last - k > e]
        blocks = [("G", e - k) for k in range(e + 1)]
        if reduces and gathers:
            if e == last:
                rows.append([None] + blocks[1:-1] + [None] + blocks[-1:])
            else:
                woven = blocks[:-1] + sums[:1] + blocks[-1:] + sums[1:]
                rows.append(woven)
        elif reduces:
            rows.append([None] * e + sums)
        else:
            rows.append(blocks if e < last else [None] + blocks[1:])
    return rows


def by_need(nz, z, k):
    last = nz - 1
    value = 0
    for at in range(nz):
        when = {to: at + last - to if to > at else last - at + to for to in range(nz) if to != at}
        blocks = sorted(when, key=lambda to: (when[to], to)) + [at]
        value = jnp.where(z == at, blocks[k], value)
    return value


def flow(reduce, gather, before=None, work=()):
    work = list(work)
    any_one = reduce or gather
    nz, z = any_one.nz, any_one.z
    table = plan(nz, reduce is not None, gather is not None)
    pending = {(way, e): [] for way in (0, 1) for e in range(nz)}

    def pace(key, make):
        queue = pending[key]
        if len(queue) >= WINDOW:
            queue.pop(0)().wait_send()
        make().start()
        queue.append(make)

    def step(way, e, kind, place_at, part):
        block = place_at if way == 0 else nz - 1 - place_at
        if kind == "R":
            if part == 0:
                reduce.across(block).wait_recv()
            if e > 0:
                reduce.along(block, way, part).wait_recv()
            reduce.add(block, (way,) if e > 0 else (), part)
            pace((way, e), functools.partial(reduce.along, block, way, part))
        else:
            mine = place_at == e
            if not mine:
                gather.copy(block, way, part).wait_recv()
            if e < nz - 1:
                pace((way, e), functools.partial(gather.copy, block, way, part, mine))
            if not mine:
                gather.copy(block, 2, part).start()

    for t in range(max(len(row) for row in table)):
        for part in range(PARTS):
            if t == 0 and before is not None:
                before(part)
            if t == 0 and gather is not None:
                gather.begin(part)
            for way in (0, 1):
                for e in range(nz):
                    op = table[e][t] if t < len(table[e]) else None
                    if op is not None:
                        pl.when(z == (e if way == 0 else nz - 1 - e))(
                            functools.partial(step, way, e, op[0], op[1], part)
                        )
            if work and (t > 0 or part == PARTS - 1):
                work.pop(0)()
    for item in work:
        item()

    def finish():
        for (way, e), queue in pending.items():
            if queue:

                @pl.when(z == (e if way == 0 else nz - 1 - e))
                def _(queue=queue):
                    for make in queue:
                        make().wait_send()

        for one in (reduce, gather):
            if one is not None:
                one.finish()

    return finish


class Spread:
    def __init__(self, source, target, send, recv, local, nx, ny):
        self.source, self.target, self.send, self.recv = source, target, send, recv
        self.nx, self.ny = nx, ny
        self.x, _, _, self.y = place()
        self.own = lambda: pltpu.make_async_copy(source(self.x, self.y), target(self.x, self.y), local)

    def copies(self):
        for i, step in enumerate(others(self.nx, self.ny)):
            px, py = data_peer(step, self.nx, self.ny)
            yield remote(
                self.source(px, py), self.target(self.x, self.y), self.send.at[i], self.recv.at[i],
                {"x": px, "y": py},
            )

    def start(self):
        for copy in self.copies():
            copy.start()
        self.own().start()

    def start_some(self, first, last):
        for i, copy in enumerate(self.copies()):
            if first <= i < last:
                copy.start()

    def start_along(self, far):
        for step, copy in zip(others(self.nx, self.ny), self.copies()):
            if step[0] == far:
                copy.start()
        if far == 0:
            self.own().start()

    def arrived(self):
        self.own().wait()
        for copy in self.copies():
            copy.wait_recv()

    def finish(self):
        for copy in self.copies():
            copy.wait_send()


class Swap:
    def __init__(self, source, slot, send, recv, local, nz, nc):
        self.source, self.slot, self.send, self.recv, self.nz, self.nc = source, slot, send, recv, nz, nc
        _, self.c, self.z, _ = place()
        self.own = lambda: pltpu.make_async_copy(source(self.z, self.c), slot(self.z, self.c), local)

    def copies(self):
        for i, step in enumerate(others(self.nz, self.nc)):
            pz, pc = team_peer(step, self.nz, self.nc)
            yield remote(
                self.source(pz, pc), self.slot(self.z, self.c), self.send.at[i], self.recv.at[i],
                {"z": pz, "core": pc},
            )

    def start(self):
        for copy in self.copies():
            copy.start()
        self.own().start()

    def arrived(self):
        self.own().wait()
        for copy in self.copies():
            copy.wait_recv()

    def finish(self):
        for copy in self.copies():
            copy.wait_send()


def call(kernel, operands, in_spaces, outs, out_spaces, scratch, number):
    return pl.pallas_call(
        kernel,
        out_shape=[jax.ShapeDtypeStruct(s, t) for s, t in outs],
        in_specs=[pl.BlockSpec(memory_space=s) for s in in_spaces],
        out_specs=[pl.BlockSpec(memory_space=s) for s in out_spaces],
        scratch_shapes=scratch,
        compiler_params=pltpu.CompilerParams(
            collective_id=number, has_side_effects=True, vmem_limit_bytes=60 << 20
        ),
    )(*operands)


def lanes(shape):
    return lax.broadcasted_iota(jnp.int32, shape, len(shape) - 1)


def by_rows(count, body):
    if count % ROWS or count == ROWS:
        body(slice(0, count))
    else:

        def step(i, carry):
            body(pl.ds(pl.multiple_of(i * ROWS, ROWS), ROWS))
            return carry

        lax.fori_loop(0, count // ROWS, step, 0)


def nt(a, b):
    return lax.dot_general(a, b, (((1,), (1,)), ((), ())), preferred_element_type=F32)


def nn(a, b):
    return jnp.dot(a, b, preferred_element_type=F32)


def tn(a, b):
    return lax.dot_general(a, b, (((0,), (0,)), ((), ())), preferred_element_type=F32)


def column(row):
    count = row.shape[1]
    down = lax.broadcasted_iota(jnp.int32, (count, count), 0)
    return jnp.sum(jnp.where(down == lanes((count, count)), row, 0.0), axis=1, keepdims=True)


def rope_lanes(tab):
    at = lanes(tab.shape)
    cos = jnp.where(at < 32, tab, 0.0)
    sin = jnp.where((at >= 32) & (at < 64), tab, 0.0)
    cos = cos + pltpu.roll(cos, 32, 1)
    cos = cos + pltpu.roll(cos, 64, 1)
    sin = sin - pltpu.roll(sin, 96, 1)
    sin = sin + pltpu.roll(sin, 64, 1)
    return cos, sin


def swap_halves(u):
    return jnp.where(lax.rem(lanes(u.shape), 64) < 32, pltpu.roll(u, 96, 1), pltpu.roll(u, 32, 1))


def two_heads(u):
    first = lanes(u.shape) < 64
    zero = jnp.zeros_like(u)
    return jnp.concatenate([jnp.where(first, u, zero), jnp.where(first, zero, u)], axis=0)


def join_heads(t):
    rows = t.shape[1] // 2
    return jnp.concatenate([t[:64, :rows], t[64:, rows:]], axis=0).T


def bias_of(tab, keys, first_row, first_key=0):
    rows = tab.shape[0]
    starts = tab.T[64:65, :].astype(jnp.int32)
    key = first_key + lax.broadcasted_iota(jnp.int32, (keys, rows), 0)
    row = first_row + lax.broadcasted_iota(jnp.int32, (keys, rows), 1)
    bias = jnp.where((key >= starts) & (key <= row), 0.0, MASKED)
    return jnp.concatenate([bias, bias], axis=1)


def forward_kernel(
    dims, tokens, positions, starts, gain_a, gain_m, frequency, w_query, w_key, w_value, w_out_t, w_gate, w_up,
    down, cot,
    gains, n1_out, w_out, tab, q, kk, vv, stat, ob, mid, n2g, cotg, w_mlp, w_dn,
    n1g, w_attn, table, n1, blocks, mlp_blocks, mlp_t, kv, vt, part, held, came, n2,
    gs, gr, gl, ts, tr, ss, sr, ds, dr, ws, wr, us, ur, ys, yr, rs, rr, rxs, rxr, cs, cr, cl, ns, nr, nl, ms, mr, local,
):
    nx, nc, nz, ny = dims
    x, c, z, y = place()
    rows, width = tokens.shape
    own = w_query.shape[0]
    qcols = q.shape[-1]
    pairs = qcols // 128
    span = w_gate.shape[1] // (nx * nc * nz)
    keys_span = ny * rows
    dn = Spread(lambda px, py: down, lambda px, py: w_dn.at[px, py], ws, wr, local.at[0], nx, ny)
    swap = Swap(
        lambda pz, pc: blocks.at[pz, pc], lambda pz, pc: w_attn.at[x, pc, pz, y], ss, sr, local.at[1], nz, nc
    )
    tabs = Swap(lambda pz, pc: table, lambda pz, pc: tab.at[pz, pc], ts, tr, local.at[2], nz, nc)
    mlp_swap = Swap(
        lambda pz, pc: mlp_blocks.at[pz, pc], lambda pz, pc: mlp_t.at[pc, pz], us, ur, local.at[3], nz, nc
    )
    gu = Spread(lambda px, py: mlp_t, lambda px, py: w_mlp.at[px, :, :, py], ms, mr, local.at[4], nx, ny)
    first_rows = Gather(n1, n1g, gs, gr, gl)
    reduce = Reduce(part, held, came, rs, rr, rxs, rxr)
    cots = Gather(cot, cotg, cs, cr, cl)
    next_rows = Gather(n2, n2g, ns, nr, nl)
    met = greet(*dims)

    def pack(at):
        gain = gains[at, 0:1]
        for t in range(nz * nc):
            cols = slice(t * qcols, (t + 1) * qcols)
            blocks[t // nc, t % nc, at, :qcols] = (w_query[at, cols].astype(F32) * gain).astype(BF)
            blocks[t // nc, t % nc, at, qcols + 128 :] = w_out_t[at, cols]
        for pair in range(KV_HEADS // 2):
            cols = slice(pair * 128, pair * 128 + 128)
            key, value = w_key[at, cols].astype(F32) * gain, w_value[at, cols].astype(F32) * gain
            first = lanes(key.shape) < 64
            both = (
                jnp.where(first, key, pltpu.roll(value, 64, 1)),
                jnp.where(first, pltpu.roll(key, 64, 1), value),
            )
            for k in range(2):
                for rep in range(nz * nc // KV_HEADS):
                    t = (pair * 2 + k) * (nz * nc // KV_HEADS) + rep
                    blocks[t // nc, t % nc, at, qcols : qcols + 128] = both[k].astype(BF)

    def norm(at):
        value = tokens[at, :].astype(F32)
        inverse = lax.rsqrt(jnp.mean(value * value, axis=-1, keepdims=True) + EPSILON)
        n1[at, :] = (value * inverse).astype(BF)

    first_lanes = lanes((own, 128)) < 64
    gains[...] = jnp.where(first_lanes, column(gain_a[...].astype(F32)), column(gain_m[...].astype(F32)))
    by_rows(rows, norm)
    by_rows(own, pack)
    angle = column(positions[...].astype(F32)) * frequency[...]
    at = lanes(angle.shape)
    doc = jnp.broadcast_to(column(starts[...].astype(F32)), angle.shape)
    table[...] = jnp.where(at < 32, jnp.cos(angle), jnp.where(at < 64, jnp.sin(angle), doc))
    met()
    swap.start()
    tabs.start()
    dn.start()

    def spread_copies():
        for i, step in enumerate(others(nx, ny)):
            px, py = data_peer(step, nx, ny)
            slot = w_attn.at[x, :, :, y]
            yield remote(slot, slot, ds.at[i], dr.at[i], {"x": px, "y": py})

    def spread():
        swap.arrived()
        for copy in spread_copies():
            copy.start()

    def pack_mlp(at):
        gain = gains[at, 64:65]
        for k, weight in enumerate((w_gate, w_up)):
            for t in range(nz * nc):
                for i in range(nx):
                    chunk = (i * nc + t % nc) * nz + t // nc
                    to = (k * nx + i) * span
                    piece = weight[at, chunk * span : (chunk + 1) * span].astype(F32) * gain
                    mlp_blocks[t // nc, t % nc, at, to : to + span] = piece.astype(BF)

    end = flow(None, first_rows, None, [spread, lambda: by_rows(own, pack_mlp)])
    end()
    mlp_swap.start()
    keep_rows = pltpu.make_async_copy(n1g, n1_out, local.at[5])
    keep_rows.start()
    tabs.arrived()
    for copy in spread_copies():
        copy.wait_recv()
    keep_weights = pltpu.make_async_copy(w_attn, w_out, local.at[6])
    keep_weights.start()

    def project_kv(i, carry):
        u = nn(n1g[i].reshape(nc * rows, width), w_attn[..., qcols : qcols + 128].reshape(width, 128))
        cos, sin = rope_lanes(tab[i].reshape(nc * rows, 128))
        u = jnp.where(lanes(u.shape) < 64, u * cos + swap_halves(u) * sin, u).astype(BF)
        for pc in range(nc):
            kv[pc, i, y] = u[pc * rows : (pc + 1) * rows]
        return carry

    def project_q(i, carry):
        res = nn(n1g[i].reshape(nc * rows, width), w_attn[..., :qcols].reshape(width, qcols))
        cos, sin = rope_lanes(tab[i].reshape(nc * rows, 128))
        for p in range(pairs):
            u = res[:, p * 128 : p * 128 + 128]
            u = (u * cos + swap_halves(u) * sin) * (HEAD_DIM ** (-0.5))
            q[i, :, :, p * 128 : p * 128 + 128] = u.astype(BF).reshape(nc, rows, 128)
        return carry

    lax.fori_loop(0, nz, project_kv, 0)
    sends = []
    for i in range(ny - 1):
        slot = kv.at[:, :, y]
        sends.append(remote(slot, slot, ys.at[i], yr.at[i], {"y": lax.rem(y + 1 + i, ny)}))
    for copy in sends:
        copy.start()
    lax.fori_loop(0, nz, project_q, 0)
    for copy in sends:
        copy.wait_recv()

    def double(i, carry):
        pc, pz = i // nz, lax.rem(i, nz)
        u = kv[pc, pz].reshape(keys_span, 128).astype(F32)
        r = pltpu.roll(u, 64, 1)
        first = lanes(u.shape) < 64
        at = pl.ds(pl.multiple_of(pz * keys_span, keys_span), keys_span)
        kk[pc, at, :] = jnp.where(first, u, r).astype(BF)
        values = jnp.where(first, r, u)
        vv[pc, at, :] = values.astype(BF)
        vt[pc, :, at] = values.T.astype(BF)
        return carry

    lax.fori_loop(0, nc * nz, double, 0)

    def attend(pc, carry):
        for pz in range(nz):
            keys = (pz + 1) * keys_span
            bias = bias_of(tab[pz, pc], keys, (pz * ny + y) * rows)
            for p in range(pairs):
                q2 = two_heads(q[pz, pc, :, p * 128 : p * 128 + 128])
                s = nt(kk[pc, :keys, :], q2) + bias
                top = jnp.max(s, axis=0, keepdims=True)
                e = jnp.exp(s - top)
                total = jnp.sum(e, axis=0, keepdims=True)
                stat[pz, pc, p : p + 1, :] = top + jnp.log(total)
                weights = (e * (1.0 / total)).astype(BF)
                o = join_heads(nn(vt[pc, :, :keys], weights))
                ob[pz, pc, :, p * 128 : p * 128 + 128] = o.astype(BF)
        return carry

    lax.fori_loop(0, nc, attend, 0)

    def output(i, carry):
        half, odd = i // 2, lax.rem(i, 2)
        pz = odd * half + (1 - odd) * (nz - 1 - half)
        for px in range(nx):
            cols = slice(px * (width // nx), (px + 1) * (width // nx))
            weights = w_attn[px, :, :, :, :, qcols + 128 :].reshape(width // nx, qcols)
            res = nt(ob[pz].reshape(nc * rows, qcols), weights)
            part[pz, :, :, cols] = res.astype(BF).reshape(nc, rows, width // nx)
        reduce.across(pz).start()
        return carry

    lax.fori_loop(0, nz, output, 0)

    def spread_mlp():
        mlp_swap.arrived()
        gu.start()

    end2 = flow(reduce, cots, None, [spread_mlp])

    def settle(at, total):
        value = tokens[at, :].astype(F32) + total
        mid[at, :] = value
        inverse = lax.rsqrt(jnp.mean(value * value, axis=-1, keepdims=True) + EPSILON)
        n2[at, :] = (value * inverse).astype(BF)

    end3 = flow(None, next_rows, lambda half: reduce.last(half, settle))
    end3()
    end2()
    keep_rows.wait()
    keep_weights.wait()
    gu.arrived()
    dn.arrived()
    for one in (swap, tabs, mlp_swap, gu, dn):
        one.finish()
    for copy in list(spread_copies()) + sends:
        copy.wait_send()


def forward_call(
    dims, tokens, positions, starts, gain_a, gain_m, w_query, w_key, w_value, w_out_t, w_gate, w_up, down, cot
):
    nx, nc, nz, ny = dims
    rows, width = tokens.shape
    own = w_query.shape[0]
    qcols = HEADS // (nz * nc) * HEAD_DIM
    cols = 2 * qcols + 128
    peers, members = nx * ny - 1, nz * nc - 1
    mlp_cols = 2 * w_gate.shape[1] // (nz * nc)
    keys = nz * ny * rows
    team_rows = (nz, nc, rows, width)
    half = HEAD_DIM // 2
    exponents = np.tile(np.arange(half), 128 // half)[None, :] * (-2.0 / HEAD_DIM)
    frequency = jnp.asarray(10000.0**exponents, F32)
    return call(
        functools.partial(forward_kernel, dims),
        (
            tokens, positions, starts, gain_a, gain_m, frequency, w_query, w_key, w_value, w_out_t, w_gate, w_up,
            down, cot,
        ),
        (VM,) * 12 + (pl.ANY, VM),
        [
            ((own, 128), F32),
            (team_rows, BF),
            ((nx, nc, nz, ny, own, cols), BF),
            ((nz, nc, rows, 128), F32),
            ((nz, nc, rows, qcols), BF),
            ((nc, keys, 128), BF),
            ((nc, keys, 128), BF),
            ((nz, nc, 8, 2 * rows), F32),
            ((nz, nc, rows, qcols), BF),
            ((rows, width), F32),
            (team_rows, BF),
            (team_rows, BF),
            ((nx, nc, nz, ny, own, mlp_cols), BF),
            ((nx, ny) + down.shape, BF),
        ],
        (VM,) + (pl.ANY,) * 2 + (VM,) * 7 + (pl.ANY,) * 4,
        [
            VM(team_rows, BF),
            VM((nx, nc, nz, ny, own, cols), BF),
            VM((rows, 128), F32),
            VM((rows, width), BF),
            VM((nz, nc, own, cols), BF),
            VM((nz, nc, own, mlp_cols), BF),
            VM((nc, nz, own, mlp_cols), BF),
            VM((nc, nz, ny, rows, 128), BF),
            VM((nc, 128, keys), BF),
            VM(team_rows, BF),
        ]
        + Reduce.buffers(nz, rows, width)
        + [VM((rows, width), BF)]
        + Gather.SEMS
        + [DMA((members,))] * 4
        + [DMA((peers,))] * 4
        + [DMA((members,))] * 2
        + [DMA((max(ny - 1, 1),))] * 2
        + Reduce.SEMS
        + Gather.SEMS * 2
        + [DMA((peers,))] * 2
        + [DMA((7,))],
        1,
    )


def mlp_kernel(
    dims, n2g, cotg, w_mlp, w_dn, mid, cot,
    dx2, dag, output, came_mlp, grad_dn,
    n2v, cotv, wv, wd, hid, hid_t, dmlp, part, mlp_out, grad_mlp,
    held, came, held2, came2, low,
    loads, rs, rr, rxs, rxr, os, orr, oxs, oxr, ds, dr, dl, ms, mr, local,
):
    nx, nc, nz, ny = dims
    x, c, z, y = place()
    rows, width = mid.shape
    ff2 = wv.shape[-1]
    ff = ff2 // 2
    piece = wd.shape[2]
    block = nc * rows
    fetch_w = pltpu.make_async_copy(w_mlp, wv, loads.at[0])
    fetch_d = pltpu.make_async_copy(w_dn, wd, loads.at[1])
    fetch_w.start()

    def fetch(at, k):
        source, target = ((n2g, n2v), (cotg, cotv))[k]
        return pltpu.make_async_copy(source.at[at], target.at[at], loads.at[2 + k * nz + at])

    for k in range(nz):
        fetch(by_need(nz, z, k), 0).start()
        if k == 0:
            fetch_d.start()
        fetch(by_need(nz, z, k), 1).start()
    met = greet(*dims)
    reduce = Reduce(part, held, came, rs, rr, rxs, rxr)
    reduce2 = Reduce(mlp_out, held2, came2, os, orr, oxs, oxr)
    into = Gather(low, dag, ds, dr, dl)
    gu = Spread(
        lambda px, py: grad_mlp.at[px, :, :, py], lambda px, py: came_mlp.at[px, py], ms, mr, local.at[0], nx, ny
    )

    def down_rows(cols):
        if piece % ROWS:
            return jnp.concatenate([wd[px, py, :, cols] for px in range(nx) for py in range(ny)], axis=0)
        return wd[:, :, :, cols].reshape(ff, -1)

    def weights(px):
        return wv[px].reshape(width // nx, ff2)

    fetch_w.wait()

    def forward_back(k):
        at = by_need(nz, z, k)
        fetch(at, 0).wait()
        u = nn(n2v[at].reshape(block, width), wv[...].reshape(width, ff2))
        gt, up = u[:, :ff], u[:, ff:]
        sg = jax.nn.sigmoid(gt)
        silu = gt * sg
        value = (silu * up).astype(BF)
        hid[at] = value
        hid_t[:, pl.ds(pl.multiple_of(at * block, block), block)] = value.astype(F32).T.astype(BF)
        if k == 0:
            fetch_d.wait()
        fetch(at, 1).wait()
        dh = nt(cotv[at].reshape(block, width), down_rows(slice(None)))
        dgt = dh * up * sg * (1.0 + gt * (1.0 - sg))
        dmlp[at] = jnp.concatenate([dgt, dh * silu], axis=1).astype(BF)

        for px in range(nx):
            cols = slice(px * (width // nx), (px + 1) * (width // nx))
            res = nt(dmlp[at], weights(px))
            part[at, :, :, cols] = res.astype(BF).reshape(nc, rows, width // nx)
        if k == 0:
            met()
        reduce.across(at).start()

    forward_back(0)
    chunk = width // 4

    def down_grad(n, carry):
        cols = pl.ds(pl.multiple_of(n * chunk, chunk), chunk)
        res = nn(hid_t[...], cotv[:, :, :, cols].reshape(nz * block, chunk)).astype(BF)
        for px in range(nx):
            for py in range(ny):
                k = (px * ny + py) * piece
                grad_dn[px, py, :, cols] = res[k : k + piece]
        return carry

    def mlp_grad(far):
        px = lax.rem(x + far, nx)
        size = width // (nx * 4)

        def body(j, carry):
            cols = pl.ds(pl.multiple_of(px * (width // nx) + j * size, size), size)
            res = tn(n2v[:, :, :, cols].reshape(nz * block, size), dmlp[...].reshape(nz * block, ff2))
            own = grad_mlp.shape[4]
            grad_mlp[px, j // 2, pl.ds(lax.rem(j, 2) * (nz // 2), nz // 2)] = res.astype(BF).reshape(
                nz // 2, ny, own, ff2
            )
            return carry

        lax.fori_loop(0, 4, body, 0)
        gu.start_along(far)

    def mlp_sum(n, carry):
        cols = pl.ds(pl.multiple_of(n * chunk, chunk), chunk)
        res = nn(hid[...].reshape(nz * block, ff), down_rows(cols))
        mlp_out[:, :, :, cols] = res.astype(BF).reshape(nz, nc, rows, chunk)
        return carry

    def down_first():
        lax.fori_loop(0, 2, down_grad, 0)

    def down_second():
        lax.fori_loop(2, 4, down_grad, 0)

    def sum_all():
        lax.fori_loop(0, 4, mlp_sum, 0)
        reduce2.start()

    def other_blocks():
        for k in range(2, nz):
            forward_back(k)

    forward_back(1)
    work = [other_blocks] + [functools.partial(mlp_grad, far) for far in reversed(range(nx))]
    end = flow(reduce, None, None, work + [sum_all])

    def settle(at, total):
        value = mid[at, :]
        inverse = lax.rsqrt(jnp.mean(value * value, axis=-1, keepdims=True) + EPSILON)
        normed = value * inverse
        gradient = cot[at, :].astype(F32) + inverse * (
            total - normed * jnp.mean(total * normed, axis=-1, keepdims=True)
        )
        dx2[at, :] = gradient
        low[at, :] = gradient.astype(BF)

    end2 = flow(reduce2, into, lambda part: reduce.last(part, settle), [down_first, down_second])

    def finish(at, total):
        output[at, :] = (mid[at, :] + total).astype(BF)

    for half in range(PARTS):
        reduce2.last(half, finish)
    end2()
    end()
    gu.arrived()
    gu.finish()


def mlp_call(dims, n2g, cotg, w_mlp, w_dn, mid, cot):
    nx, nc, nz, ny = dims
    rows, width = mid.shape
    own, ff2 = w_mlp.shape[4:]
    block = nc * rows
    peers = nx * ny - 1
    return call(
        functools.partial(mlp_kernel, dims),
        (n2g, cotg, w_mlp, w_dn, mid, cot),
        (pl.ANY, pl.ANY, pl.ANY, pl.ANY, VM, VM),
        [
            ((rows, width), F32),
            ((nz, nc, rows, width), BF),
            ((rows, width), BF),
            ((nx, ny, nc, nz, own, ff2), BF),
            (w_dn.shape, BF),
        ],
        (VM, pl.ANY, VM, pl.ANY, VM),
        [
            VM(n2g.shape, BF),
            VM(cotg.shape, BF),
            VM(w_mlp.shape, BF),
            VM(w_dn.shape, BF),
            VM((nz, block, ff2 // 2), BF),
            VM((ff2 // 2, nz * block), BF),
            VM((nz, block, ff2), BF),
            VM(n2g.shape, BF),
            VM(n2g.shape, BF),
            VM(w_mlp.shape, BF),
        ]
        + Reduce.buffers(nz, rows, width) * 2
        + [VM((rows, width), BF), DMA((2 + 2 * nz,))]
        + Reduce.SEMS * 2
        + Gather.SEMS
        + [DMA((peers,))] * 2
        + [DMA((1,))],
        3,
    )


def backward_kernel(
    dims, dag, w_in, tab_in, q_in, kk_in, vv_in, stat_in, ob_in, came_mlp, grad_dn, n1g,
    dn1, raw_gate, raw_up, came_dn, own_o, own_p,
    w, tab, q, kk, vv, stat, ob, do, kt, dk, dv, out, near, dqkv, part, team, stage, mlp_sum, mlp_g,
    grad_o, came_o, sums_o, grad_p, came_p, sums_p,
    held, came,
    ins, loads, us, ur, ys, yr, ws, wr, rs, rr, rxs, rxr, ds, dr, ss, sr, es, er, fs, fr, local,
):
    nx, nc, nz, ny = dims
    x, c, z, y = place()
    rows, width = dn1.shape
    own = grad_o.shape[4]
    qcols = q.shape[-1]
    pairs = qcols // 128
    keys_span = ny * rows
    fetch_dag = pltpu.make_async_copy(dag, team, loads.at[2])
    fetch = pltpu.make_async_copy(n1g, team, loads.at[2])
    pairs_in = zip((w_in, kk_in, q_in, tab_in, stat_in, vv_in, ob_in), (w, kk, q, tab, stat, vv, ob))
    fetch_rest = [pltpu.make_async_copy(a, b, ins.at[i]) for i, (a, b) in enumerate(pairs_in)]
    mlp_swap = Swap(
        lambda pz, pc: mlp_sum.at[pz, pc], lambda pz, pc: mlp_g.at[pz, pc], us, ur, local.at[0], nz, nc
    )
    dn = Spread(lambda px, py: grad_dn.at[px, py], lambda px, py: came_dn.at[px, py], ws, wr, local.at[1], nx, ny)
    reduce = Reduce(part, held, came, rs, rr, rxs, rxr)
    spread_o = Spread(
        lambda px, py: grad_o.at[px, :, :, py], lambda px, py: came_o.at[px, py], ds, dr, local.at[2], nx, ny
    )
    swap_o = Swap(lambda pz, pc: sums_o.at[pz, pc], lambda pz, pc: own_o.at[pz, pc], ss, sr, local.at[3], nz, nc)
    spread_p = Spread(
        lambda px, py: grad_p.at[px, :, :, py], lambda px, py: came_p.at[px, py], es, er, local.at[4], nx, ny
    )
    swap_p = Swap(lambda pz, pc: sums_p.at[pz, pc], lambda pz, pc: own_p.at[pz, pc], fs, fr, local.at[5], nz, nc)

    steps = others(nz, nc) + [(0, 0)]

    def load(i):
        pz, pc = team_peer(steps[i], nz, nc)
        return pltpu.make_async_copy(came_mlp.at[:, :, pc, pz], stage.at[i % 2], loads.at[i % 2])

    load(0).start()
    fetch_dag.start()
    for copy in fetch_rest:
        copy.start()
    met = greet(*dims, cross=True)
    early = 2 * (nx * ny - 1) // 3
    for i, copy in enumerate(list(mlp_swap.copies()) + [mlp_swap.own()]):
        if i + 1 < len(steps):
            load(i + 1).start()
        load(i).wait()
        pz, pc = team_peer(steps[i], nz, nc)

        def add(at, i=i, pz=pz, pc=pc):
            total = stage[i % 2, 0, 0, at, :].astype(F32)
            for px, py in others(nx, ny):
                total = total + stage[i % 2, px, py, at, :].astype(F32)
            mlp_sum[pz, pc, at, :] = total.astype(BF)

        by_rows(own, add)
        if i == 0:
            met()
            dn.start_some(0, early)
            dn.own().start()
        copy.start()
    fetch_dag.wait()
    for copy in fetch_rest:
        copy.wait()

    def turned(i, carry):
        pc, pz = i // nz, lax.rem(i, nz)
        at = pl.ds(pl.multiple_of(pz * keys_span, keys_span), keys_span)
        kt[pc, :, at] = kk[pc, at, :].astype(F32).T.astype(BF)
        return carry

    lax.fori_loop(0, nc * nz, turned, 0)

    def project(i, carry):
        weights = w[..., qcols + 128 :].reshape(width, qcols)
        do[i] = nn(team[i].reshape(nc * rows, width), weights).astype(BF).reshape(nc, rows, qcols)
        return carry

    lax.fori_loop(0, nz, project, 0)

    def attend(pc, carry):
        for pz in reversed(range(nz)):
            keys = (pz + 1) * keys_span
            most = KEYS if nz * keys_span <= KEYS else KEYS // 4
            cuts = [slice(a, min(a + most, keys)) for a in range(0, keys, most)]

            def bias_at(i, cuts=cuts, pz=pz):
                cut = cuts[i]
                return bias_of(tab[pz, pc], cut.stop - cut.start, (pz * ny + y) * rows, cut.start)

            only = bias_at(0) if len(cuts) == 1 else None
            cos, sin = rope_lanes(tab[pz, pc])
            for p in range(pairs):
                q2 = two_heads(q[pz, pc, :, p * 128 : p * 128 + 128])
                do2 = two_heads(do[pz, pc, :, p * 128 : p * 128 + 128])

                def scores(i, cuts=cuts, only=only, bias_at=bias_at, q2=q2, do2=do2, p=p, pz=pz):
                    s = nt(kk[pc, cuts[i], :], q2) + (bias_at(i) if only is None else only)
                    weights = jnp.exp(s - stat[pz, pc, p : p + 1, :])
                    return weights, weights * nt(vv[pc, cuts[i], :], do2)

                delta = sum(jnp.sum(scores(i)[1], axis=0, keepdims=True) for i in range(1, len(cuts)))
                u = 0.0
                for i, cut in enumerate(cuts):
                    weights, dw = scores(i)
                    if i == 0:
                        delta = delta + jnp.sum(dw, axis=0, keepdims=True)
                    score_grad = (dw - weights * delta).astype(BF)
                    dv_new = nn(weights.astype(BF), do2)
                    dk_new = nn(score_grad, q2)
                    if pz == nz - 1 and p == 0:
                        dv[pc, cut, :] = dv_new
                        dk[pc, cut, :] = dk_new
                    else:
                        dv[pc, cut, :] += dv_new
                        dk[pc, cut, :] += dk_new
                    u = u + nn(kt[pc, :, cut], score_grad)
                u = join_heads(u) * (HEAD_DIM ** (-0.5))
                u = u * cos - swap_halves(u) * sin
                dqkv[pz, pc, :, p * 128 : p * 128 + 128] = u.astype(BF)
        return carry

    lax.fori_loop(0, nc, attend, 0)

    def fold(i, carry):
        pc, pz = i // nz, lax.rem(i, nz)
        at = pl.ds(pl.multiple_of(pz * keys_span, keys_span), keys_span)
        key, value = dk[pc, at, :], dv[pc, at, :]
        first = lanes(key.shape) < 64
        both = jnp.where(first, key + pltpu.roll(key, 64, 1), value + pltpu.roll(value, 64, 1))
        both = both.astype(BF)
        for py in range(ny):
            out[pc, py, pz] = both[py * rows : (py + 1) * rows]
        return carry

    lax.fori_loop(0, nc * nz, fold, 0)
    sends = []
    for i, (sy, sc) in enumerate(others(ny, nc)):
        py, pc = lax.rem(y + sy, ny), lax.rem(c + sc, nc)
        sends.append(remote(out.at[pc, py], near.at[i], ys.at[i], yr.at[i], {"y": py, "core": pc}))
    for copy in sends:
        copy.start()

    def weight_grad(right, target):
        def body(j, carry):
            px, k = j // 4, lax.rem(j, 4)
            size = width // (nx * 4)
            cols = pl.ds(pl.multiple_of(j * size, size), size)
            res = tn(team[:, :, :, cols].reshape(nz * nc * rows, size), right.reshape(nz * nc * rows, -1))
            target[px, k // 2, pl.ds(lax.rem(k, 2) * (nz // 2), nz // 2)] = res.astype(BF).reshape(
                nz // 2, ny, own, -1
            )
            return carry

        lax.fori_loop(0, nx * 4, body, 0)

    weight_grad(ob[...], grad_o)
    fetch.start()
    for copy in sends:
        copy.wait_recv()
    spread_o.start()

    def settle_kv(pz, carry):
        total = out[c, y, pz].astype(F32)
        for i in range(len(sends)):
            total = total + near[i, pz].astype(F32)
        cos, sin = rope_lanes(tab[pz, c])
        first = lanes(total.shape) < 64
        total = jnp.where(first, total * cos - swap_halves(total) * sin, total)
        dqkv[pz, c, :, qcols : qcols + 128] = total.astype(BF)
        dqkv[pz, 1 - c, :, qcols : qcols + 128] = jnp.zeros((rows, 128), BF)
        return carry

    lax.fori_loop(0, nz, settle_kv, 0)

    def output(i, carry):
        half, odd = i // 2, lax.rem(i, 2)
        pz = odd * half + (1 - odd) * (nz - 1 - half)
        for px in range(nx):
            cols = slice(px * (width // nx), (px + 1) * (width // nx))
            weights = w[px, :, :, :, :, : qcols + 128].reshape(width // nx, qcols + 128)
            res = nt(dqkv[pz].reshape(nc * rows, qcols + 128), weights)
            part[pz, :, :, cols] = res.astype(BF).reshape(nc, rows, width // nx)
        reduce.across(pz).start()
        return carry

    lax.fori_loop(0, nz, output, 0)

    def own_weights():
        fetch.wait()
        weight_grad(dqkv[...], grad_p)
        spread_p.start()

    def unpack_mlp(at):
        span = mlp_g.shape[-1] // (2 * nx)
        for k, raw in enumerate((raw_gate, raw_up)):
            for t in range(nz * nc):
                for i in range(nx):
                    chunk = (i * nc + t % nc) * nz + t // nc
                    piece = mlp_g[t // nc, t % nc, at, (k * nx + i) * span : (k * nx + i + 1) * span]
                    raw[at, chunk * span : (chunk + 1) * span] = piece

    def unpack_all():
        mlp_swap.arrived()
        by_rows(own, unpack_mlp)

    def down_rest():
        dn.start_some(early, nx * ny - 1)

    def exchange(spread, arrived, sums, swap):
        spread.arrived()

        def add(at):
            for pz in range(nz):
                for pc in range(nc):
                    total = arrived[0, 0, pc, pz, at, :].astype(F32)
                    for px, py in others(nx, ny):
                        total = total + arrived[px, py, pc, pz, at, :].astype(F32)
                    sums[pz, pc, at, :] = total.astype(BF)

        by_rows(own, add)
        swap.start()

    work = [
        own_weights,
        unpack_all,
        down_rest,
        functools.partial(exchange, spread_o, came_o, sums_o, swap_o),
        functools.partial(exchange, spread_p, came_p, sums_p, swap_p),
    ]
    end = flow(reduce, None, None, work)

    def settle(at, total):
        dn1[at, :] = total

    for half in range(PARTS):
        reduce.last(half, settle)
    end()
    for one in (dn, swap_o, swap_p):
        one.arrived()
    for one in (mlp_swap, dn, spread_o, swap_o, spread_p, swap_p):
        one.finish()
    for copy in sends:
        copy.wait_send()


def backward_call(dims, dag, w, tab, q, kk, vv, stat, ob, came_mlp, grad_dn, n1g):
    nx, nc, nz, ny = dims
    rows, width = dag.shape[2:]
    own, mlp_cols = came_mlp.shape[4:]
    qcols = q.shape[-1]
    keys = nz * ny * rows
    peers, members, near = nx * ny - 1, nz * nc - 1, ny * nc - 1
    team_rows = (nz, nc, rows, width)
    return call(
        functools.partial(backward_kernel, dims),
        (dag, w, tab, q, kk, vv, stat, ob, came_mlp, grad_dn, n1g),
        (pl.ANY,) * 11,
        [
            ((rows, width), F32),
            ((own, mlp_cols // 2 * nz * nc), BF),
            ((own, mlp_cols // 2 * nz * nc), BF),
            (grad_dn.shape, BF),
            ((nz, nc, own, qcols), BF),
            ((nz, nc, own, qcols + 128), BF),
        ],
        (VM,) * 3 + (pl.ANY,) * 3,
        [VM(a.shape, a.dtype) for a in (w, tab, q, kk, vv, stat, ob)]
        + [
            VM((nz, nc, rows, qcols), BF),
            VM((nc, 128, keys), BF),
            VM((nc, keys, 128), F32),
            VM((nc, keys, 128), F32),
            VM((nc, ny, nz, rows, 128), BF),
            VM((near, nz, rows, 128), BF),
            VM((nz, nc, rows, qcols + 128), BF),
            VM(team_rows, BF),
            VM(team_rows, BF),
            VM((2, nx, ny, own, mlp_cols), BF),
            VM((nz, nc, own, mlp_cols), BF),
            VM((nz, nc, own, mlp_cols), BF),
        ]
        + [
            VM(shape + (own, n), BF)
            for n in (qcols, qcols + 128)
            for shape in ((nx, nc, nz, ny), (nx, ny, nc, nz), (nz, nc))
        ]
        + Reduce.buffers(nz, rows, width)
        + [DMA((7,)), DMA((3,))]
        + [DMA((members,))] * 2
        + [DMA((near,))] * 2
        + [DMA((peers,))] * 2
        + Reduce.SEMS
        + ([DMA((peers,))] * 2 + [DMA((members,))] * 2) * 2
        + [DMA((6,))],
        6,
    )


def final_kernel(
    dims, low, dn1, tokens, dx2, raw_gate, raw_up, came_dn, own_o, own_p, gains, w_query, w_key, w_value, w_gate, w_up,
    output, input_grad, grad_query, grad_key, grad_value, grad_out_t, grad_gate, grad_up, grad_down, grad_gain_a, grad_gain_m,
):
    nx, nc, nz, ny = dims
    team = nz * nc
    output[...] = low[...]
    value = tokens[...].astype(F32)
    total = dn1[...]
    inverse = lax.rsqrt(jnp.mean(value * value, axis=-1, keepdims=True) + EPSILON)
    normed = value * inverse
    input_grad[...] = dx2[...] + inverse * (total - normed * jnp.mean(total * normed, axis=-1, keepdims=True))

    down = came_dn[0, 0].astype(F32)
    for px, py in others(nx, ny):
        down = down + came_dn[px, py].astype(F32)
    grad_down[...] = down

    gain = gains[:, 64:65]
    both = 0.0
    for raw, weight, grad in ((raw_gate, w_gate, grad_gate), (raw_up, w_up, grad_up)):
        got = raw[...].astype(F32)
        grad[...] = got * gain
        both = both + got * weight[...].astype(F32)
    dots_mlp = jnp.sum(both, axis=-1, keepdims=True)

    gain = gains[:, 0:1]
    qcols = own_o.shape[-1]
    both = 0.0
    heads = []
    for t in range(team):
        block = own_p[t // nc, t % nc].astype(F32)
        cols = slice(t * qcols, (t + 1) * qcols)
        grad_out_t[:, cols] = own_o[t // nc, t % nc].astype(F32)
        grad_query[:, cols] = block[:, :qcols] * gain
        both = both + block[:, :qcols] * w_query[:, cols].astype(F32)
        if t % (team // KV_HEADS):
            heads[-1] = heads[-1] + block[:, qcols:]
        else:
            heads.append(block[:, qcols:])
    dots = jnp.sum(both, axis=-1, keepdims=True)
    for pair in range(KV_HEADS // 2):
        one, two = heads[2 * pair], heads[2 * pair + 1]
        first = lanes(one.shape) < 64
        cols = slice(pair * 128, pair * 128 + 128)
        key = jnp.where(first, one, pltpu.roll(two, 64, 1))
        val = jnp.where(first, pltpu.roll(one, 64, 1), two)
        grad_key[:, cols] = key * gain
        grad_value[:, cols] = val * gain
        both = key * w_key[:, cols].astype(F32) + val * w_value[:, cols].astype(F32)
        dots = dots + jnp.sum(both, axis=-1, keepdims=True)
    shape = (dots.shape[0], grad_gain_a.shape[1])
    step = pl.program_id(0)
    mine = lanes(shape) == step * shape[0] + lax.broadcasted_iota(jnp.int32, shape, 0)
    for target, column_of in ((grad_gain_a, dots), (grad_gain_m, dots_mlp)):
        row = jnp.sum(jnp.where(mine, column_of, 0.0), axis=0, keepdims=True)
        target[...] = jnp.where(step == 0, row, target[...] + row)


def final_call(
    dims, low, dn1, tokens, dx2, raw_gate, raw_up, came_dn, own_o, own_p, gains,
    w_query, w_key, w_value, w_gate, w_up,
):
    own = w_query.shape[0]
    steps = max(own // ROWS, 1)

    def rows_of(shape, axis):
        count = shape[axis]
        each = count if steps == 1 else -(-count // (steps * ROWS)) * ROWS
        block = shape[:axis] + (each,) + shape[axis + 1 :]
        return pl.BlockSpec(block, lambda i: tuple(i if k == axis else 0 for k in range(len(shape))))

    operands = (
        low, dn1, tokens, dx2, raw_gate, raw_up, came_dn, own_o, own_p, gains, w_query, w_key, w_value, w_gate, w_up
    )
    outs = [
        low.shape, dn1.shape, w_query.shape, w_key.shape, w_value.shape, w_query.shape, w_gate.shape, w_up.shape,
        came_dn.shape[2:], (1, own), (1, own),
    ]
    return pl.pallas_call(
        functools.partial(final_kernel, dims),
        grid=(steps,),
        out_shape=[jax.ShapeDtypeStruct(s, BF if i == 0 else F32) for i, s in enumerate(outs)],
        in_specs=[rows_of(a.shape, len(a.shape) - 2) for a in operands],
        out_specs=[rows_of(s, 0) for s in outs[:-2]] + [pl.BlockSpec((1, own), lambda i: (0, 0))] * 2,
        compiler_params=pltpu.CompilerParams(vmem_limit_bytes=60 << 20),
    )(*operands)


def shards(
    tokens, positions, doc_start, cotangent, w_query, w_key, w_value, w_out,
    attn_gain, w_gate, w_up, w_down, mlp_gain,
):
    dims = tuple(lax.axis_size(a) for a in ALL)
    gains, n1g, w_attn, tab, q, kk, vv, stat, ob, mid, n2g, cotg, w_mlp, w_dn = forward_call(
        dims, tokens, positions[None], doc_start[None], attn_gain[None], mlp_gain[None],
        w_query, w_key, w_value, w_out.T, w_gate, w_up, w_down, cotangent,
    )
    dx2, dag, output, came_mlp, grad_dn = mlp_call(dims, n2g, cotg, w_mlp, w_dn, mid, cotangent)
    dn1, raw_gate, raw_up, came_dn, own_o, own_p = backward_call(
        dims, dag, w_attn, tab, q, kk, vv, stat, ob, came_mlp, grad_dn, n1g
    )
    (
        output, input_grad, grad_query, grad_key, grad_value, grad_out_t, grad_gate, grad_up, grad_down,
        grad_gain_a, grad_gain_m,
    ) = final_call(
        dims, output, dn1, tokens, dx2, raw_gate, raw_up, came_dn, own_o, own_p, gains,
        w_query, w_key, w_value, w_gate, w_up,
    )
    return (
        output, input_grad, grad_query, grad_key, grad_value, grad_out_t.T, grad_gain_a[0],
        grad_gate, grad_up, grad_down, grad_gain_m[0],
    )


def solution(mesh):
    fsdp, seq = mesh.shape["fsdp"], mesh.shape["seq"]
    nc, nz = 2, 4
    grid = Mesh(mesh.devices.reshape(fsdp // nc, nc, nz, seq // nz), ALL)
    row, col, vec = P(ALL, None), P(None, ALL), P(ALL)
    in_specs = (row, vec, vec, row, row, row, row, col, vec, row, row, row, vec)
    out_specs = (row, row, row, row, row, col, vec, row, row, row, vec)
    return jax.shard_map(shards, mesh=grid, in_specs=in_specs, out_specs=out_specs, check_vma=False)
```
